32 devices in a mesh: groups: 2 (over x), rows: 16 (over z, y, core).
Axes of the slice: x: 2, y: 2, z: 4, core: 2. Of those that a mesh axis runs over, the one named last changes fastest.
Arguments:
- queries: float32 [1024, 4096], P('groups', 'rows'), parts along dimension 0, may hold values from -6 to 6
- precond: float32 [4096, 4096], P('rows'), may hold values from -0.125 to 0.125
- train: bfloat16 [256, 32, 4096], P('rows', 'groups'), parts along dimension 1, may hold values from -0.09375 to 0.09375
- query_cluster: int32 [1024], P('groups'), parts along dimension 0, may hold values from 0 to 7
- cand_blocks: int32 [16, 12], P('groups'), parts along dimension 0, may hold values from 0 to 15, as said below
- cand_count: int32 [16], P('groups'), parts along dimension 0, may hold values from 1 to 12, 64 in all
- slot_block: int32 [32], P('groups'), parts along dimension 0, may hold values from 0 to 15, each once
Outputs:
- scores: float32 [256, 32, 512], P(None, ('groups', 'rows')), parts along dimension 1
The draws below stay inside these ranges and needn't reach their ends.
There are 2 independent parts, one for each index of `groups`. The reference program is written for one: setup_inputs(seed, part) draws one part's arguments, and reference() takes and returns one part's arrays. A program takes and returns all parts, laid end to end along the dimension named above; an argument that names none is the same for every part. Nothing has to cross between parts.
Inputs may be any that keep to these rules, and one draw needn't show every extreme that they name: `cand_blocks`: each row holds 12 different block ids; the first cand_count[c] entries of row c are cluster c's candidates.
All inputs are finite; a program needn't handle non-finite values.
Results may differ from the reference program's by a relative error of at most 0.0029.
Values may be sent and summed in bfloat16 or wider, within the bound.
No kernel may reach another device: no remote copies, remote signals or barrier semaphores. Data moves between devices by JAX's collectives and lax.ppermute only.
A program may use at most 64 MiB of HBM per device.

```python
import math
import jax
import jax.numpy as jnp
import numpy as np
from jax import lax

D = 4096
BROWS = 256
NQ = 512
NC = 8
NB = 16
KMAX = 12


def draw_cand_blocks(key, part):
    key = jax.random.fold_in(key, 7)
    keys = jax.random.split(key, NC)
    rows = jax.vmap(lambda k: jax.random.permutation(k, NB)[:KMAX])(keys)
    return rows.astype(jnp.int32)


def place_ends(entries, rng, least, top_value):
    longest = entries.shape.index(max(entries.shape))
    spots = []
    for shift in (0, 1):
        where = [jax.random.randint(jax.random.fold_in(rng, axis), (), 0, length) for axis, length in enumerate(entries.shape)]
        where[longest] = (where[longest] + shift) % entries.shape[longest]
        spots.append(tuple(where))
    return entries.at[spots[0]].set(least).at[spots[1]].set(top_value)


def spiked(drawn, rng, source, target, blocks, factor):
    def block_of(dim):
        return (jnp.arange(drawn.shape[dim]) // (drawn.shape[dim] // blocks)).reshape((-1,) + (1,) * (drawn.ndim - 1 - dim))

    first = jax.random.permutation(rng, blocks)[block_of(target)]
    far = (block_of(target) + blocks // 2) % blocks
    return jnp.where((block_of(source) == first) | (block_of(source) == far), factor * drawn, drawn)


def levels(rng, dims, cuts, smallest, high):
    def one(dim, shards_of):
        draws = jax.random.uniform(jax.random.fold_in(jax.random.fold_in(rng, 6), dim), (shards_of,), jnp.float32, smallest / len(cuts), high / len(cuts))
        return jnp.repeat(jnp.exp(draws), dims[dim] // shards_of).reshape((-1,) + (1,) * (len(dims) - dim - 1))

    gain = one(*cuts[0])
    for cut in cuts[1:]:
        gain = gain * one(*cut)
    return gain


def length_profile(count, total, reach, skew):
    loads = [(1 << 20) // math.isqrt(rank ** skew) + 1 for rank in range(2, count + 1)]
    surplus, holding = total - reach - (count - 1), [1] * (count - 1)
    while surplus > 0:
        free = [i for i in range(count - 1) if holding[i] < reach]
        pool, budget = sum([loads[i] for i in free]), surplus
        for i in free:
            addition = min(reach - holding[i], max(1, budget * loads[i] // pool), surplus)
            holding[i] = holding[i] + addition
            surplus = surplus - addition
    return np.array([reach] + holding)


def ragged(key, number_of, total, bound, lean):
    if number_of == 2:
        one = jax.random.randint(key, (), max(1, total - bound), min(bound, total - 1) + 1)
        return jnp.stack([one, total - one])
    tallies = jnp.asarray(length_profile(number_of, total, bound, lean), jnp.int32)
    pairs = (number_of - 1) // 2
    source_of, taker = tallies[1:1 + 2 * pairs:2], tallies[2:2 + 2 * pairs:2]
    margin = jnp.minimum(source_of - 1, bound - taker)
    shifted = jax.random.randint(jax.random.fold_in(key, 1), (pairs,), 0, 1 << 20) % (margin + 1)
    tallies = tallies.at[1:1 + 2 * pairs:2].set(source_of - shifted).at[2:2 + 2 * pairs:2].set(taker + shifted)
    return tallies[jax.random.permutation(jax.random.fold_in(key, 2), number_of)]


def bell_draw(rng, extent, scale, bound, shards=(), kind=jnp.bfloat16):
    loudness = levels(rng, extent, shards, -0.22, 0.18) if shards else 1.0
    drawn = jax.random.normal(rng, extent, jnp.float32) * scale * loudness
    return jnp.minimum(jnp.maximum(drawn, -bound), bound).astype(kind)


def heavy_noise(key, dims, spread, limit, pieces, heavy, dtype=jnp.bfloat16):
    entries = spread * jax.random.normal(key, dims, jnp.float32)
    if pieces:
        entries = entries * levels(key, dims, pieces, -0.22, 0.18)
    return jnp.clip(spiked(entries, jax.random.fold_in(key, 3), *heavy), -limit, limit).astype(dtype)


def setup_inputs(seed: int = 0, part: int = 0) -> dict:
    splits = jax.random.split(jax.random.key(seed), 8)
    own_keys = jax.random.split(jax.random.fold_in(splits[7], part), 8)
    queries = bell_draw(own_keys[0], (NQ, D), 1.0, 6.0, ((1, 16),), jnp.float32)
    precond = heavy_noise(splits[1], (D, D), D ** -0.5, 0.125, ((0, 16),), (0, 1, 16, 2.0), jnp.float32)
    train = bell_draw(own_keys[2], (BROWS, NB, D), D ** -0.5, 0.09375, ((0, 16),))
    query_cluster = place_ends(jax.random.randint(own_keys[3], (NQ,), 0, NC), jax.random.fold_in(own_keys[3], 1), 0, NC - 1).astype(jnp.int32)
    cand_blocks = draw_cand_blocks(jax.random.fold_in(jax.random.fold_in(splits[7], part), 71), part)
    cand_count = ragged(own_keys[5], NC, NC * NB // 2, KMAX, 2).astype(jnp.int32)
    slot_block = jax.random.permutation(own_keys[6], NB).astype(jnp.int32)
    return {"queries": queries, "precond": precond, "train": train, "query_cluster": query_cluster, "cand_blocks": cand_blocks, "cand_count": cand_count, "slot_block": slot_block}


def listed_mask(query_cluster, cand_blocks, cand_count, nblocks):
    nclusters = cand_blocks.shape[0]
    valid = jnp.arange(cand_blocks.shape[1])[None, :] < cand_count[:, None]
    hits = (cand_blocks[:, :, None] == jnp.arange(nblocks)[None, None, :]) & valid[:, :, None]
    listed = jnp.any(hits, axis=1).astype(jnp.float32)
    onehot = (query_cluster[:, None] == jnp.arange(nclusters)[None, :]).astype(jnp.float32)
    return jnp.dot(listed.T, onehot.T, preferred_element_type=jnp.float32)


def reference(queries, precond, train, query_cluster, cand_blocks, cand_count, slot_block):
    prequery = jnp.dot(queries, precond, precision=lax.Precision.HIGHEST, preferred_element_type=jnp.float32).astype(jnp.bfloat16)
    allowed = listed_mask(query_cluster, cand_blocks, cand_count, train.shape[1])

    def one_slot(slot):
        block = slot_block[slot]
        tile = lax.dynamic_index_in_dim(train, block, 1, keepdims=False)
        raw = jnp.dot(tile, prequery.T, preferred_element_type=jnp.float32)
        row = lax.dynamic_index_in_dim(allowed, block, 0, keepdims=False)
        return raw * row[None, :]

    stacked = lax.map(one_slot, jnp.arange(train.shape[1]))
    return jnp.swapaxes(stacked, 0, 1)
```

```python
import jax
import jax.numpy as jnp
from jax import lax
from jax.sharding import PartitionSpec as P

CORES = 2
CHUNKS = 4
UNIT = 4.0


def listed_mask(query_cluster, cand_blocks, cand_count, nblocks):
    nclusters = cand_blocks.shape[0]
    valid = jnp.arange(cand_blocks.shape[1])[None, :] < cand_count[:, None]
    hits = (cand_blocks[:, :, None] == jnp.arange(nblocks)[None, None, :]) & valid[:, :, None]
    listed = jnp.any(hits, axis=1).astype(jnp.float32)
    onehot = (query_cluster[:, None] == jnp.arange(nclusters)[None, :]).astype(jnp.float32)
    return jnp.dot(listed.T, onehot.T, preferred_element_type=jnp.float32)


def shards(queries, precond, train, query_cluster, cand_blocks, cand_count, slot_block):
    n = lax.axis_size("rows")
    chips = n // CORES
    ny = 1 << ((chips.bit_length() - 1) // 2)
    nz = chips // ny
    me = lax.axis_index("rows")
    core = me % CORES
    y = (me // CORES) % ny
    z = me // (CORES * ny)

    examples, nblocks, width = train.shape
    nq = queries.shape[0]
    half = nq // CORES

    def swap(value, step):
        return lax.ppermute(value, "rows", [(r, r ^ step) for r in range(n)])

    def pack(value):
        return (value * UNIT).astype(jnp.float16)

    def unpack(value):
        return value.astype(jnp.float32) * (1.0 / UNIT)

    def reduce_scatter(value, place, count, stride):
        rows = value.shape[0] // count
        got = [
            swap(pack(lax.dynamic_slice_in_dim(value, (place ^ k) * rows, rows)), k * stride)
            for k in range(1, count)
        ]
        total = lax.dynamic_slice_in_dim(value, place * rows, rows)
        for part in got:
            total = total + unpack(part)
        return total

    def gather(value, place, count, stride):
        rows = value.shape[0]
        full = jnp.zeros((rows * count,) + value.shape[1:], value.dtype)
        full = lax.dynamic_update_slice_in_dim(full, value, place * rows, 0)
        for k in range(1, count):
            full = lax.dynamic_update_slice_in_dim(full, swap(value, k * stride), (place ^ k) * rows, 0)
        return full

    both = jnp.concatenate([train, swap(train, 1)], axis=0).reshape(CORES * examples * nblocks, width)

    mine = lax.dynamic_slice_in_dim(queries, core * half, half)
    other = lax.dynamic_slice_in_dim(queries, (1 - core) * half, half)

    def product(columns, rows):
        return lax.dot_general(
            columns, rows, (((0,), (1,)), ((), ())),
            precision=lax.Precision.HIGH, preferred_element_type=jnp.float32,
        )

    depth = width // CHUNKS
    prequery = []
    for chunk in range(CHUNKS):
        columns = precond[:, chunk * depth:(chunk + 1) * depth]
        sent = swap(pack(product(columns, other)), 1)
        value = product(columns, mine) + unpack(sent)
        value = reduce_scatter(value, y, ny, CORES)
        value = reduce_scatter(value, z, nz, CORES * ny)
        value = gather(value.astype(jnp.bfloat16), z, nz, CORES * ny)
        prequery.append(gather(value, y, ny, CORES))
    prequery = jnp.concatenate(prequery, axis=0)

    raw = jnp.dot(both, prequery, preferred_element_type=jnp.float32)
    raw = raw.reshape(CORES * examples, nblocks, half)
    ordered = jnp.take(jnp.swapaxes(raw, 0, 1), slot_block, axis=0, mode="clip")
    owned_count = nblocks // n
    ordered = ordered.reshape(n, owned_count, CORES * examples, half)
    got = lax.all_to_all(ordered, "rows", split_axis=0, concat_axis=0, tiled=True)
    got = got.reshape(chips, CORES, owned_count, CORES, examples, half)
    got = jnp.stack([got[:, 0], got[:, 1, :, ::-1]], axis=4)
    got = got.transpose(0, 2, 3, 1, 4, 5).reshape(n * examples, owned_count, nq)

    allowed = listed_mask(query_cluster, cand_blocks, cand_count, nblocks)
    slots = lax.dynamic_slice_in_dim(slot_block, me * owned_count, owned_count)
    return got * jnp.take(allowed, slots, axis=0, mode="clip")[None]


def solution(mesh):
    placed = (
        P("groups", "rows"),
        P("rows", None),
        P("rows", "groups", None),
        P("groups"),
        P("groups", None),
        P("groups"),
        P("groups"),
    )
    return jax.shard_map(
        shards,
        mesh=mesh,
        in_specs=placed,
        out_specs=P(None, ("groups", "rows"), None),
        check_vma=False,
    )
```

```python
import jax
import jax.numpy as jnp
from jax import lax
from jax.sharding import PartitionSpec as P

CORES = 2
UNIT = 4.0


def listed_mask(query_cluster, cand_blocks, cand_count, nblocks):
    nclusters = cand_blocks.shape[0]
    valid = jnp.arange(cand_blocks.shape[1])[None, :] < cand_count[:, None]
    hits = (cand_blocks[:, :, None] == jnp.arange(nblocks)[None, None, :]) & valid[:, :, None]
    listed = jnp.any(hits, axis=1).astype(jnp.float32)
    onehot = (query_cluster[:, None] == jnp.arange(nclusters)[None, :]).astype(jnp.float32)
    return jnp.dot(listed.T, onehot.T, preferred_element_type=jnp.float32)


def shards(queries, precond, train, query_cluster, cand_blocks, cand_count, slot_block):
    n = lax.axis_size("rows")
    chips = n // CORES
    bits = chips.bit_length() - 1
    ybits = [1 + b for b in range(bits // 2)]
    zbits = [1 + b for b in range(bits // 2, bits)]
    orders = (ybits + zbits, zbits[:1] + ybits + zbits[1:])
    me = lax.axis_index("rows")
    core = me & 1

    examples, nblocks, width = train.shape
    nq = queries.shape[0]
    half = nq // CORES

    def swap(value, bit):
        return lax.ppermute(value, "rows", [(r, r ^ (1 << bit)) for r in range(n)])

    def side(bit):
        return (me >> bit) & 1

    def pack(value):
        return (value * UNIT).astype(jnp.float16)

    def unpack(value):
        return value.astype(jnp.float32) * (1.0 / UNIT)

    def split(value, bit):
        rows = value.shape[0] // 2
        keep = lax.dynamic_slice_in_dim(value, side(bit) * rows, rows)
        give = lax.dynamic_slice_in_dim(value, (1 - side(bit)) * rows, rows)
        return keep, pack(give)

    def join(own, got, bit):
        rows = own.shape[0]
        full = jnp.zeros((2 * rows,) + own.shape[1:], own.dtype)
        full = lax.dynamic_update_slice_in_dim(full, own, side(bit) * rows, 0)
        return lax.dynamic_update_slice_in_dim(full, got, (1 - side(bit)) * rows, 0)

    def product(rows):
        return jnp.dot(rows, precond, precision=lax.Precision.HIGH, preferred_element_type=jnp.float32)

    part = half // 2
    mine = lax.dynamic_slice_in_dim(queries, core * half, half)
    other = lax.dynamic_slice_in_dim(queries, (1 - core) * half, half)
    sent = [swap(pack(product(other[i * part:(i + 1) * part])), 0) for i in range(2)]
    other_train = swap(train, 0)
    values = [product(mine[i * part:(i + 1) * part]) + unpack(sent[i]) for i in range(2)]

    for step in range(bits - 1):
        pieces = [split(values[i], orders[i][step]) for i in range(2)]
        got = [swap(pieces[i][1], orders[i][step]) for i in range(2)]
        values = [pieces[i][0] + unpack(got[i]) for i in range(2)]
    last = orders[0][-1]
    pieces = [split(value, last) for value in values]
    got = swap(jnp.concatenate([give for _, give in pieces]), last)
    kept = jnp.concatenate([keep for keep, _ in pieces])
    own = (kept + unpack(got)).astype(jnp.bfloat16)
    got = swap(own, last)
    rows = own.shape[0] // 2
    values = [join(own[i * rows:(i + 1) * rows], got[i * rows:(i + 1) * rows], last) for i in range(2)]
    for step in reversed(range(bits - 1)):
        got = [swap(values[i], orders[i][step]) for i in range(2)]
        values = [join(values[i], got[i], orders[i][step]) for i in range(2)]
    prequery = jnp.concatenate(values, axis=0)

    both = jnp.concatenate([train, other_train], axis=0).reshape(CORES * examples * nblocks, width)
    raw = lax.dot_general(both, prequery, (((1,), (1,)), ((), ())), preferred_element_type=jnp.float32)
    raw = raw.astype(jnp.bfloat16).reshape(CORES * examples, nblocks, half)
    ordered = jnp.take(jnp.swapaxes(raw, 0, 1), slot_block, axis=0, mode="clip")
    owned_count = nblocks // n
    ordered = ordered.reshape(n, owned_count, CORES * examples, half)
    got = lax.all_to_all(ordered, "rows", split_axis=0, concat_axis=0, tiled=True)
    got = got.reshape(chips, CORES, owned_count, CORES, examples, half)
    got = jnp.stack([got[:, 0], got[:, 1, :, ::-1]], axis=4)
    got = got.transpose(0, 2, 3, 1, 4, 5).reshape(n * examples, owned_count, nq)

    allowed = listed_mask(query_cluster, cand_blocks, cand_count, nblocks)
    slots = lax.dynamic_slice_in_dim(slot_block, me * owned_count, owned_count)
    return got.astype(jnp.float32) * jnp.take(allowed, slots, axis=0, mode="clip")[None]


def solution(mesh):
    placed = (
        P("groups", "rows"),
        P("rows", None),
        P("rows", "groups", None),
        P("groups"),
        P("groups", None),
        P("groups"),
        P("groups"),
    )
    return jax.shard_map(
        shards,
        mesh=mesh,
        in_specs=placed,
        out_specs=P(None, ("groups", "rows"), None),
        check_vma=False,
    )
```

```python
import jax
import jax.numpy as jnp
from jax import lax
from jax.experimental import pallas as pl
from jax.experimental.pallas import tpu as pltpu
from jax.sharding import PartitionSpec as P

CORES = 2
CHUNKS = 2
PATHS = 2
UNIT = 4.0


def listed_mask(query_cluster, cand_blocks, cand_count, nblocks):
    nclusters = cand_blocks.shape[0]
    valid = jnp.arange(cand_blocks.shape[1])[None, :] < cand_count[:, None]
    hits = (cand_blocks[:, :, None] == jnp.arange(nblocks)[None, None, :]) & valid[:, :, None]
    listed = jnp.any(hits, axis=1).astype(jnp.float32)
    onehot = (query_cluster[:, None] == jnp.arange(nclusters)[None, :]).astype(jnp.float32)
    return jnp.dot(listed.T, onehot.T, preferred_element_type=jnp.float32)


def product_kernel(rows_ref, columns_ref, out_ref, split_ref):
    nrows = rows_ref.shape[0]

    @pl.when(pl.program_id(0) == 0)
    def _():
        rows = rows_ref[...]
        high = rows.astype(jnp.bfloat16)
        split_ref[:nrows] = high
        split_ref[nrows:] = (rows - high.astype(jnp.float32)).astype(jnp.bfloat16)

    columns = columns_ref[...]
    high = columns.astype(jnp.bfloat16)
    low = (columns - high.astype(jnp.float32)).astype(jnp.bfloat16)
    both = jnp.dot(split_ref[...], high, preferred_element_type=jnp.float32)
    out_ref[...] = (
        both[:nrows] + both[nrows:] + jnp.dot(split_ref[:nrows], low, preferred_element_type=jnp.float32)
    )


def product(rows, columns):
    nrows, depth = rows.shape
    width = columns.shape[1]
    block = min(512, width)
    return pl.pallas_call(
        product_kernel,
        grid=(width // block,),
        in_specs=[
            pl.BlockSpec((nrows, depth), lambda i: (0, 0)),
            pl.BlockSpec((depth, block), lambda i: (0, i)),
        ],
        out_specs=pl.BlockSpec((nrows, block), lambda i: (0, i)),
        out_shape=jax.ShapeDtypeStruct((nrows, width), jnp.float32),
        scratch_shapes=[pltpu.VMEM((2 * nrows, depth), jnp.bfloat16)],
        compiler_params=pltpu.CompilerParams(vmem_limit_bytes=16 * 1024 * 1024),
        cost_estimate=pl.CostEstimate(
            flops=6 * nrows * depth * width, bytes_accessed=4 * width * (nrows + depth), transcendentals=0
        ),
    )(rows, columns)


def shards(queries, precond, train, query_cluster, cand_blocks, cand_count, slot_block):
    n = lax.axis_size("rows")
    chips = n // CORES
    bits = chips.bit_length() - 1
    ybits = [1 + b for b in range(bits // 2)]
    zbits = [1 + b for b in range(bits // 2, bits)]
    orders = (ybits + zbits, zbits[:1] + ybits + zbits[1:])
    me = lax.axis_index("rows")
    core = me & 1

    examples, nblocks, width = train.shape
    nq = queries.shape[0]
    half = nq // CORES

    def swap(value, bit):
        return lax.ppermute(value, "rows", [(r, r ^ (1 << bit)) for r in range(n)])

    def side(bit):
        return (me >> bit) & 1

    def pack(value):
        return (value * UNIT).astype(jnp.float16)

    def unpack(value):
        return value.astype(jnp.float32) * (1.0 / UNIT)

    def part(value, index, count):
        rows = value.shape[0] // count
        return lax.dynamic_slice_in_dim(value, index * rows, rows)

    def join(own, got, bit):
        rows = own.shape[0]
        full = jnp.zeros((2 * rows,) + own.shape[1:], own.dtype)
        full = lax.dynamic_update_slice_in_dim(full, own, side(bit) * rows, 0)
        return lax.dynamic_update_slice_in_dim(full, got, (1 - side(bit)) * rows, 0)

    def after(values, first):
        return list(lax.optimization_barrier((tuple(values), tuple(first)))[0])

    def messages(values, step):
        return [pack(part(values[i], 1 - side(orders[i][step]), 2)) for i in range(PATHS)]

    def exchange(values, sent, step):
        got = [swap(sent[i], orders[i][step]) for i in range(PATHS)]
        return [part(values[i], side(orders[i][step]), 2) + unpack(got[i]) for i in range(PATHS)]

    def gather(values, step):
        got = [swap(values[i], orders[i][step]) for i in range(PATHS)]
        return [join(values[i], got[i], orders[i][step]) for i in range(PATHS)]

    def whole(values):
        return pack(jnp.concatenate(values))

    def total(values, sent):
        got = swap(sent, orders[0][-1])
        rows = values[0].shape[0]
        return [
            (values[i] + unpack(got[i * rows:(i + 1) * rows])).astype(jnp.bfloat16) for i in range(PATHS)
        ]

    other_train = swap(train, 0)

    chunked = queries.reshape(CORES, CHUNKS, half // CHUNKS, queries.shape[1])
    values = []
    for chunk in range(CHUNKS):
        full = product(chunked[:, chunk].reshape(nq // CHUNKS, queries.shape[1]), precond)
        got = swap(pack(part(full, 1 - core, CORES)), 0)
        mixed = part(full, core, CORES) + unpack(got)
        rows = mixed.shape[0] // PATHS
        values.append([mixed[i * rows:(i + 1) * rows] for i in range(PATHS)])
    one, two = values

    steps = bits - 1
    sent = messages(one, 0)
    one = exchange(one, sent, 0)
    sent_two = after(messages(two, 0), one)
    two = exchange(two, sent_two, 0)
    for step in range(1, steps):
        one = exchange(one, messages(one, step), step)
        two = exchange(two, messages(two, step), step)
    one = total(one, whole(one))
    sent_two = whole(two)
    one = after(one, [sent_two])
    two = total(two, sent_two)
    for step in reversed(range(steps)):
        one = gather(one, step)
        if step:
            two = after(two, one)
        two = gather(two, step)
    prequery = jnp.concatenate(one + two, axis=0)

    both = jnp.concatenate([train, other_train], axis=0)
    both, _ = lax.optimization_barrier((both, sent))
    both = jnp.take(jnp.swapaxes(both, 0, 1), slot_block, axis=0, mode="clip")
    both = both.reshape(nblocks * CORES * examples, width)
    raw = lax.dot_general(both, prequery, (((1,), (1,)), ((), ())), preferred_element_type=jnp.float32)
    owned_count = nblocks // n
    ordered = raw.astype(jnp.bfloat16).reshape(n, owned_count, CORES * examples, half)
    got = lax.all_to_all(ordered, "rows", split_axis=0, concat_axis=0, tiled=True)
    got = got.reshape(chips, CORES, owned_count, CORES, examples, half)
    got = jnp.stack([got[:, 0], got[:, 1, :, ::-1]], axis=4)
    got = got.transpose(0, 2, 3, 1, 4, 5).reshape(n * examples, owned_count, nq)

    allowed = listed_mask(query_cluster, cand_blocks, cand_count, nblocks)
    slots = lax.dynamic_slice_in_dim(slot_block, me * owned_count, owned_count)
    return got.astype(jnp.float32) * jnp.take(allowed, slots, axis=0, mode="clip")[None]


def solution(mesh):
    placed = (
        P("groups", "rows"),
        P("rows", None),
        P("rows", "groups", None),
        P("groups"),
        P("groups", None),
        P("groups"),
        P("groups"),
    )
    return jax.shard_map(
        shards,
        mesh=mesh,
        in_specs=placed,
        out_specs=P(None, ("groups", "rows"), None),
        check_vma=False,
    )
```

```python
import jax
import jax.numpy as jnp
from jax import lax
from jax.experimental import pallas as pl
from jax.experimental.pallas import tpu as pltpu
from jax.sharding import PartitionSpec as P

CORES = 2
CHUNKS = 2
PATHS = 2
UNIT = 4.0
LANES = 128
PRODUCT_VMEM = 43


def listed_mask(query_cluster, cand_blocks, cand_count, nblocks):
    nclusters = cand_blocks.shape[0]
    valid = jnp.arange(cand_blocks.shape[1])[None, :] < cand_count[:, None]
    hits = (cand_blocks[:, :, None] == jnp.arange(nblocks)[None, None, :]) & valid[:, :, None]
    listed = jnp.any(hits, axis=1).astype(jnp.float32)
    onehot = (query_cluster[:, None] == jnp.arange(nclusters)[None, :]).astype(jnp.float32)
    return jnp.dot(listed.T, onehot.T, preferred_element_type=jnp.float32)


def product_kernel(rows_ref, columns_hbm, *refs):
    outs, (columns_ref, left_ref, right_ref, sems) = refs[:-4], refs[-4:]
    depth = rows_ref.shape[-1]
    nrows = rows_ref.size // depth
    steps, _, block = columns_ref.shape
    step = pl.program_id(0)

    def load(i):
        return pltpu.make_async_copy(
            columns_hbm.at[:, pl.ds(pl.multiple_of(i * block, block), block)], columns_ref.at[i], sems.at[i]
        )

    @pl.when(step == 0)
    def _():
        for i in range(steps):
            load(i).start()
        rows = rows_ref[...].reshape(nrows, depth)
        high = rows.astype(jnp.bfloat16)
        left_ref[:, :depth] = high
        left_ref[:, depth:2 * depth] = (rows - high.astype(jnp.float32)).astype(jnp.bfloat16)
        left_ref[:, 2 * depth:] = high

    load(step).wait()
    columns = columns_ref[step]
    high = columns.astype(jnp.bfloat16)
    right_ref[:depth] = high
    right_ref[depth:2 * depth] = high
    right_ref[2 * depth:] = (columns - high.astype(jnp.float32)).astype(jnp.bfloat16)
    result = jnp.dot(left_ref[...], right_ref[...], preferred_element_type=jnp.float32)
    result = result.reshape(CORES, CHUNKS, nrows // CORES // CHUNKS, block)
    for chunk, out_ref in enumerate(outs):
        out_ref[...] = result[:, chunk]


def product(rows, columns):
    nrows, depth = rows.shape
    width = columns.shape[1]
    block = min(512, width)
    part = nrows // CORES // CHUNKS
    return pl.pallas_call(
        product_kernel,
        grid=(width // block,),
        in_specs=[
            pl.BlockSpec((nrows, depth), lambda i: (0, 0)),
            pl.BlockSpec(memory_space=pltpu.HBM),
        ],
        out_specs=[pl.BlockSpec((CORES, part, block), lambda i: (0, 0, i))] * CHUNKS,
        out_shape=[jax.ShapeDtypeStruct((CORES, part, width), jnp.float32)] * CHUNKS,
        scratch_shapes=[
            pltpu.VMEM((width // block, depth, block), jnp.float32),
            pltpu.VMEM((nrows, 3 * depth), jnp.bfloat16),
            pltpu.VMEM((3 * depth, block), jnp.bfloat16),
            pltpu.SemaphoreType.DMA((width // block,)),
        ],
        compiler_params=pltpu.CompilerParams(vmem_limit_bytes=PRODUCT_VMEM * 1024 * 1024),
        cost_estimate=pl.CostEstimate(
            flops=6 * nrows * depth * width, bytes_accessed=4 * width * (nrows + depth), transcendentals=0
        ),
    )(rows, columns)


def order_kernel(slots_ref, raw_ref, out_ref, lanes_ref):
    nblocks, examples, _ = out_ref.shape
    parts = lanes_ref.shape[0]
    for i in range(parts):
        lanes_ref[i] = raw_ref[:, i * LANES:(i + 1) * LANES]
    for slot in range(nblocks):
        rows = pl.ds(slots_ref[slot], examples, stride=nblocks)
        for i in range(parts):
            out_ref[slot, :, i * LANES:(i + 1) * LANES] = lanes_ref[i, rows, :].astype(out_ref.dtype)


def in_slot_order(raw, slots):
    nblocks = slots.shape[0]
    examples = raw.shape[0] // nblocks
    return pl.pallas_call(
        order_kernel,
        in_specs=[pl.BlockSpec(memory_space=pltpu.SMEM), pl.BlockSpec(memory_space=pltpu.VMEM)],
        out_specs=pl.BlockSpec(memory_space=pltpu.VMEM),
        out_shape=jax.ShapeDtypeStruct((nblocks, examples, raw.shape[1]), jnp.bfloat16),
        scratch_shapes=[pltpu.VMEM((raw.shape[1] // LANES, raw.shape[0], LANES), jnp.float32)],
        compiler_params=pltpu.CompilerParams(vmem_limit_bytes=4 * 1024 * 1024),
        cost_estimate=pl.CostEstimate(flops=raw.size, bytes_accessed=6 * raw.size, transcendentals=0),
    )(slots, raw)


def finish_kernel(got_ref, allowed_ref, out_ref):
    chips, cores, owned, rows, half = got_ref.shape
    parts = half // LANES
    per_row = owned * cores * parts
    for chip in range(chips):
        for core in range(cores):
            for slot in range(owned):
                scores = got_ref[chip, core, slot].astype(jnp.float32)
                if core:
                    scores = jnp.concatenate([scores[rows // 2:], scores[:rows // 2]], axis=0)
                scores = scores * allowed_ref[slot:slot + 1, core * half:(core + 1) * half]
                for i in range(parts):
                    first = chip * rows * per_row + slot * cores * parts + core * parts + i
                    out_ref[pl.ds(first, rows, stride=per_row), :] = scores[:, i * LANES:(i + 1) * LANES]


def finish(got, allowed):
    chips, cores, owned, rows, half = got.shape
    flat = pl.pallas_call(
        finish_kernel,
        out_shape=jax.ShapeDtypeStruct((chips * rows * owned * cores * half // LANES, LANES), jnp.float32),
        compiler_params=pltpu.CompilerParams(vmem_limit_bytes=4 * 1024 * 1024),
        cost_estimate=pl.CostEstimate(flops=got.size, bytes_accessed=6 * got.size, transcendentals=0),
    )(got, allowed)
    return flat.reshape(chips * rows, owned, cores * half)


def shards(queries, precond, train, query_cluster, cand_blocks, cand_count, slot_block):
    n = lax.axis_size("rows")
    chips = n // CORES
    bits = chips.bit_length() - 1
    ybits = [1 + b for b in range(bits // 2)]
    zbits = [1 + b for b in range(bits // 2, bits)]
    orders = (ybits + zbits, zbits[:1] + ybits + zbits[1:])
    me = lax.axis_index("rows")
    core = me & 1

    examples, nblocks, width = train.shape
    nq = queries.shape[0]
    half = nq // CORES

    def swap(value, bit):
        return lax.ppermute(value, "rows", [(r, r ^ (1 << bit)) for r in range(n)])

    def side(bit):
        return (me >> bit) & 1

    def pack(value):
        return (value * UNIT).astype(jnp.float16)

    def unpack(value):
        return value.astype(jnp.float32) * (1.0 / UNIT)

    def part(value, index, count):
        rows = value.shape[0] // count
        return lax.dynamic_slice_in_dim(value, index * rows, rows)

    def join(own, got, bit):
        rows = own.shape[0]
        full = jnp.zeros((2 * rows,) + own.shape[1:], own.dtype)
        full = lax.dynamic_update_slice_in_dim(full, own, side(bit) * rows, 0)
        return lax.dynamic_update_slice_in_dim(full, got, (1 - side(bit)) * rows, 0)

    def after(values, first):
        return list(lax.optimization_barrier((tuple(values), tuple(first)))[0])

    def messages(values, step):
        return [pack(part(values[i], 1 - side(orders[i][step]), 2)) for i in range(PATHS)]

    def exchange(values, sent, step):
        got = [swap(sent[i], orders[i][step]) for i in range(PATHS)]
        return [part(values[i], side(orders[i][step]), 2) + unpack(got[i]) for i in range(PATHS)]

    def gather(values, step):
        got = [swap(values[i], orders[i][step]) for i in range(PATHS)]
        return [join(values[i], got[i], orders[i][step]) for i in range(PATHS)]

    def whole(values):
        return pack(jnp.concatenate(values))

    def total(values, sent):
        got = swap(sent, orders[0][-1])
        rows = values[0].shape[0]
        return [
            (values[i] + unpack(got[i * rows:(i + 1) * rows])).astype(jnp.bfloat16) for i in range(PATHS)
        ]

    products = product(queries, precond)
    sent = [swap(pack(lax.dynamic_index_in_dim(full, 1 - core, 0, False)), 0) for full in products]
    values = []
    for chunk in range(CHUNKS):
        mixed = lax.dynamic_index_in_dim(products[chunk], core, 0, False) + unpack(sent[chunk])
        rows = mixed.shape[0] // PATHS
        values.append([mixed[i * rows:(i + 1) * rows] for i in range(PATHS)])
    one, two = values

    steps = bits - 1
    sent = messages(one, 0)
    train = after([train], sent)[0]
    other_train = swap(train, 0)
    one = exchange(one, sent, 0)
    sent_two = after(messages(two, 0), one)
    two = exchange(two, sent_two, 0)
    for step in range(1, steps):
        one = exchange(one, messages(one, step), step)
        two = exchange(two, messages(two, step), step)
    one = total(one, whole(one))
    sent_two = whole(two)
    one = after(one, [sent_two])
    two = total(two, sent_two)
    for step in reversed(range(steps)):
        one = gather(one, step)
        if step:
            two = after(two, one)
        two = gather(two, step)
    prequery = jnp.concatenate(one + two, axis=0)

    both = jnp.concatenate([train, other_train], axis=0).reshape(CORES * examples * nblocks, width)
    raw = lax.dot_general(both, prequery, (((1,), (1,)), ((), ())), preferred_element_type=jnp.float32)
    owned = nblocks // n
    ordered = in_slot_order(raw, slot_block).reshape(n, owned, CORES * examples, half)
    got = lax.all_to_all(ordered, "rows", split_axis=0, concat_axis=0, tiled=True)

    allowed = listed_mask(query_cluster, cand_blocks, cand_count, nblocks)
    slots = lax.dynamic_slice_in_dim(slot_block, me * owned, owned)
    own_allowed = jnp.take(allowed, slots, axis=0, mode="clip")
    return finish(got.reshape(chips, CORES, owned, CORES * examples, half), own_allowed)


def solution(mesh):
    placed = (
        P("groups", "rows"),
        P("rows", None),
        P("rows", "groups", None),
        P("groups"),
        P("groups", None),
        P("groups"),
        P("groups"),
    )
    return jax.shard_map(
        shards,
        mesh=mesh,
        in_specs=placed,
        out_specs=P(None, ("groups", "rows"), None),
        check_vma=False,
    )
```

```python
import jax
import jax.numpy as jnp
from jax import lax
from jax.experimental import pallas as pl
from jax.experimental.pallas import tpu as pltpu
from jax.sharding import PartitionSpec as P

CORES = 2
CHUNKS = 2
UNIT = 4.0
LANES = 128
OTHER_VMEM = 47
MINE_VMEM = 43


def listed_mask(query_cluster, cand_blocks, cand_count, nblocks):
    nclusters = cand_blocks.shape[0]
    valid = jnp.arange(cand_blocks.shape[1])[None, :] < cand_count[:, None]
    hits = (cand_blocks[:, :, None] == jnp.arange(nblocks)[None, None, :]) & valid[:, :, None]
    listed = jnp.any(hits, axis=1).astype(jnp.float32)
    onehot = (query_cluster[:, None] == jnp.arange(nclusters)[None, :]).astype(jnp.float32)
    return jnp.dot(listed.T, onehot.T, preferred_element_type=jnp.float32)


def product_kernel(core_ref, rows_ref, columns_hbm, *refs):
    outs, (columns_ref, sems) = refs[:-2], refs[-2:]
    steps, _, block = columns_ref.shape

    def load(i):
        return pltpu.make_async_copy(
            columns_hbm.at[:, i * block:(i + 1) * block], columns_ref.at[i], sems.at[i]
        )

    for i in range(steps):
        load(i).start()
    half = rows_ref.shape[0] // CORES
    rows = rows_ref[pl.ds(pl.multiple_of(core_ref[0] * half, half), half), :]
    high = rows.astype(jnp.bfloat16)
    low = (rows - high.astype(jnp.float32)).astype(jnp.bfloat16)
    left = jnp.concatenate([high, low, high], axis=1)
    part = half // len(outs)
    for i in range(steps):
        load(i).wait()
        columns = columns_ref[i]
        high = columns.astype(jnp.bfloat16)
        low = (columns - high.astype(jnp.float32)).astype(jnp.bfloat16)
        right = jnp.concatenate([high, high, low], axis=0)
        result = jnp.dot(left, right, preferred_element_type=jnp.float32)
        for chunk, out_ref in enumerate(outs):
            out_ref[:, i * block:(i + 1) * block] = result[chunk * part:(chunk + 1) * part]


def product(core, rows, columns, vmem):
    nrows, depth = rows.shape
    width = columns.shape[1]
    block = min(512, width)
    part = nrows // CORES // CHUNKS
    return pl.pallas_call(
        product_kernel,
        in_specs=[
            pl.BlockSpec(memory_space=pltpu.SMEM),
            pl.BlockSpec(memory_space=pltpu.VMEM),
            pl.BlockSpec(memory_space=pltpu.HBM),
        ],
        out_specs=[pl.BlockSpec(memory_space=pltpu.VMEM)] * CHUNKS,
        out_shape=[jax.ShapeDtypeStruct((part, width), jnp.float32)] * CHUNKS,
        scratch_shapes=[
            pltpu.VMEM((width // block, depth, block), jnp.float32),
            pltpu.SemaphoreType.DMA((width // block,)),
        ],
        compiler_params=pltpu.CompilerParams(vmem_limit_bytes=vmem * 1024 * 1024),
        cost_estimate=pl.CostEstimate(
            flops=3 * nrows * depth * width,
            bytes_accessed=4 * width * depth + 2 * width * nrows,
            transcendentals=0,
        ),
    )(core.reshape(1), rows, columns)


def pieces_kernel(order_ref, *refs):
    raws, outs = refs[:CHUNKS], refs[CHUNKS:]
    nblocks = order_ref.shape[0]
    owned = nblocks // len(outs)
    for k, out_ref in enumerate(outs):
        for slot in range(owned):
            examples = out_ref.shape[1]
            rows = pl.ds(order_ref[k * owned + slot], examples, stride=nblocks)
            for i in range(CHUNKS):
                width = raws[i].shape[1]
                out_ref[slot, :, i * width:(i + 1) * width] = raws[i][rows, :].astype(out_ref.dtype)


def pieces(raws, order, n):
    nblocks = order.shape[0]
    rows, width = raws[0].shape
    shape = jax.ShapeDtypeStruct((nblocks // n, rows // nblocks, CHUNKS * width), jnp.bfloat16)
    return pl.pallas_call(
        pieces_kernel,
        in_specs=[pl.BlockSpec(memory_space=pltpu.SMEM)] + [pl.BlockSpec(memory_space=pltpu.VMEM)] * CHUNKS,
        out_specs=[pl.BlockSpec(memory_space=pltpu.VMEM)] * n,
        out_shape=[shape] * n,
        compiler_params=pltpu.CompilerParams(vmem_limit_bytes=4 * 1024 * 1024),
        cost_estimate=pl.CostEstimate(flops=rows * width, bytes_accessed=12 * rows * width, transcendentals=0),
    )(order, *raws)


def finish_kernel(me_ref, allowed_ref, *refs):
    got, out_ref = refs[:-1], refs[-1]
    owned, rows, half = got[0].shape
    parts = half // LANES
    per_row = owned * CORES * parts
    examples = rows // CORES
    for k, got_ref in enumerate(got):
        source = me_ref[0] ^ k
        core = source & 1
        for slot in range(owned):
            scores = got_ref[slot].astype(jnp.float32)
            for i in range(parts):
                allowed = allowed_ref[pl.ds(slot * CORES * parts + core * parts + i, 1), :]
                lanes = scores[:, i * LANES:(i + 1) * LANES] * allowed
                for j in range(CORES):
                    first = ((source >> 1) * CORES + (core ^ j)) * examples * per_row
                    first = first + (slot * CORES + core) * parts + i
                    out_ref[pl.ds(first, examples, stride=per_row), :] = lanes[j * examples:(j + 1) * examples]


def finish(me, allowed, got):
    owned, rows, half = got[0].shape
    total = len(got) * rows * half
    flat = pl.pallas_call(
        finish_kernel,
        in_specs=[pl.BlockSpec(memory_space=pltpu.SMEM)]
        + [pl.BlockSpec(memory_space=pltpu.VMEM)] * (1 + len(got)),
        out_specs=pl.BlockSpec(memory_space=pltpu.VMEM),
        out_shape=jax.ShapeDtypeStruct((owned * total // LANES, LANES), jnp.float32),
        compiler_params=pltpu.CompilerParams(vmem_limit_bytes=4 * 1024 * 1024),
        cost_estimate=pl.CostEstimate(flops=total, bytes_accessed=6 * total, transcendentals=0),
    )(me.reshape(1), allowed.reshape(-1, LANES), *got)
    return flat.reshape(len(got) * rows // CORES, owned, CORES * half)


def shards(queries, precond, train, query_cluster, cand_blocks, cand_count, slot_block):
    n = lax.axis_size("rows")
    chips = n // CORES
    bits = chips.bit_length() - 1
    ybits = [1 + b for b in range(bits // 2)]
    zbits = [1 + b for b in range(bits // 2, bits)]
    orders = (ybits + zbits, zbits[:1] + ybits + zbits[1:])
    me = lax.axis_index("rows")
    core = me & 1

    examples, nblocks, width = train.shape
    nq = queries.shape[0]

    def swap(value, step):
        return lax.ppermute(value, "rows", [(r, r ^ step) for r in range(n)])

    def swap_level(value, step):
        return lax.ppermute(value, "rows", [(r, r ^ (1 << orders[r & 1][step])) for r in range(n)])

    def side(step):
        return jnp.where(core == 0, (me >> orders[0][step]) & 1, (me >> orders[1][step]) & 1)

    def pack(value):
        return (value * UNIT).astype(jnp.float16)

    def unpack(value):
        return value.astype(jnp.float32) * (1.0 / UNIT)

    def part(value, index):
        rows = value.shape[0] // 2
        return lax.dynamic_slice_in_dim(value, index * rows, rows)

    def join(own, got, index):
        rows = own.shape[0]
        full = jnp.zeros((2 * rows,) + own.shape[1:], own.dtype)
        full = lax.dynamic_update_slice_in_dim(full, own, index * rows, 0)
        return lax.dynamic_update_slice_in_dim(full, got, (1 - index) * rows, 0)

    def after(value, first):
        return lax.optimization_barrier((value, first))[0]

    def message(value, step):
        return pack(part(value, 1 - side(step)))

    def exchange(value, sent, step):
        return part(value, side(step)) + unpack(swap_level(sent, step))

    def total(value, sent):
        return (value + unpack(swap_level(sent, bits - 1))).astype(jnp.bfloat16)

    def gather(value, step):
        return join(value, swap_level(value, step), side(step))

    sent = [pack(value) for value in product(1 - core, queries, precond, OTHER_VMEM)]
    got = [swap(value, 1) for value in sent]
    mine = product(core, after(queries, sent[0]), precond, MINE_VMEM)
    one, two = [value + unpack(other) for value, other in zip(mine, got)]

    steps = bits - 1
    sent = message(one, 0)
    train = after(train, sent)
    other_train = swap(train, 1)
    one = exchange(one, sent, 0)
    two = exchange(two, after(message(two, 0), one), 0)
    for step in range(1, steps):
        one = exchange(one, message(one, step), step)
        two = exchange(two, message(two, step), step)
    one = total(one, pack(one))
    sent = pack(two)
    one = after(one, sent)
    two = total(two, sent)
    for step in reversed(range(steps)):
        one = gather(one, step)
        if step:
            two = after(two, one)
        two = gather(two, step)

    both = jnp.concatenate([train, other_train], axis=0).reshape(CORES * examples * nblocks, width)
    raws = [
        lax.dot_general(both, value, (((1,), (1,)), ((), ())), preferred_element_type=jnp.float32)
        for value in (one, two)
    ]
    owned = nblocks // n
    order = jnp.take(slot_block.reshape(n, owned), me ^ jnp.arange(n), axis=0, mode="clip").reshape(nblocks)
    parts = pieces(raws, order, n)
    got = [None] * n
    got[0] = parts[0]
    for k in reversed(range(1, n)):
        got[k] = swap(parts[k], k)

    allowed = listed_mask(query_cluster, cand_blocks, cand_count, nblocks)
    slots = lax.dynamic_slice_in_dim(slot_block, me * owned, owned)
    own_allowed = jnp.take(allowed, slots, axis=0, mode="clip")
    return finish(me, own_allowed, got)


def solution(mesh):
    placed = (
        P("groups", "rows"),
        P("rows", None),
        P("rows", "groups", None),
        P("groups"),
        P("groups", None),
        P("groups"),
        P("groups"),
    )
    return jax.shard_map(
        shards,
        mesh=mesh,
        in_specs=placed,
        out_specs=P(None, ("groups", "rows"), None),
        check_vma=False,
    )
```

```python
import jax
import jax.numpy as jnp
from jax import lax
from jax.experimental import pallas as pl
from jax.experimental.pallas import tpu as pltpu
from jax.sharding import PartitionSpec as P

CORES = 2
CHUNKS = 2
PATHS = 2
UNIT = 4.0
LANES = 128
OTHER_VMEM = 48
MINE_VMEM = 47


def listed_mask(query_cluster, cand_blocks, cand_count, nblocks):
    nclusters = cand_blocks.shape[0]
    valid = jnp.arange(cand_blocks.shape[1])[None, :] < cand_count[:, None]
    hits = (cand_blocks[:, :, None] == jnp.arange(nblocks)[None, None, :]) & valid[:, :, None]
    listed = jnp.any(hits, axis=1).astype(jnp.float32)
    onehot = (query_cluster[:, None] == jnp.arange(nclusters)[None, :]).astype(jnp.float32)
    return jnp.dot(listed.T, onehot.T, preferred_element_type=jnp.float32)


def product_kernel(core_ref, rows_ref, columns_hbm, *refs):
    outs, (columns_ref, sems) = refs[:-2], refs[-2:]
    steps, _, block = columns_ref.shape

    def load(i):
        return pltpu.make_async_copy(
            columns_hbm.at[:, i * block:(i + 1) * block], columns_ref.at[i], sems.at[i]
        )

    for i in range(steps):
        load(i).start()
    half = rows_ref.shape[0] // CORES
    rows = rows_ref[pl.ds(pl.multiple_of(core_ref[0] * half, half), half), :]
    high = rows.astype(jnp.bfloat16)
    low = (rows - high.astype(jnp.float32)).astype(jnp.bfloat16)
    left = jnp.concatenate([high, low, high], axis=1)
    part = half // len(outs)
    for i in range(steps):
        load(i).wait()
        columns = columns_ref[i]
        high = columns.astype(jnp.bfloat16)
        low = (columns - high.astype(jnp.float32)).astype(jnp.bfloat16)
        right = jnp.concatenate([high, high, low], axis=0)
        result = jnp.dot(left, right, preferred_element_type=jnp.float32)
        for chunk, out_ref in enumerate(outs):
            out_ref[:, i * block:(i + 1) * block] = result[chunk * part:(chunk + 1) * part]


def product(core, rows, columns, vmem):
    nrows, depth = rows.shape
    width = columns.shape[1]
    block = min(512, width)
    part = nrows // CORES // CHUNKS
    return pl.pallas_call(
        product_kernel,
        in_specs=[
            pl.BlockSpec(memory_space=pltpu.SMEM),
            pl.BlockSpec(memory_space=pltpu.VMEM),
            pl.BlockSpec(memory_space=pltpu.HBM),
        ],
        out_specs=[pl.BlockSpec(memory_space=pltpu.VMEM)] * CHUNKS,
        out_shape=[jax.ShapeDtypeStruct((part, width), jnp.float32)] * CHUNKS,
        scratch_shapes=[
            pltpu.VMEM((width // block, depth, block), jnp.float32),
            pltpu.SemaphoreType.DMA((width // block,)),
        ],
        compiler_params=pltpu.CompilerParams(vmem_limit_bytes=vmem * 1024 * 1024),
        cost_estimate=pl.CostEstimate(
            flops=3 * nrows * depth * width,
            bytes_accessed=4 * width * depth + 2 * width * nrows,
            transcendentals=0,
        ),
    )(core.reshape(1), rows, columns)


def order_kernel(slots_ref, *refs):
    raws, out_ref = refs[:-1], refs[-1]
    nblocks, examples, _ = out_ref.shape
    for slot in range(nblocks):
        rows = pl.ds(slots_ref[slot], examples, stride=nblocks)
        for i, raw_ref in enumerate(raws):
            width = raw_ref.shape[1]
            out_ref[slot, :, i * width:(i + 1) * width] = raw_ref[rows, :].astype(out_ref.dtype)


def in_slot_order(raws, slots):
    nblocks = slots.shape[0]
    rows, width = raws[0].shape
    return pl.pallas_call(
        order_kernel,
        in_specs=[pl.BlockSpec(memory_space=pltpu.SMEM)] + [pl.BlockSpec(memory_space=pltpu.VMEM)] * CHUNKS,
        out_specs=pl.BlockSpec(memory_space=pltpu.VMEM),
        out_shape=jax.ShapeDtypeStruct((nblocks, rows // nblocks, CHUNKS * width), jnp.bfloat16),
        compiler_params=pltpu.CompilerParams(vmem_limit_bytes=4 * 1024 * 1024),
        cost_estimate=pl.CostEstimate(flops=rows * width, bytes_accessed=12 * rows * width, transcendentals=0),
    )(slots, *raws)


def finish_kernel(got_ref, allowed_ref, out_ref):
    chips, cores, owned, rows, half = got_ref.shape
    parts = half // LANES
    per_row = owned * cores * parts
    for chip in range(chips):
        for core in range(cores):
            for slot in range(owned):
                scores = got_ref[chip, core, slot].astype(jnp.float32)
                if core:
                    scores = jnp.concatenate([scores[rows // 2:], scores[:rows // 2]], axis=0)
                scores = scores * allowed_ref[slot:slot + 1, core * half:(core + 1) * half]
                for i in range(parts):
                    first = chip * rows * per_row + slot * cores * parts + core * parts + i
                    out_ref[pl.ds(first, rows, stride=per_row), :] = scores[:, i * LANES:(i + 1) * LANES]


def finish(got, allowed):
    chips, cores, owned, rows, half = got.shape
    flat = pl.pallas_call(
        finish_kernel,
        out_shape=jax.ShapeDtypeStruct((chips * rows * owned * cores * half // LANES, LANES), jnp.float32),
        compiler_params=pltpu.CompilerParams(vmem_limit_bytes=4 * 1024 * 1024),
        cost_estimate=pl.CostEstimate(flops=got.size, bytes_accessed=6 * got.size, transcendentals=0),
    )(got, allowed)
    return flat.reshape(chips * rows, owned, cores * half)


def shards(queries, precond, train, query_cluster, cand_blocks, cand_count, slot_block):
    n = lax.axis_size("rows")
    chips = n // CORES
    bits = chips.bit_length() - 1
    ybits = [1 + b for b in range(bits // 2)]
    zbits = [1 + b for b in range(bits // 2, bits)]
    orders = (ybits + zbits, zbits[:1] + ybits + zbits[1:])
    me = lax.axis_index("rows")
    core = me & 1

    examples, nblocks, width = train.shape
    nq = queries.shape[0]

    def swap(value, bit):
        return lax.ppermute(value, "rows", [(r, r ^ (1 << bit)) for r in range(n)])

    def side(bit):
        return (me >> bit) & 1

    def pack(value):
        return (value * UNIT).astype(jnp.float16)

    def unpack(value):
        return value.astype(jnp.float32) * (1.0 / UNIT)

    def part(value, index):
        rows = value.shape[0] // 2
        return lax.dynamic_slice_in_dim(value, index * rows, rows)

    def join(own, got, index):
        rows = own.shape[0]
        full = jnp.zeros((2 * rows,) + own.shape[1:], own.dtype)
        full = lax.dynamic_update_slice_in_dim(full, own, index * rows, 0)
        return lax.dynamic_update_slice_in_dim(full, got, (1 - index) * rows, 0)

    def after(value, first):
        return lax.optimization_barrier((value, first))[0]

    def messages(values, step):
        return [pack(part(value, 1 - side(order[step]))) for value, order in zip(values, orders)]

    def exchange(values, sent, step):
        got = [swap(message, order[step]) for message, order in zip(sent, orders)]
        return [
            part(value, side(order[step])) + unpack(message)
            for value, message, order in zip(values, got, orders)
        ]

    def gather(values, step):
        got = [swap(value, order[step]) for value, order in zip(values, orders)]
        return [join(value, message, side(order[step])) for value, message, order in zip(values, got, orders)]

    def whole(values):
        return pack(jnp.concatenate(values))

    def total(values, got):
        rows = values[0].shape[0]
        return [
            (value + unpack(got[i * rows:(i + 1) * rows])).astype(jnp.bfloat16)
            for i, value in enumerate(values)
        ]

    sent = [pack(value) for value in product(1 - core, queries, precond, OTHER_VMEM)]
    got = [swap(value, 0) for value in sent]
    mine = product(core, after(queries, sent[0]), precond, MINE_VMEM)
    rows = mine[0].shape[0] // PATHS

    def paths(value, other):
        value = value + unpack(other)
        return [value[i * rows:(i + 1) * rows] for i in range(PATHS)]

    steps = bits - 1
    last = orders[0][-1]
    one = paths(mine[0], got[0])
    sent = messages(one, 0)
    two = paths(mine[1], after(got[1], sent))
    one = exchange(one, sent, 0)
    for step in range(1, steps):
        one = exchange(one, messages(one, step), step)
    sent = whole(one)
    train, two = after((train, two), sent)
    got_one = swap(sent, last)
    for step in range(steps):
        two = exchange(two, messages(two, step), step)
    other_train = swap(train, 0)
    sent = whole(two)
    one = after(total(one, got_one), sent)
    two = total(two, swap(sent, last))
    both = jnp.concatenate([train, other_train], axis=0).reshape(CORES * examples * nblocks, width)
    two = after(two, both)
    for step in reversed(range(steps)):
        one = gather(one, step)
        if step:
            two = after(two, one)
        two = gather(two, step)

    raws = [
        lax.dot_general(
            both, jnp.concatenate(values), (((1,), (1,)), ((), ())), preferred_element_type=jnp.float32
        )
        for values in (one, two)
    ]
    owned = nblocks // n
    ordered = in_slot_order(raws, slot_block).reshape(n, owned, CORES * examples, nq // CORES)
    got = lax.all_to_all(ordered, "rows", split_axis=0, concat_axis=0, tiled=True)

    allowed = listed_mask(query_cluster, cand_blocks, cand_count, nblocks)
    slots = lax.dynamic_slice_in_dim(slot_block, me * owned, owned)
    own_allowed = jnp.take(allowed, slots, axis=0, mode="clip")
    return finish(got.reshape(chips, CORES, owned, CORES * examples, nq // CORES), own_allowed)


def solution(mesh):
    placed = (
        P("groups", "rows"),
        P("rows", None),
        P("rows", "groups", None),
        P("groups"),
        P("groups", None),
        P("groups"),
        P("groups"),
    )
    return jax.shard_map(
        shards,
        mesh=mesh,
        in_specs=placed,
        out_specs=P(None, ("groups", "rows"), None),
        check_vma=False,
    )
```

```python
import jax
import jax.numpy as jnp
from jax import lax
from jax.experimental import pallas as pl
from jax.experimental.pallas import tpu as pltpu
from jax.sharding import PartitionSpec as P

CORES = 2
CHUNKS = 2
PATHS = 2
UNIT = 4.0
LANES = 128
OTHER_VMEM = 48
MINE_VMEM = 44


def listed_mask(query_cluster, cand_blocks, cand_count, nblocks):
    nclusters = cand_blocks.shape[0]
    valid = jnp.arange(cand_blocks.shape[1])[None, :] < cand_count[:, None]
    hits = (cand_blocks[:, :, None] == jnp.arange(nblocks)[None, None, :]) & valid[:, :, None]
    listed = jnp.any(hits, axis=1).astype(jnp.float32)
    onehot = (query_cluster[:, None] == jnp.arange(nclusters)[None, :]).astype(jnp.float32)
    return jnp.dot(listed.T, onehot.T, preferred_element_type=jnp.float32)


def product_kernel(core_ref, rows_ref, columns_hbm, *refs):
    outs, (columns_ref, sems) = refs[:-2], refs[-2:]
    steps, _, block = columns_ref.shape

    def load(i):
        return pltpu.make_async_copy(
            columns_hbm.at[:, i * block:(i + 1) * block], columns_ref.at[i], sems.at[i]
        )

    for i in range(steps):
        load(i).start()
    half = rows_ref.shape[0] // CORES
    rows = rows_ref[pl.ds(pl.multiple_of(core_ref[0] * half, half), half), :]
    high = rows.astype(jnp.bfloat16)
    low = (rows - high.astype(jnp.float32)).astype(jnp.bfloat16)
    left = jnp.concatenate([high, low, high], axis=1)
    part = half // len(outs)
    for i in range(steps):
        load(i).wait()
        columns = columns_ref[i]
        high = columns.astype(jnp.bfloat16)
        low = (columns - high.astype(jnp.float32)).astype(jnp.bfloat16)
        right = jnp.concatenate([high, high, low], axis=0)
        result = jnp.dot(left, right, preferred_element_type=jnp.float32)
        for chunk, out_ref in enumerate(outs):
            out_ref[:, i * block:(i + 1) * block] = result[chunk * part:(chunk + 1) * part]


def product(core, rows, columns, vmem):
    nrows, depth = rows.shape
    width = columns.shape[1]
    block = min(512, width)
    part = nrows // CORES // CHUNKS
    return pl.pallas_call(
        product_kernel,
        in_specs=[
            pl.BlockSpec(memory_space=pltpu.SMEM),
            pl.BlockSpec(memory_space=pltpu.VMEM),
            pl.BlockSpec(memory_space=pltpu.HBM),
        ],
        out_specs=[pl.BlockSpec(memory_space=pltpu.VMEM)] * CHUNKS,
        out_shape=[jax.ShapeDtypeStruct((part, width), jnp.float32)] * CHUNKS,
        scratch_shapes=[
            pltpu.VMEM((width // block, depth, block), jnp.float32),
            pltpu.SemaphoreType.DMA((width // block,)),
        ],
        compiler_params=pltpu.CompilerParams(vmem_limit_bytes=vmem * 1024 * 1024),
        cost_estimate=pl.CostEstimate(
            flops=3 * nrows * depth * width,
            bytes_accessed=4 * width * depth + 2 * width * nrows,
            transcendentals=0,
        ),
    )(core.reshape(1), rows, columns)


def order_kernel(slots_ref, *refs):
    raws, out_ref = refs[:-1], refs[-1]
    nblocks, examples, _ = out_ref.shape
    for slot in range(nblocks):
        rows = pl.ds(slots_ref[slot], examples, stride=nblocks)
        for i, raw_ref in enumerate(raws):
            width = raw_ref.shape[1]
            out_ref[slot, :, i * width:(i + 1) * width] = raw_ref[rows, :].astype(out_ref.dtype)


def in_slot_order(raws, slots):
    nblocks = slots.shape[0]
    rows, width = raws[0].shape
    return pl.pallas_call(
        order_kernel,
        in_specs=[pl.BlockSpec(memory_space=pltpu.SMEM)] + [pl.BlockSpec(memory_space=pltpu.VMEM)] * CHUNKS,
        out_specs=pl.BlockSpec(memory_space=pltpu.VMEM),
        out_shape=jax.ShapeDtypeStruct((nblocks, rows // nblocks, CHUNKS * width), jnp.bfloat16),
        compiler_params=pltpu.CompilerParams(vmem_limit_bytes=4 * 1024 * 1024),
        cost_estimate=pl.CostEstimate(flops=rows * width, bytes_accessed=12 * rows * width, transcendentals=0),
    )(slots, *raws)


def finish_kernel(got_ref, allowed_ref, out_ref):
    n, owned, quad, examples, half = got_ref.shape
    parts = half // LANES
    per_row = owned * CORES * parts
    for device in range(n):
        for core in range(CORES):
            sources = [(device & ~3) | (y << 1) | core for y in range(quad // CORES)]
            for slot in range(owned):
                scores = sum(got_ref[s, slot, s ^ device].astype(jnp.float32) for s in sources)
                scores = scores * allowed_ref[slot:slot + 1, core * half:(core + 1) * half]
                for i in range(parts):
                    first = device * examples * per_row + (slot * CORES + core) * parts + i
                    out_ref[pl.ds(first, examples, stride=per_row), :] = scores[:, i * LANES:(i + 1) * LANES]


def finish(got, allowed):
    n, owned, _, examples, half = got.shape
    flat = pl.pallas_call(
        finish_kernel,
        out_shape=jax.ShapeDtypeStruct((n * examples * owned * CORES * half // LANES, LANES), jnp.float32),
        compiler_params=pltpu.CompilerParams(vmem_limit_bytes=4 * 1024 * 1024),
        cost_estimate=pl.CostEstimate(flops=got.size, bytes_accessed=4 * got.size, transcendentals=0),
    )(got, allowed)
    return flat.reshape(n * examples, owned, CORES * half)


def shards(queries, precond, train, query_cluster, cand_blocks, cand_count, slot_block):
    n = lax.axis_size("rows")
    chips = n // CORES
    bits = chips.bit_length() - 1
    ybit, zbit = 1, 1 + bits // 2
    rest = [bit for bit in range(1, 1 + bits) if bit not in (ybit, zbit)]
    me = lax.axis_index("rows")
    core = me & 1

    examples, nblocks, width = train.shape
    nq = queries.shape[0]

    def swap(value, bit):
        return lax.ppermute(value, "rows", [(r, r ^ (1 << bit)) for r in range(n)])

    def side(bit):
        return (me >> bit) & 1

    def pack(value):
        return (value * UNIT).astype(jnp.float16)

    def unpack(value):
        return value.astype(jnp.float32) * (1.0 / UNIT)

    def part(value, index, axis):
        size = value.shape[axis] // 2
        return lax.dynamic_slice_in_dim(value, index * size, size, axis)

    def give(value, bit, axis):
        return pack(part(value, 1 - side(bit), axis))

    def keep(value, got, bit, axis):
        return part(value, side(bit), axis) + unpack(got)

    def join(own, got, bit):
        size = own.shape[1]
        full = jnp.zeros((own.shape[0], 2 * size) + own.shape[2:], own.dtype)
        full = lax.dynamic_update_slice_in_dim(full, own, side(bit) * size, 1)
        return lax.dynamic_update_slice_in_dim(full, got, (1 - side(bit)) * size, 1)

    def after(value, first):
        return lax.optimization_barrier((value, first))[0]

    def paths(value, other):
        value = value + unpack(other)
        rows = value.shape[0] // PATHS
        return [value[i * rows:(i + 1) * rows] for i in range(PATHS)]

    levels = ((ybit, 1), (zbit, 0)), ((zbit, 0), (ybit, 1))

    def messages(values, step):
        return [give(value, *level[step]) for value, level in zip(values, levels)]

    def exchange(values, sent, step):
        got = [swap(message, level[step][0]) for message, level in zip(sent, levels)]
        return [keep(value, message, *level[step]) for value, message, level in zip(values, got, levels)]

    def halve(values):
        value = jnp.stack(values)
        for bit in rest[:-1]:
            value = keep(value, swap(give(value, bit, 1), bit), bit, 1)
        return value

    def gather(value):
        for bit in reversed([zbit] + rest[:-1]):
            value = join(value, swap(value, bit), bit)
        return value.reshape(-1, value.shape[-1])

    rows = train.reshape(examples * nblocks, width)
    near = part(rows, side(ybit), 1)
    far = part(rows, 1 - side(ybit), 1)
    far = [part(far, i, 0) for i in range(2)]

    early = swap(far[0], ybit)
    queries = after(queries, far[0])
    sent = [pack(value) for value in product(1 - core, queries, precond, OTHER_VMEM)]
    got = [swap(value, 0) for value in sent]
    mine = product(core, after(queries, sent[0]), precond, MINE_VMEM)
    one = paths(mine[0], got[0])
    sent = messages(one, 0)
    two = paths(mine[1], after(got[1], sent))
    one = exchange(one, sent, 0)
    sent = messages(one, 1)
    two = exchange(two, after(messages(two, 0), sent), 0)
    one = halve(exchange(one, sent, 1))
    sent = pack(one)
    far[1], near, early = after((far[1], near, early), sent)
    got_one = swap(sent, rest[-1])
    two = halve(exchange(two, messages(two, 1), 1))
    late = swap(far[1], ybit)
    moved = [near, swap(near, 0), early, late, swap(early, 0)]
    sent = pack(two)
    one = (after(one, sent) + unpack(got_one)).astype(jnp.bfloat16)
    got_two = swap(sent, rest[-1])
    one, late = after((one, late), sent)
    both = jnp.concatenate(moved + [swap(late, 0)], axis=0)
    one = gather(one)
    two, both = lax.optimization_barrier(((two + unpack(got_two)).astype(jnp.bfloat16), both))
    two = gather(two)

    raws = [
        lax.dot_general(both, value, (((1,), (1,)), ((), ())), preferred_element_type=jnp.float32)
        for value in (one, two)
    ]
    owned = nblocks // n
    ordered = in_slot_order(raws, slot_block).reshape(n, owned, 2 * CORES * examples, nq // CORES)
    got = lax.all_to_all(ordered, "rows", split_axis=0, concat_axis=0, tiled=True)

    allowed = listed_mask(query_cluster, cand_blocks, cand_count, nblocks)
    slots = lax.dynamic_slice_in_dim(slot_block, me * owned, owned)
    own_allowed = jnp.take(allowed, slots, axis=0, mode="clip")
    return finish(got.reshape(n, owned, 2 * CORES, examples, nq // CORES), own_allowed)


def solution(mesh):
    placed = (
        P("groups", "rows"),
        P("rows", None),
        P("rows", "groups", None),
        P("groups"),
        P("groups", None),
        P("groups"),
        P("groups"),
    )
    return jax.shard_map(
        shards,
        mesh=mesh,
        in_specs=placed,
        out_specs=P(None, ("groups", "rows"), None),
        check_vma=False,
    )
```

```python
import jax
import jax.numpy as jnp
from jax import lax
from jax.experimental import pallas as pl
from jax.experimental.pallas import tpu as pltpu
from jax.sharding import PartitionSpec as P

CORES = 2
CHUNKS = 2
PATHS = 2
UNIT = 4.0
LANES = 128
OTHER_VMEM = 43
MINE_VMEM = 16


def listed_mask(query_cluster, cand_blocks, cand_count, nblocks):
    nclusters = cand_blocks.shape[0]
    valid = jnp.arange(cand_blocks.shape[1])[None, :] < cand_count[:, None]
    hits = (cand_blocks[:, :, None] == jnp.arange(nblocks)[None, None, :]) & valid[:, :, None]
    listed = jnp.any(hits, axis=1).astype(jnp.float32)
    onehot = (query_cluster[:, None] == jnp.arange(nclusters)[None, :]).astype(jnp.float32)
    return jnp.dot(listed.T, onehot.T, preferred_element_type=jnp.float32)


def split(value):
    high = value.astype(jnp.bfloat16)
    return high, (value - high.astype(jnp.float32)).astype(jnp.bfloat16)


def rows_of(core_ref, rows_ref):
    half = rows_ref.shape[0] // CORES
    high, low = split(rows_ref[pl.ds(pl.multiple_of(core_ref[0] * half, half), half), :])
    return jnp.concatenate([high, low, high], axis=1)


def multiply(left, high, low, outs, columns):
    right = jnp.concatenate([high, high, low], axis=0)
    result = jnp.dot(left, right, preferred_element_type=jnp.float32)
    part = result.shape[0] // len(outs)
    for chunk, out_ref in enumerate(outs):
        out_ref[:, columns] = result[chunk * part:(chunk + 1) * part]


def other_kernel(core_ref, rows_ref, columns_hbm, *refs):
    outs, (high_ref, low_ref, columns_ref, sems) = refs[:-4], refs[-4:]
    steps, _, block = columns_ref.shape

    def load(i):
        return pltpu.make_async_copy(
            columns_hbm.at[:, i * block:(i + 1) * block], columns_ref.at[i], sems.at[i]
        )

    for i in range(steps):
        load(i).start()
    left = rows_of(core_ref, rows_ref)
    for i in range(steps):
        load(i).wait()
        columns = slice(i * block, (i + 1) * block)
        high, low = split(columns_ref[i])
        high_ref[:, columns] = high
        low_ref[:, columns] = low
        multiply(left, high, low, outs, columns)


def mine_kernel(core_ref, rows_ref, high_ref, low_ref, *outs):
    left = rows_of(core_ref, rows_ref)
    width = high_ref.shape[1]
    block = min(512, width)
    for i in range(width // block):
        columns = slice(i * block, (i + 1) * block)
        multiply(left, high_ref[:, columns], low_ref[:, columns], outs, columns)


def product(core, rows, columns, kernel, vmem):
    first = kernel is other_kernel
    nrows, depth = rows.shape
    width = columns[0].shape[1]
    block = min(512, width)
    part = nrows // CORES // CHUNKS
    out = [jax.ShapeDtypeStruct((part, width), jnp.float32)] * CHUNKS
    if first:
        out = out + [jax.ShapeDtypeStruct((depth, width), jnp.bfloat16)] * 2
    vmem_spec = pl.BlockSpec(memory_space=pltpu.VMEM)
    return pl.pallas_call(
        kernel,
        in_specs=[pl.BlockSpec(memory_space=pltpu.SMEM), vmem_spec]
        + [pl.BlockSpec(memory_space=pltpu.HBM) if first else vmem_spec] * len(columns),
        out_specs=[vmem_spec] * len(out),
        out_shape=out,
        scratch_shapes=[
            pltpu.VMEM((width // block, depth, block), jnp.float32),
            pltpu.SemaphoreType.DMA((width // block,)),
        ] if first else [],
        compiler_params=pltpu.CompilerParams(vmem_limit_bytes=vmem * 1024 * 1024),
        cost_estimate=pl.CostEstimate(
            flops=3 * nrows * depth * width,
            bytes_accessed=4 * width * depth + 2 * width * nrows,
            transcendentals=0,
        ),
    )(core.reshape(1), rows, *columns)


def order_kernel(slots_ref, *refs):
    raws, out_ref = refs[:-1], refs[-1]
    nblocks = slots_ref.shape[0]
    groups = len(raws) // CHUNKS
    for slot in range(nblocks):
        for i, raw_ref in enumerate(raws):
            examples, width = raw_ref.shape[0] // nblocks, raw_ref.shape[1]
            chunk, group = divmod(i, groups)
            rows = pl.ds(slots_ref[slot], examples, stride=nblocks)
            out_ref[
                slot, group * examples:(group + 1) * examples, chunk * width:(chunk + 1) * width
            ] = raw_ref[rows, :].astype(out_ref.dtype)


def in_slot_order(raws, slots):
    nblocks = slots.shape[0]
    rows, width = raws[0].shape
    groups = len(raws) // CHUNKS
    return pl.pallas_call(
        order_kernel,
        in_specs=[pl.BlockSpec(memory_space=pltpu.SMEM)] + [pl.BlockSpec(memory_space=pltpu.VMEM)] * len(raws),
        out_specs=pl.BlockSpec(memory_space=pltpu.VMEM),
        out_shape=jax.ShapeDtypeStruct((nblocks, groups * rows // nblocks, CHUNKS * width), jnp.bfloat16),
        compiler_params=pltpu.CompilerParams(vmem_limit_bytes=4 * 1024 * 1024),
        cost_estimate=pl.CostEstimate(
            flops=rows * width, bytes_accessed=6 * len(raws) * rows * width, transcendentals=0
        ),
    )(slots, *raws)


def finish_kernel(got_ref, allowed_ref, out_ref):
    n, owned, quad, examples, half = got_ref.shape
    parts = half // LANES
    per_row = owned * CORES * parts
    for device in range(n):
        for core in range(CORES):
            sources = [(device & ~3) | (y << 1) | core for y in range(quad // CORES)]
            for slot in range(owned):
                scores = sum(got_ref[s, slot, s ^ device].astype(jnp.float32) for s in sources)
                scores = scores * allowed_ref[slot:slot + 1, core * half:(core + 1) * half]
                for i in range(parts):
                    first = device * examples * per_row + (slot * CORES + core) * parts + i
                    out_ref[pl.ds(first, examples, stride=per_row), :] = scores[:, i * LANES:(i + 1) * LANES]


def finish(got, allowed):
    n, owned, _, examples, half = got.shape
    flat = pl.pallas_call(
        finish_kernel,
        out_shape=jax.ShapeDtypeStruct((n * examples * owned * CORES * half // LANES, LANES), jnp.float32),
        compiler_params=pltpu.CompilerParams(vmem_limit_bytes=4 * 1024 * 1024),
        cost_estimate=pl.CostEstimate(flops=got.size, bytes_accessed=4 * got.size, transcendentals=0),
    )(got, allowed)
    return flat.reshape(n * examples, owned, CORES * half)


def shards(queries, precond, train, query_cluster, cand_blocks, cand_count, slot_block):
    n = lax.axis_size("rows")
    chips = n // CORES
    bits = chips.bit_length() - 1
    ybit, zbit = 1, 1 + bits // 2
    rest = [bit for bit in range(1, 1 + bits) if bit not in (ybit, zbit)]
    me = lax.axis_index("rows")
    core = me & 1

    examples, nblocks, width = train.shape
    nq = queries.shape[0]

    def swap(value, bit):
        return lax.ppermute(value, "rows", [(r, r ^ (1 << bit)) for r in range(n)])

    def side(bit):
        return (me >> bit) & 1

    def pack(value):
        return (value * UNIT).astype(jnp.float16)

    def unpack(value):
        return value.astype(jnp.float32) * (1.0 / UNIT)

    def part(value, index, axis):
        size = value.shape[axis] // 2
        return lax.dynamic_slice_in_dim(value, index * size, size, axis)

    def give(value, bit, axis):
        return pack(part(value, 1 - side(bit), axis))

    def keep(value, got, bit, axis):
        return part(value, side(bit), axis) + unpack(got)

    def join(own, got, bit):
        size = own.shape[1]
        full = jnp.zeros((own.shape[0], 2 * size) + own.shape[2:], own.dtype)
        full = lax.dynamic_update_slice_in_dim(full, own, side(bit) * size, 1)
        return lax.dynamic_update_slice_in_dim(full, got, (1 - side(bit)) * size, 1)

    def after(value, first):
        return lax.optimization_barrier((value, first))[0]

    def paths(value, other):
        value = value + unpack(other)
        rows = value.shape[0] // PATHS
        return [value[i * rows:(i + 1) * rows] for i in range(PATHS)]

    levels = ((ybit, 1), (zbit, 0)), ((zbit, 0), (ybit, 1))

    def messages(values, step):
        return [give(value, *level[step]) for value, level in zip(values, levels)]

    def exchange(values, sent, step):
        got = [swap(message, level[step][0]) for message, level in zip(sent, levels)]
        return [keep(value, message, *level[step]) for value, message, level in zip(values, got, levels)]

    def halve(values):
        value = jnp.stack(values)
        for bit in rest[:-1]:
            value = keep(value, swap(give(value, bit, 1), bit), bit, 1)
        return value

    def gather(value):
        for bit in reversed([zbit] + rest[:-1]):
            value = join(value, swap(value, bit), bit)
        return value.reshape(-1, value.shape[-1])

    rows = train.reshape(examples * nblocks, width)
    far = part(rows, 1 - side(ybit), 1)
    far = [part(far, i, 0) for i in range(2)]
    early = swap(far[0], ybit)
    queries = after(queries, far[0])

    *full, high, low = product(1 - core, queries, [precond], other_kernel, OTHER_VMEM)
    sent = [pack(value) for value in full]
    got = [swap(value, 0) for value in sent]
    rows = after(rows, sent)
    near = part(rows, side(ybit), 1)
    sibling = swap(near, 0)
    mine = product(after(core, sent), queries, [high, low], mine_kernel, MINE_VMEM)
    one = paths(mine[0], got[0])
    sent = messages(one, 0)
    two = paths(mine[1], after(got[1], sent))
    one = exchange(one, sent, 0)
    sent = messages(one, 1)
    two = exchange(two, after(messages(two, 0), sent), 0)
    one = halve(exchange(one, sent, 1))
    got_one = swap(pack(one), rest[-1])
    two = halve(exchange(two, messages(two, 1), 1))
    sent = pack(two)
    one = (after(one, sent) + unpack(got_one)).astype(jnp.bfloat16)
    got_two = swap(sent, rest[-1])
    late = swap(after(far[1], one), ybit)
    one = gather(one)
    far = jnp.concatenate([early, late], axis=0)
    groups = [jnp.concatenate([near, sibling], axis=0), jnp.concatenate([far, swap(far, 0)], axis=0)]
    two = gather((two + unpack(got_two)).astype(jnp.bfloat16))

    raws = [
        lax.dot_general(group, value, (((1,), (1,)), ((), ())), preferred_element_type=jnp.float32)
        for value in (one, two)
        for group in groups
    ]
    owned = nblocks // n
    ordered = in_slot_order(raws, slot_block).reshape(n, owned, 2 * CORES * examples, nq // CORES)
    got = lax.all_to_all(ordered, "rows", split_axis=0, concat_axis=0, tiled=True)

    allowed = listed_mask(query_cluster, cand_blocks, cand_count, nblocks)
    slots = lax.dynamic_slice_in_dim(slot_block, me * owned, owned)
    own_allowed = jnp.take(allowed, slots, axis=0, mode="clip")
    return finish(got.reshape(n, owned, 2 * CORES, examples, nq // CORES), own_allowed)


def solution(mesh):
    placed = (
        P("groups", "rows"),
        P("rows", None),
        P("rows", "groups", None),
        P("groups"),
        P("groups", None),
        P("groups"),
        P("groups"),
    )
    return jax.shard_map(
        shards,
        mesh=mesh,
        in_specs=placed,
        out_specs=P(None, ("groups", "rows"), None),
        check_vma=False,
    )
```

```python
import jax
import jax.numpy as jnp
from jax import lax
from jax.experimental import pallas as pl
from jax.experimental.pallas import tpu as pltpu
from jax.sharding import PartitionSpec as P

CORES = 2
CHUNKS = 2
PATHS = 2
UNIT = 4.0
LANES = 128
OTHER_VMEM = 43
MINE_VMEM = 16


def listed_mask(query_cluster, cand_blocks, cand_count, nblocks):
    nclusters = cand_blocks.shape[0]
    valid = jnp.arange(cand_blocks.shape[1])[None, :] < cand_count[:, None]
    hits = (cand_blocks[:, :, None] == jnp.arange(nblocks)[None, None, :]) & valid[:, :, None]
    listed = jnp.any(hits, axis=1).astype(jnp.float32)
    onehot = (query_cluster[:, None] == jnp.arange(nclusters)[None, :]).astype(jnp.float32)
    return jnp.dot(listed.T, onehot.T, preferred_element_type=jnp.float32)


def split(value):
    high = value.astype(jnp.bfloat16)
    return high, (value - high.astype(jnp.float32)).astype(jnp.bfloat16)


def rows_of(core_ref, rows_ref):
    half = rows_ref.shape[0] // CORES
    high, low = split(rows_ref[pl.ds(pl.multiple_of(core_ref[0] * half, half), half), :])
    return jnp.concatenate([high, low, high], axis=1)


def multiply(left, high, low, outs, columns):
    right = jnp.concatenate([high, high, low], axis=0)
    result = jnp.dot(left, right, preferred_element_type=jnp.float32)
    part = result.shape[0] // len(outs)
    for chunk, out_ref in enumerate(outs):
        out_ref[:, columns] = result[chunk * part:(chunk + 1) * part]


def other_kernel(core_ref, rows_ref, columns_hbm, *refs):
    outs, (high_ref, low_ref, columns_ref, sems) = refs[:-4], refs[-4:]
    steps, _, block = columns_ref.shape

    def load(i):
        return pltpu.make_async_copy(
            columns_hbm.at[:, i * block:(i + 1) * block], columns_ref.at[i], sems.at[i]
        )

    for i in range(steps):
        load(i).start()
    left = rows_of(core_ref, rows_ref)
    for i in range(steps):
        load(i).wait()
        columns = slice(i * block, (i + 1) * block)
        high, low = split(columns_ref[i])
        high_ref[:, columns] = high
        low_ref[:, columns] = low
        multiply(left, high, low, outs, columns)


def mine_kernel(core_ref, rows_ref, high_ref, low_ref, *outs):
    left = rows_of(core_ref, rows_ref)
    width = high_ref.shape[1]
    block = min(512, width)
    for i in range(width // block):
        columns = slice(i * block, (i + 1) * block)
        multiply(left, high_ref[:, columns], low_ref[:, columns], outs, columns)


def product(core, rows, columns, kernel, vmem):
    first = kernel is other_kernel
    nrows, depth = rows.shape
    width = columns[0].shape[1]
    block = min(512, width)
    part = nrows // CORES // CHUNKS
    out = [jax.ShapeDtypeStruct((part, width), jnp.float32)] * CHUNKS
    if first:
        out = out + [jax.ShapeDtypeStruct((depth, width), jnp.bfloat16)] * 2
    vmem_spec = pl.BlockSpec(memory_space=pltpu.VMEM)
    return pl.pallas_call(
        kernel,
        in_specs=[pl.BlockSpec(memory_space=pltpu.SMEM), vmem_spec]
        + [pl.BlockSpec(memory_space=pltpu.HBM) if first else vmem_spec] * len(columns),
        out_specs=[vmem_spec] * len(out),
        out_shape=out,
        scratch_shapes=[
            pltpu.VMEM((width // block, depth, block), jnp.float32),
            pltpu.SemaphoreType.DMA((width // block,)),
        ] if first else [],
        compiler_params=pltpu.CompilerParams(vmem_limit_bytes=vmem * 1024 * 1024),
        cost_estimate=pl.CostEstimate(
            flops=3 * nrows * depth * width,
            bytes_accessed=4 * width * depth + 2 * width * nrows,
            transcendentals=0,
        ),
    )(core.reshape(1), rows, *columns)


def order_kernel(slots_ref, *refs):
    raws, out_ref = refs[:-1], refs[-1]
    nblocks = slots_ref.shape[0]
    groups = len(raws) // CHUNKS
    for slot in range(nblocks):
        for i, raw_ref in enumerate(raws):
            examples, width = raw_ref.shape[0] // nblocks, raw_ref.shape[1]
            chunk, group = divmod(i, groups)
            rows = pl.ds(slots_ref[slot], examples, stride=nblocks)
            out_ref[
                slot, group * examples:(group + 1) * examples, chunk * width:(chunk + 1) * width
            ] = raw_ref[rows, :].astype(out_ref.dtype)


def in_slot_order(raws, slots):
    nblocks = slots.shape[0]
    rows, width = raws[0].shape
    groups = len(raws) // CHUNKS
    return pl.pallas_call(
        order_kernel,
        in_specs=[pl.BlockSpec(memory_space=pltpu.SMEM)] + [pl.BlockSpec(memory_space=pltpu.VMEM)] * len(raws),
        out_specs=pl.BlockSpec(memory_space=pltpu.VMEM),
        out_shape=jax.ShapeDtypeStruct((nblocks, groups * rows // nblocks, CHUNKS * width), jnp.bfloat16),
        compiler_params=pltpu.CompilerParams(vmem_limit_bytes=4 * 1024 * 1024),
        cost_estimate=pl.CostEstimate(
            flops=rows * width, bytes_accessed=6 * len(raws) * rows * width, transcendentals=0
        ),
    )(slots, *raws)


def finish_kernel(got_ref, allowed_ref, out_ref):
    n, owned, quad, examples, half = got_ref.shape
    parts = half // LANES
    per_row = owned * CORES * parts
    for device in range(n):
        for core in range(CORES):
            sources = [(device & ~3) | (y << 1) | core for y in range(quad // CORES)]
            for slot in range(owned):
                scores = sum(got_ref[s, slot, s ^ device].astype(jnp.float32) for s in sources)
                scores = scores * allowed_ref[slot:slot + 1, core * half:(core + 1) * half]
                for i in range(parts):
                    first = device * examples * per_row + (slot * CORES + core) * parts + i
                    out_ref[pl.ds(first, examples, stride=per_row), :] = scores[:, i * LANES:(i + 1) * LANES]


def finish(got, allowed):
    n, owned, _, examples, half = got.shape
    flat = pl.pallas_call(
        finish_kernel,
        out_shape=jax.ShapeDtypeStruct((n * examples * owned * CORES * half // LANES, LANES), jnp.float32),
        compiler_params=pltpu.CompilerParams(vmem_limit_bytes=4 * 1024 * 1024),
        cost_estimate=pl.CostEstimate(flops=got.size, bytes_accessed=4 * got.size, transcendentals=0),
    )(got, allowed)
    return flat.reshape(n * examples, owned, CORES * half)


def shards(queries, precond, train, query_cluster, cand_blocks, cand_count, slot_block):
    n = lax.axis_size("rows")
    chips = n // CORES
    bits = chips.bit_length() - 1
    ybit, zbit = 1, 1 + bits // 2
    rest = [bit for bit in range(1, 1 + bits) if bit not in (ybit, zbit)]
    me = lax.axis_index("rows")
    core = me & 1

    examples, nblocks, width = train.shape
    nq = queries.shape[0]

    def swap(value, bit):
        return lax.ppermute(value, "rows", [(r, r ^ (1 << bit)) for r in range(n)])

    rows = nq // CORES // CHUNKS // PATHS
    sizes = {(ybit, width // 2), (zbit, rows // 2)} | {(bit, rows >> (i + 2)) for i, bit in enumerate(rest[:-1])}
    offsets = {}
    first_half = {}
    for bit, size in sorted(sizes):
        side = (me >> bit) & 1
        offsets[bit, size] = (side * size, (1 - side) * size)
        first_half[bit] = side == 0
    owned = nblocks // n
    first_slot = me * owned
    scalars = (core, 1 - core, first_slot, offsets, first_half)
    scalars, queries, train = lax.optimization_barrier((scalars, queries, train))
    core, other_core, first_slot, offsets, first_half = scalars

    def pack(value):
        return (value * UNIT).astype(jnp.float16)

    def unpack(value):
        return value.astype(jnp.float32) * (1.0 / UNIT)

    def part(value, bit, axis, other=0):
        shape = list(value.shape)
        shape[axis] //= 2
        starts = [0] * value.ndim
        starts[axis] = offsets[bit, shape[axis]][other]
        return lax.dynamic_slice(value, starts, shape, allow_negative_indices=False)

    def give(value, bit, axis):
        return pack(part(value, bit, axis, 1))

    def keep(value, got, bit, axis):
        return part(value, bit, axis) + unpack(got)

    def join(own, got, bit):
        mine_first = jnp.concatenate([own, got], axis=1)
        return jnp.where(first_half[bit], mine_first, jnp.concatenate([got, own], axis=1))

    def after(value, first):
        return lax.optimization_barrier((value, first))[0]

    def paths(value, other):
        value = value + unpack(other)
        return [value[i * rows:(i + 1) * rows] for i in range(PATHS)]

    levels = ((ybit, 1), (zbit, 0)), ((zbit, 0), (ybit, 1))

    def messages(values, step):
        return [give(value, *level[step]) for value, level in zip(values, levels)]

    def exchange(values, sent, step):
        got = [swap(message, level[step][0]) for message, level in zip(sent, levels)]
        return [keep(value, message, *level[step]) for value, message, level in zip(values, got, levels)]

    def halve(values):
        value = jnp.stack(values)
        for bit in rest[:-1]:
            value = keep(value, swap(give(value, bit, 1), bit), bit, 1)
        return value

    def gather(value, first=None):
        for bit in reversed([zbit] + rest[:-1]):
            got = swap(value, bit)
            if first is not None and bit == zbit:
                got = after(got, first)
            value = join(value, got, bit)
        return value.reshape(-1, value.shape[-1])

    def scores(group, value):
        return lax.dot_general(group, value, (((1,), (1,)), ((), ())), preferred_element_type=jnp.float32)

    blocks = train.reshape(examples * nblocks, width)
    middle = examples // 2 * nblocks

    def features(blocks, first, count, other):
        start = offsets[ybit, width // 2][other]
        return lax.dynamic_slice(blocks, (first, start), (count, width // 2), allow_negative_indices=False)

    early = features(blocks, 0, middle, 1)
    queries, blocks = after((queries, blocks), early)
    early = swap(early, ybit)

    *full, high, low = product(other_core, queries, [precond], other_kernel, OTHER_VMEM)
    sent = [pack(value) for value in full]
    got = [swap(value, 0) for value in sent]
    blocks = after(blocks, sent)
    near = features(blocks, 0, 2 * middle, 0)
    late = features(blocks, middle, middle, 1)
    sibling = swap(near, 0)
    mine = product(after(core, sent), queries, [high, low], mine_kernel, MINE_VMEM)
    one = paths(mine[0], got[0])
    sent = messages(one, 0)
    two = paths(mine[1], after(got[1], sent))
    one = exchange(one, sent, 0)
    sent = messages(one, 1)
    two = exchange(two, after(messages(two, 0), sent), 0)
    one = halve(exchange(one, sent, 1))
    got_one = swap(pack(one), rest[-1])
    two = halve(exchange(two, messages(two, 1), 1))
    sent = pack(two)
    one = (after(one, sent) + unpack(got_one)).astype(jnp.bfloat16)
    got_two = swap(sent, rest[-1])
    late = swap(after(late, one), ybit)
    one = gather(one)
    far = jnp.concatenate([early, late], axis=0)
    groups = [jnp.concatenate([near, sibling], axis=0), jnp.concatenate([far, swap(far, 0)], axis=0)]
    raws = [scores(group, one) for group in groups]
    two = gather((two + unpack(got_two)).astype(jnp.bfloat16), raws)
    raws = raws + [scores(group, two) for group in groups]

    ordered = in_slot_order(raws, slot_block).reshape(n, owned, 2 * CORES * examples, nq // CORES)
    got = lax.all_to_all(ordered, "rows", split_axis=0, concat_axis=0, tiled=True)

    lists = (query_cluster, cand_blocks, cand_count, slot_block, first_slot)
    query_cluster, cand_blocks, cand_count, slot_block, first_slot = after(lists, ordered)
    allowed = listed_mask(query_cluster, cand_blocks, cand_count, nblocks)
    slots = lax.dynamic_slice(slot_block, (first_slot,), (owned,), allow_negative_indices=False)
    own_allowed = jnp.take(allowed, slots, axis=0, mode="clip")
    return finish(got.reshape(n, owned, 2 * CORES, examples, nq // CORES), own_allowed)


def solution(mesh):
    placed = (
        P("groups", "rows"),
        P("rows", None),
        P("rows", "groups", None),
        P("groups"),
        P("groups", None),
        P("groups"),
        P("groups"),
    )
    return jax.shard_map(
        shards,
        mesh=mesh,
        in_specs=placed,
        out_specs=P(None, ("groups", "rows"), None),
        check_vma=False,
    )
```

```python
import jax
import jax.numpy as jnp
from jax import lax
from jax.experimental import pallas as pl
from jax.experimental.pallas import tpu as pltpu
from jax.sharding import PartitionSpec as P

CORES = 2
CHUNKS = 2
PATHS = 2
UNIT = 4.0
LANES = 128
OTHER_VMEM = 44
MINE_VMEM = 16


def listed_mask(query_cluster, cand_blocks, cand_count, nblocks):
    nclusters = cand_blocks.shape[0]
    valid = jnp.arange(cand_blocks.shape[1])[None, :] < cand_count[:, None]
    hits = (cand_blocks[:, :, None] == jnp.arange(nblocks)[None, None, :]) & valid[:, :, None]
    listed = jnp.any(hits, axis=1).astype(jnp.float32)
    onehot = (query_cluster[:, None] == jnp.arange(nclusters)[None, :]).astype(jnp.float32)
    return jnp.dot(listed.T, onehot.T, preferred_element_type=jnp.float32)


def split(value):
    high = value.astype(jnp.bfloat16)
    return high, (value - high.astype(jnp.float32)).astype(jnp.bfloat16)


def rows_of(core_ref, rows_ref):
    half = rows_ref.shape[0] // CORES
    high, low = split(rows_ref[pl.ds(pl.multiple_of(core_ref[0] * half, half), half), :])
    return jnp.concatenate([high, low, high], axis=1)


def multiply(left, high, low, outs, columns):
    right = jnp.concatenate([high, high, low], axis=0)
    result = jnp.dot(left, right, preferred_element_type=jnp.float32)
    part = result.shape[0] // len(outs)
    for chunk, out_ref in enumerate(outs):
        out_ref[:, columns] = result[chunk * part:(chunk + 1) * part]


def other_kernel(core_ref, rows_hbm, columns_hbm, *refs):
    outs, (high_ref, low_ref, rows_ref, columns_ref, sems) = refs[:-5], refs[-5:]
    steps, _, block = columns_ref.shape

    def load(i):
        return pltpu.make_async_copy(
            columns_hbm.at[:, i * block:(i + 1) * block], columns_ref.at[i], sems.at[i]
        )

    load_rows = pltpu.make_async_copy(rows_hbm, rows_ref, sems.at[steps])
    load_rows.start()
    for i in range(steps):
        load(i).start()
    load_rows.wait()
    left = rows_of(core_ref, rows_ref)
    for i in range(steps):
        load(i).wait()
        columns = slice(i * block, (i + 1) * block)
        high, low = split(columns_ref[i])
        high_ref[:, columns] = high
        low_ref[:, columns] = low
        multiply(left, high, low, outs, columns)


def mine_kernel(core_ref, rows_ref, high_ref, low_ref, *outs):
    left = rows_of(core_ref, rows_ref)
    width = high_ref.shape[1]
    block = min(512, width)
    for i in range(width // block):
        columns = slice(i * block, (i + 1) * block)
        multiply(left, high_ref[:, columns], low_ref[:, columns], outs, columns)


def product(core, rows, columns, kernel, vmem):
    nrows, depth = rows.shape
    width = columns[0].shape[1]
    block = min(512, width)
    part = nrows // CORES // CHUNKS
    out = [jax.ShapeDtypeStruct((part, width), jnp.float32)] * CHUNKS
    in_vmem = pl.BlockSpec(memory_space=pltpu.VMEM)
    operand, scratch = in_vmem, []
    if kernel is other_kernel:
        out = out + [jax.ShapeDtypeStruct((depth, width), jnp.bfloat16)] * 2
        operand = pl.BlockSpec(memory_space=pltpu.HBM)
        scratch = [
            pltpu.VMEM((nrows, depth), jnp.float32),
            pltpu.VMEM((width // block, depth, block), jnp.float32),
            pltpu.SemaphoreType.DMA((1 + width // block,)),
        ]
    return pl.pallas_call(
        kernel,
        in_specs=[pl.BlockSpec(memory_space=pltpu.SMEM)] + [operand] * (1 + len(columns)),
        out_specs=[in_vmem] * len(out),
        out_shape=out,
        scratch_shapes=scratch,
        compiler_params=pltpu.CompilerParams(vmem_limit_bytes=vmem * 1024 * 1024),
        cost_estimate=pl.CostEstimate(
            flops=3 * nrows * depth * width,
            bytes_accessed=4 * width * depth + 2 * width * nrows,
            transcendentals=0,
        ),
    )(core.reshape(1), rows, *columns)


def order_kernel(slots_ref, *refs):
    raws, out_ref = refs[:-1], refs[-1]
    nblocks = slots_ref.shape[0]
    groups = len(raws) // CHUNKS
    for slot in range(nblocks):
        for i, raw_ref in enumerate(raws):
            examples, width = raw_ref.shape[0] // nblocks, raw_ref.shape[1]
            chunk, group = divmod(i, groups)
            rows = pl.ds(slots_ref[slot], examples, stride=nblocks)
            out_ref[
                slot, group * examples:(group + 1) * examples, chunk * width:(chunk + 1) * width
            ] = raw_ref[rows, :].astype(out_ref.dtype)


def in_slot_order(raws, slots):
    nblocks = slots.shape[0]
    rows, width = raws[0].shape
    groups = len(raws) // CHUNKS
    return pl.pallas_call(
        order_kernel,
        in_specs=[pl.BlockSpec(memory_space=pltpu.SMEM)] + [pl.BlockSpec(memory_space=pltpu.VMEM)] * len(raws),
        out_specs=pl.BlockSpec(memory_space=pltpu.VMEM),
        out_shape=jax.ShapeDtypeStruct((nblocks, groups * rows // nblocks, CHUNKS * width), jnp.bfloat16),
        compiler_params=pltpu.CompilerParams(vmem_limit_bytes=4 * 1024 * 1024),
        cost_estimate=pl.CostEstimate(
            flops=rows * width, bytes_accessed=6 * len(raws) * rows * width, transcendentals=0
        ),
    )(slots, *raws)


def finish_kernel(got_ref, allowed_ref, out_ref):
    n, owned, quad, examples, half = got_ref.shape
    parts = half // LANES
    per_row = owned * CORES * parts
    for device in range(n):
        for core in range(CORES):
            sources = [(device & ~3) | (y << 1) | core for y in range(quad // CORES)]
            for slot in range(owned):
                scores = sum(got_ref[s, slot, s ^ device].astype(jnp.float32) for s in sources)
                scores = scores * allowed_ref[slot:slot + 1, core * half:(core + 1) * half]
                for i in range(parts):
                    first = device * examples * per_row + (slot * CORES + core) * parts + i
                    out_ref[pl.ds(first, examples, stride=per_row), :] = scores[:, i * LANES:(i + 1) * LANES]


def finish(got, allowed):
    n, owned, _, examples, half = got.shape
    flat = pl.pallas_call(
        finish_kernel,
        out_shape=jax.ShapeDtypeStruct((n * examples * owned * CORES * half // LANES, LANES), jnp.float32),
        compiler_params=pltpu.CompilerParams(vmem_limit_bytes=4 * 1024 * 1024),
        cost_estimate=pl.CostEstimate(flops=got.size, bytes_accessed=4 * got.size, transcendentals=0),
    )(got, allowed)
    return flat.reshape(n * examples, owned, CORES * half)


def shards(queries, precond, train, query_cluster, cand_blocks, cand_count, slot_block):
    n = lax.axis_size("rows")
    chips = n // CORES
    bits = chips.bit_length() - 1
    ybit, zbit = 1, 1 + bits // 2
    rest = [bit for bit in range(1, 1 + bits) if bit not in (ybit, zbit)]
    me = lax.axis_index("rows")
    core = me & 1

    examples, nblocks, width = train.shape
    nq = queries.shape[0]

    def swap(value, bit):
        return lax.ppermute(value, "rows", [(r, r ^ (1 << bit)) for r in range(n)])

    rows = nq // CORES // CHUNKS // PATHS
    sizes = {(ybit, width // 2), (zbit, rows // 2)} | {(bit, rows >> (i + 2)) for i, bit in enumerate(rest[:-1])}
    offsets = {}
    first_half = {}
    for bit, size in sorted(sizes):
        side = (me >> bit) & 1
        offsets[bit, size] = (side * size, (1 - side) * size)
        first_half[bit] = side == 0
    owned = nblocks // n
    first_slot = me * owned
    scalars = (core, 1 - core, first_slot, offsets, first_half)
    scalars, queries, train = lax.optimization_barrier((scalars, queries, train))
    core, other_core, first_slot, offsets, first_half = scalars

    def pack(value):
        return (value * UNIT).astype(jnp.float16)

    def unpack(value):
        return value.astype(jnp.float32) * (1.0 / UNIT)

    def part(value, bit, axis, other=0):
        shape = list(value.shape)
        shape[axis] //= 2
        starts = [0] * value.ndim
        starts[axis] = offsets[bit, shape[axis]][other]
        return lax.dynamic_slice(value, starts, shape, allow_negative_indices=False)

    def give(value, bit, axis):
        return pack(part(value, bit, axis, 1))

    def keep(value, got, bit, axis):
        return part(value, bit, axis) + unpack(got)

    def join(own, got, bit):
        mine_first = jnp.concatenate([own, got], axis=1)
        return jnp.where(first_half[bit], mine_first, jnp.concatenate([got, own], axis=1))

    def after(value, first):
        return lax.optimization_barrier((value, first))[0]

    def paths(value, other):
        value = value + unpack(other)
        return [value[i * rows:(i + 1) * rows] for i in range(PATHS)]

    levels = ((ybit, 1), (zbit, 0)), ((zbit, 0), (ybit, 1))

    def messages(values, step):
        return [give(value, *level[step]) for value, level in zip(values, levels)]

    def exchange(values, sent, step):
        got = [swap(message, level[step][0]) for message, level in zip(sent, levels)]
        return [keep(value, message, *level[step]) for value, message, level in zip(values, got, levels)]

    def halve(values):
        value = jnp.stack(values)
        for bit in rest[:-1]:
            value = keep(value, swap(give(value, bit, 1), bit), bit, 1)
        return value

    def gather(value, first=None):
        for bit in reversed([zbit] + rest[:-1]):
            got = swap(value, bit)
            if first is not None and bit == zbit:
                got = after(got, first)
            value = join(value, got, bit)
        return value.reshape(-1, value.shape[-1])

    def scores(group, value):
        return lax.dot_general(group, value, (((1,), (1,)), ((), ())), preferred_element_type=jnp.float32)

    blocks = train.reshape(examples * nblocks, width)
    middle = examples // 2 * nblocks

    def features(blocks, first, count, other):
        start = offsets[ybit, width // 2][other]
        return lax.dynamic_slice(blocks, (first, start), (count, width // 2), allow_negative_indices=False)

    *full, high, low = product(other_core, queries, [precond], other_kernel, OTHER_VMEM)
    sent = [pack(value) for value in full]
    got = [swap(value, 0) for value in sent]
    blocks = after(blocks, sent)
    near = features(blocks, 0, 2 * middle, 0)
    far = [features(blocks, i * middle, middle, 1) for i in range(2)]
    sibling = swap(near, 0)
    mine = product(after(core, sent), queries, [high, low], mine_kernel, MINE_VMEM)
    one = paths(mine[0], got[0])
    sent = messages(one, 0)
    two = paths(mine[1], after(got[1], sent))
    one = exchange(one, sent, 0)
    sent = messages(one, 1)
    two = exchange(two, after(messages(two, 0), (sent, sibling)), 0)
    one = halve(exchange(one, sent, 1))
    got_one = swap(pack(one), rest[-1])
    two = exchange(two, messages(two, 1), 1)
    far[0] = swap(after(far[0], two[0]), ybit)
    two = halve(two)
    sent = pack(two)
    one = (after(one, sent) + unpack(got_one)).astype(jnp.bfloat16)
    got_two = swap(sent, rest[-1])
    far[1] = swap(after(far[1], one), ybit)
    one = gather(one)
    groups = [
        jnp.concatenate([near, sibling], axis=0),
        jnp.concatenate(far + [swap(value, 0) for value in far], axis=0),
    ]
    raws = [scores(group, one) for group in groups]
    two = gather((two + unpack(got_two)).astype(jnp.bfloat16), raws)
    raws = raws + [scores(group, two) for group in groups]

    ordered = in_slot_order(raws, slot_block).reshape(n, owned, 2 * CORES * examples, nq // CORES)
    got = lax.all_to_all(ordered, "rows", split_axis=0, concat_axis=0, tiled=True)

    lists = (query_cluster, cand_blocks, cand_count, slot_block, first_slot)
    query_cluster, cand_blocks, cand_count, slot_block, first_slot = after(lists, ordered)
    allowed = listed_mask(query_cluster, cand_blocks, cand_count, nblocks)
    slots = lax.dynamic_slice(slot_block, (first_slot,), (owned,), allow_negative_indices=False)
    own_allowed = jnp.take(allowed, slots, axis=0, mode="clip")
    return finish(got.reshape(n, owned, 2 * CORES, examples, nq // CORES), own_allowed)


def solution(mesh):
    placed = (
        P("groups", "rows"),
        P("rows", None),
        P("rows", "groups", None),
        P("groups"),
        P("groups", None),
        P("groups"),
        P("groups"),
    )
    return jax.shard_map(
        shards,
        mesh=mesh,
        in_specs=placed,
        out_specs=P(None, ("groups", "rows"), None),
        check_vma=False,
    )
```

```python
import jax
import jax.numpy as jnp
from jax import lax
from jax.experimental import pallas as pl
from jax.experimental.pallas import tpu as pltpu
from jax.sharding import PartitionSpec as P

CORES = 2
CHUNKS = 2
PATHS = 2
UNIT = 4.0
LANES = 128
OTHER_VMEM = 44
MINE_VMEM = 16


def listed_mask(query_cluster, cand_blocks, cand_count, nblocks):
    nclusters = cand_blocks.shape[0]
    valid = jnp.arange(cand_blocks.shape[1])[None, :] < cand_count[:, None]
    hits = (cand_blocks[:, :, None] == jnp.arange(nblocks)[None, None, :]) & valid[:, :, None]
    listed = jnp.any(hits, axis=1).astype(jnp.float32)
    onehot = (query_cluster[:, None] == jnp.arange(nclusters)[None, :]).astype(jnp.float32)
    return jnp.dot(listed.T, onehot.T, preferred_element_type=jnp.float32)


def split(value):
    high = value.astype(jnp.bfloat16)
    return high, (value - high.astype(jnp.float32)).astype(jnp.bfloat16)


def rows_of(core_ref, rows_ref):
    half = rows_ref.shape[0] // CORES
    high, low = split(rows_ref[pl.ds(pl.multiple_of(core_ref[0] * half, half), half), :])
    return jnp.concatenate([high, low, high], axis=1)


def multiply(left, high, low, outs, columns):
    right = jnp.concatenate([high, high, low], axis=0)
    result = jnp.dot(left, right, preferred_element_type=jnp.float32)
    part = result.shape[0] // len(outs)
    for chunk, out_ref in enumerate(outs):
        out_ref[:, columns] = result[chunk * part:(chunk + 1) * part]


def other_kernel(core_ref, rows_hbm, columns_hbm, *refs):
    outs, (high_ref, low_ref, rows_ref, columns_ref, sems) = refs[:-5], refs[-5:]
    steps, _, block = columns_ref.shape

    def load(i):
        return pltpu.make_async_copy(
            columns_hbm.at[:, i * block:(i + 1) * block], columns_ref.at[i], sems.at[i]
        )

    load_rows = pltpu.make_async_copy(rows_hbm, rows_ref, sems.at[steps])
    load_rows.start()
    for i in range(steps):
        load(i).start()
    load_rows.wait()
    left = rows_of(core_ref, rows_ref)
    for i in range(steps):
        load(i).wait()
        columns = slice(i * block, (i + 1) * block)
        high, low = split(columns_ref[i])
        high_ref[:, columns] = high
        low_ref[:, columns] = low
        multiply(left, high, low, outs, columns)


def mine_kernel(core_ref, rows_ref, high_ref, low_ref, *outs):
    left = rows_of(core_ref, rows_ref)
    width = high_ref.shape[1]
    block = min(512, width)
    for i in range(width // block):
        columns = slice(i * block, (i + 1) * block)
        multiply(left, high_ref[:, columns], low_ref[:, columns], outs, columns)


def product(core, rows, columns, kernel, vmem):
    nrows, depth = rows.shape
    width = columns[0].shape[1]
    block = min(512, width)
    part = nrows // CORES // CHUNKS
    out = [jax.ShapeDtypeStruct((part, width), jnp.float32)] * CHUNKS
    in_vmem = pl.BlockSpec(memory_space=pltpu.VMEM)
    operand, scratch = in_vmem, []
    if kernel is other_kernel:
        out = out + [jax.ShapeDtypeStruct((depth, width), jnp.bfloat16)] * 2
        operand = pl.BlockSpec(memory_space=pltpu.HBM)
        scratch = [
            pltpu.VMEM((nrows, depth), jnp.float32),
            pltpu.VMEM((width // block, depth, block), jnp.float32),
            pltpu.SemaphoreType.DMA((1 + width // block,)),
        ]
    return pl.pallas_call(
        kernel,
        in_specs=[pl.BlockSpec(memory_space=pltpu.SMEM)] + [operand] * (1 + len(columns)),
        out_specs=[in_vmem] * len(out),
        out_shape=out,
        scratch_shapes=scratch,
        compiler_params=pltpu.CompilerParams(vmem_limit_bytes=vmem * 1024 * 1024),
        cost_estimate=pl.CostEstimate(
            flops=3 * nrows * depth * width,
            bytes_accessed=4 * width * depth + 2 * width * nrows,
            transcendentals=0,
        ),
    )(core.reshape(1), rows, *columns)


def order_kernel(slots_ref, *refs):
    raws, out_ref = refs[:-1], refs[-1]
    nblocks = slots_ref.shape[0]
    groups = len(raws) // CHUNKS
    for slot in range(nblocks):
        for i, raw_ref in enumerate(raws):
            examples, width = raw_ref.shape[0] // nblocks, raw_ref.shape[1]
            chunk, group = divmod(i, groups)
            rows = pl.ds(slots_ref[slot], examples, stride=nblocks)
            out_ref[
                slot, group * examples:(group + 1) * examples, chunk * width:(chunk + 1) * width
            ] = raw_ref[rows, :].astype(out_ref.dtype)


def in_slot_order(raws, slots):
    nblocks = slots.shape[0]
    rows, width = raws[0].shape
    groups = len(raws) // CHUNKS
    return pl.pallas_call(
        order_kernel,
        in_specs=[pl.BlockSpec(memory_space=pltpu.SMEM)] + [pl.BlockSpec(memory_space=pltpu.VMEM)] * len(raws),
        out_specs=pl.BlockSpec(memory_space=pltpu.VMEM),
        out_shape=jax.ShapeDtypeStruct((nblocks, groups * rows // nblocks, CHUNKS * width), jnp.bfloat16),
        compiler_params=pltpu.CompilerParams(vmem_limit_bytes=4 * 1024 * 1024),
        cost_estimate=pl.CostEstimate(
            flops=rows * width, bytes_accessed=6 * len(raws) * rows * width, transcendentals=0
        ),
    )(slots, *raws)


def finish_kernel(got_ref, allowed_ref, out_ref):
    n, owned, quad, examples, half = got_ref.shape
    parts = half // LANES
    per_row = owned * CORES * parts
    for device in range(n):
        for core in range(CORES):
            sources = [(device & ~3) | (y << 1) | core for y in range(quad // CORES)]
            for slot in range(owned):
                scores = sum(got_ref[s, slot, s ^ device].astype(jnp.float32) for s in sources)
                scores = scores * allowed_ref[slot:slot + 1, core * half:(core + 1) * half]
                for i in range(parts):
                    first = device * examples * per_row + (slot * CORES + core) * parts + i
                    out_ref[pl.ds(first, examples, stride=per_row), :] = scores[:, i * LANES:(i + 1) * LANES]


def finish(got, allowed):
    n, owned, _, examples, half = got.shape
    flat = pl.pallas_call(
        finish_kernel,
        out_shape=jax.ShapeDtypeStruct((n * examples * owned * CORES * half // LANES, LANES), jnp.float32),
        compiler_params=pltpu.CompilerParams(vmem_limit_bytes=4 * 1024 * 1024),
        cost_estimate=pl.CostEstimate(flops=got.size, bytes_accessed=4 * got.size, transcendentals=0),
    )(got, allowed)
    return flat.reshape(n * examples, owned, CORES * half)


def shards(queries, precond, train, query_cluster, cand_blocks, cand_count, slot_block):
    n = lax.axis_size("rows")
    chips = n // CORES
    bits = chips.bit_length() - 1
    ybit, zbit = 1, 1 + bits // 2
    rest = [bit for bit in range(1, 1 + bits) if bit not in (ybit, zbit)]
    me = lax.axis_index("rows")
    core = me & 1

    examples, nblocks, width = train.shape
    nq = queries.shape[0]

    def swap(value, bit):
        return lax.ppermute(value, "rows", [(r, r ^ (1 << bit)) for r in range(n)])

    rows = nq // CORES // CHUNKS // PATHS
    sizes = {(ybit, width // 2), (zbit, rows // 2)} | {(bit, rows >> (i + 2)) for i, bit in enumerate(rest[:-1])}
    offsets = {}
    first_half = {}
    for bit, size in sorted(sizes):
        side = (me >> bit) & 1
        offsets[bit, size] = (side * size, (1 - side) * size)
        first_half[bit] = side == 0
    owned = nblocks // n
    first_slot = me * owned
    scalars = (core, 1 - core, first_slot, offsets, first_half)
    scalars, queries, train = lax.optimization_barrier((scalars, queries, train))
    core, other_core, first_slot, offsets, first_half = scalars

    def pack(value):
        return (value * UNIT).astype(jnp.float16)

    def unpack(value):
        return value.astype(jnp.float32) * (1.0 / UNIT)

    def part(value, bit, axis, other=0):
        shape = list(value.shape)
        shape[axis] //= 2
        starts = [0] * value.ndim
        starts[axis] = offsets[bit, shape[axis]][other]
        return lax.dynamic_slice(value, starts, shape, allow_negative_indices=False)

    def give(value, bit, axis):
        return pack(part(value, bit, axis, 1))

    def keep(value, got, bit, axis):
        return part(value, bit, axis) + unpack(got)

    def join(own, got, bit):
        mine_first = jnp.concatenate([own, got], axis=1)
        return jnp.where(first_half[bit], mine_first, jnp.concatenate([got, own], axis=1))

    def after(value, first):
        return lax.optimization_barrier((value, first))[0]

    def paths(value, other):
        value = value + unpack(other)
        return [value[i * rows:(i + 1) * rows] for i in range(PATHS)]

    levels = ((ybit, 1), (zbit, 0)), ((zbit, 0), (ybit, 1))

    def messages(values, step):
        return [give(value, *level[step]) for value, level in zip(values, levels)]

    def exchange(values, sent, step):
        got = [swap(message, level[step][0]) for message, level in zip(sent, levels)]
        return [keep(value, message, *level[step]) for value, message, level in zip(values, got, levels)]

    def halve(values):
        value = jnp.stack(values)
        for bit in rest[:-1]:
            value = keep(value, swap(give(value, bit, 1), bit), bit, 1)
        return value

    def gather(value, first=None):
        for bit in reversed([zbit] + rest[:-1]):
            got = swap(value, bit)
            if first is not None and bit == zbit:
                got = after(got, first)
            value = join(value, got, bit)
        return value.reshape(-1, value.shape[-1])

    def scores(group, value):
        return lax.dot_general(group, value, (((1,), (1,)), ((), ())), preferred_element_type=jnp.float32)

    blocks = train.reshape(examples * nblocks, width)
    middle = examples // 2 * nblocks

    def features(blocks, first, count, other):
        start = offsets[ybit, width // 2][other]
        return lax.dynamic_slice(blocks, (first, start), (count, width // 2), allow_negative_indices=False)

    early = features(blocks, 0, middle, 1)
    other_core, blocks = after((other_core, blocks), early)
    early = swap(early, ybit)

    *full, high, low = product(other_core, queries, [precond], other_kernel, OTHER_VMEM)
    sent = [pack(value) for value in full]
    got = [swap(value, 0) for value in sent]
    blocks = after(blocks, sent)
    near = features(blocks, 0, 2 * middle, 0)
    late = features(blocks, middle, middle, 1)
    sibling = swap(near, 0)
    mine = product(after(core, sent), queries, [high, low], mine_kernel, MINE_VMEM)
    one = paths(mine[0], got[0])
    sent = messages(one, 0)
    two = paths(mine[1], after(got[1], sent))
    one = exchange(one, sent, 0)
    sent = messages(one, 1)
    two = exchange(two, after(messages(two, 0), (sent, sibling)), 0)
    one = halve(exchange(one, sent, 1))
    got_one = swap(pack(one), rest[-1])
    two = exchange(two, messages(two, 1), 1)
    two = halve(two)
    sent = pack(two)
    one = (after(one, sent) + unpack(got_one)).astype(jnp.bfloat16)
    got_two = swap(sent, rest[-1])
    late, early = after((late, early), one)
    late = swap(late, ybit)
    one = gather(one)
    groups = [
        jnp.concatenate([near, sibling], axis=0),
        jnp.concatenate([early, late, swap(early, 0), swap(late, 0)], axis=0),
    ]
    raws = [scores(group, one) for group in groups]
    two = gather((two + unpack(got_two)).astype(jnp.bfloat16), raws)
    raws = raws + [scores(group, two) for group in groups]

    ordered = in_slot_order(raws, slot_block).reshape(n, owned, 2 * CORES * examples, nq // CORES)
    got = lax.all_to_all(ordered, "rows", split_axis=0, concat_axis=0, tiled=True)

    lists = (query_cluster, cand_blocks, cand_count, slot_block, first_slot)
    query_cluster, cand_blocks, cand_count, slot_block, first_slot = after(lists, ordered)
    allowed = listed_mask(query_cluster, cand_blocks, cand_count, nblocks)
    slots = lax.dynamic_slice(slot_block, (first_slot,), (owned,), allow_negative_indices=False)
    own_allowed = jnp.take(allowed, slots, axis=0, mode="clip")
    return finish(got.reshape(n, owned, 2 * CORES, examples, nq // CORES), own_allowed)


def solution(mesh):
    placed = (
        P("groups", "rows"),
        P("rows", None),
        P("rows", "groups", None),
        P("groups"),
        P("groups", None),
        P("groups"),
        P("groups"),
    )
    return jax.shard_map(
        shards,
        mesh=mesh,
        in_specs=placed,
        out_specs=P(None, ("groups", "rows"), None),
        check_vma=False,
    )
```

```python
import jax
import jax.numpy as jnp
from jax import lax
from jax.experimental import pallas as pl
from jax.experimental.pallas import tpu as pltpu
from jax.sharding import PartitionSpec as P

CORES = 2
CHUNKS = 2
PATHS = 2
UNIT = 4.0
LANES = 128
OTHER_VMEM = 44
MINE_VMEM = 16


def listed_mask(query_cluster, cand_blocks, cand_count, nblocks):
    nclusters = cand_blocks.shape[0]
    valid = jnp.arange(cand_blocks.shape[1])[None, :] < cand_count[:, None]
    hits = (cand_blocks[:, :, None] == jnp.arange(nblocks)[None, None, :]) & valid[:, :, None]
    listed = jnp.any(hits, axis=1).astype(jnp.float32)
    onehot = (query_cluster[:, None] == jnp.arange(nclusters)[None, :]).astype(jnp.float32)
    return jnp.dot(listed.T, onehot.T, preferred_element_type=jnp.float32)


def split(value):
    high = value.astype(jnp.bfloat16)
    return high, (value - high.astype(jnp.float32)).astype(jnp.bfloat16)


def rows_of(core_ref, rows_ref):
    half = rows_ref.shape[0] // CORES
    return rows_ref[pl.ds(pl.multiple_of(core_ref[0] * half, half), half), :]


def multiply(left, high, low, outs, columns):
    right = jnp.concatenate([high, high, low], axis=0)
    result = jnp.dot(left, right, preferred_element_type=jnp.float32)
    part = result.shape[0] // len(outs)
    for chunk, out_ref in enumerate(outs):
        out_ref[:, columns] = result[chunk * part:(chunk + 1) * part]


def other_kernel(core_ref, rows_ref, columns_hbm, *refs):
    outs, (high_ref, low_ref, columns_ref, sems) = refs[:-4], refs[-4:]
    steps, _, block = columns_ref.shape

    def load(i):
        return pltpu.make_async_copy(
            columns_hbm.at[:, i * block:(i + 1) * block], columns_ref.at[i], sems.at[i]
        )

    for i in range(steps):
        load(i).start()
    left = rows_of(core_ref, rows_ref)
    for i in range(steps):
        load(i).wait()
        columns = slice(i * block, (i + 1) * block)
        high, low = split(columns_ref[i])
        high_ref[:, columns] = high
        low_ref[:, columns] = low
        multiply(left, high, low, outs, columns)


def mine_kernel(core_ref, rows_ref, high_ref, low_ref, *outs):
    left = rows_of(core_ref, rows_ref)
    width = high_ref.shape[1]
    block = min(512, width)
    for i in range(width // block):
        columns = slice(i * block, (i + 1) * block)
        multiply(left, high_ref[:, columns], low_ref[:, columns], outs, columns)


def product(core, rows, columns, kernel, vmem):
    nrows = rows.shape[0]
    depth, width = columns[0].shape
    block = min(512, width)
    part = nrows // CORES // CHUNKS
    out = [jax.ShapeDtypeStruct((part, width), jnp.float32)] * CHUNKS
    in_vmem = pl.BlockSpec(memory_space=pltpu.VMEM)
    operand, scratch = in_vmem, []
    if kernel is other_kernel:
        out = out + [jax.ShapeDtypeStruct((depth, width), jnp.bfloat16)] * 2
        operand = pl.BlockSpec(memory_space=pltpu.HBM)
        scratch = [
            pltpu.VMEM((width // block, depth, block), jnp.float32),
            pltpu.SemaphoreType.DMA((width // block,)),
        ]
    return pl.pallas_call(
        kernel,
        in_specs=[pl.BlockSpec(memory_space=pltpu.SMEM), in_vmem] + [operand] * len(columns),
        out_specs=[in_vmem] * len(out),
        out_shape=out,
        scratch_shapes=scratch,
        compiler_params=pltpu.CompilerParams(vmem_limit_bytes=vmem * 1024 * 1024),
        cost_estimate=pl.CostEstimate(
            flops=3 * nrows * depth * width,
            bytes_accessed=4 * width * depth + 2 * width * nrows,
            transcendentals=0,
        ),
    )(core.reshape(1), rows, *columns)


def order_kernel(slots_ref, *refs):
    raws, out_ref = refs[:-1], refs[-1]
    nblocks = slots_ref.shape[0]
    groups = len(raws) // CHUNKS
    first = pl.program_id(0) * out_ref.shape[0]
    for slot in range(out_ref.shape[0]):
        for i, raw_ref in enumerate(raws):
            examples, width = raw_ref.shape[0] // nblocks, raw_ref.shape[1]
            chunk, group = divmod(i, groups)
            rows = pl.ds(slots_ref[first + slot], examples, stride=nblocks)
            out_ref[
                slot, group * examples:(group + 1) * examples, chunk * width:(chunk + 1) * width
            ] = raw_ref[rows, :].astype(out_ref.dtype)


def in_slot_order(raws, slots):
    nblocks = slots.shape[0]
    rows, width = raws[0].shape
    groups = len(raws) // CHUNKS
    shape = (nblocks, groups * rows // nblocks, CHUNKS * width)
    return pl.pallas_call(
        order_kernel,
        grid=(4,),
        in_specs=[pl.BlockSpec(memory_space=pltpu.SMEM)] + [pl.BlockSpec(memory_space=pltpu.VMEM)] * len(raws),
        out_specs=pl.BlockSpec((nblocks // 4,) + shape[1:], lambda i: (i, 0, 0)),
        out_shape=jax.ShapeDtypeStruct(shape, jnp.bfloat16),
        compiler_params=pltpu.CompilerParams(vmem_limit_bytes=8 * 1024 * 1024),
        cost_estimate=pl.CostEstimate(
            flops=rows * width, bytes_accessed=6 * len(raws) * rows * width, transcendentals=0
        ),
    )(slots, *raws)


def finish_kernel(got_ref, allowed_ref, out_ref):
    n, owned, quad, examples, half = got_ref.shape
    parts = half // LANES
    per_row = owned * CORES * parts
    for device in range(n):
        for core in range(CORES):
            sources = [(device & ~3) | (y << 1) | core for y in range(quad // CORES)]
            for slot in range(owned):
                scores = sum(got_ref[s, slot, s ^ device].astype(jnp.float32) for s in sources)
                scores = scores * allowed_ref[slot:slot + 1, core * half:(core + 1) * half]
                for i in range(parts):
                    first = device * examples * per_row + (slot * CORES + core) * parts + i
                    out_ref[pl.ds(first, examples, stride=per_row), :] = scores[:, i * LANES:(i + 1) * LANES]


def finish(got, allowed):
    n, owned, _, examples, half = got.shape
    flat = pl.pallas_call(
        finish_kernel,
        out_shape=jax.ShapeDtypeStruct((n * examples * owned * CORES * half // LANES, LANES), jnp.float32),
        compiler_params=pltpu.CompilerParams(vmem_limit_bytes=4 * 1024 * 1024),
        cost_estimate=pl.CostEstimate(flops=got.size, bytes_accessed=4 * got.size, transcendentals=0),
    )(got, allowed)
    return flat.reshape(n * examples, owned, CORES * half)


def shards(queries, precond, train, query_cluster, cand_blocks, cand_count, slot_block):
    n = lax.axis_size("rows")
    chips = n // CORES
    bits = chips.bit_length() - 1
    ybit, zbit = 1, 1 + bits // 2
    rest = [bit for bit in range(1, 1 + bits) if bit not in (ybit, zbit)]
    me = lax.axis_index("rows")
    core = me & 1

    examples, nblocks, width = train.shape
    nq = queries.shape[0]

    def swap(value, bit):
        return lax.ppermute(value, "rows", [(r, r ^ (1 << bit)) for r in range(n)])

    rows = nq // CORES // CHUNKS // PATHS
    sizes = {(ybit, width // 2), (zbit, rows // 2)} | {(bit, rows >> (i + 2)) for i, bit in enumerate(rest[:-1])}
    offsets = {}
    first_half = {}
    for bit, size in sorted(sizes):
        side = (me >> bit) & 1
        offsets[bit, size] = (side * size, (1 - side) * size)
        first_half[bit] = side == 0
    owned = nblocks // n
    first_slot = me * owned
    scalars = (core, 1 - core, first_slot, offsets, first_half)
    scalars, queries, train = lax.optimization_barrier((scalars, queries, train))
    core, other_core, first_slot, offsets, first_half = scalars

    def pack(value):
        return (value * UNIT).astype(jnp.float16)

    def unpack(value):
        return value.astype(jnp.float32) * (1.0 / UNIT)

    def part(value, bit, axis, other=0):
        shape = list(value.shape)
        shape[axis] //= 2
        starts = [0] * value.ndim
        starts[axis] = offsets[bit, shape[axis]][other]
        return lax.dynamic_slice(value, starts, shape, allow_negative_indices=False)

    def give(value, bit, axis):
        return pack(part(value, bit, axis, 1))

    def keep(value, got, bit, axis):
        return part(value, bit, axis) + unpack(got)

    def join(own, got, bit):
        mine_first = jnp.concatenate([own, got], axis=1)
        return jnp.where(first_half[bit], mine_first, jnp.concatenate([got, own], axis=1))

    def after(value, first):
        return lax.optimization_barrier((value, first))[0]

    def paths(value, other):
        value = value + unpack(other)
        return [value[i * rows:(i + 1) * rows] for i in range(PATHS)]

    levels = ((ybit, 1), (zbit, 0)), ((zbit, 0), (ybit, 1))

    def messages(values, step):
        return [give(value, *level[step]) for value, level in zip(values, levels)]

    def exchange(values, sent, step):
        got = [swap(message, level[step][0]) for message, level in zip(sent, levels)]
        return [keep(value, message, *level[step]) for value, message, level in zip(values, got, levels)]

    def halve(values):
        value = jnp.stack(values)
        for bit in rest[:-1]:
            value = keep(value, swap(give(value, bit, 1), bit), bit, 1)
        return value

    def gather(value, first=None):
        for bit in reversed([zbit] + rest[:-1]):
            got = swap(value, bit)
            if first is not None and bit == zbit:
                got = after(got, first)
            value = join(value, got, bit)
        return value.reshape(-1, value.shape[-1])

    def scores(group, value):
        return lax.dot_general(group, value, (((1,), (1,)), ((), ())), preferred_element_type=jnp.float32)

    blocks = train.reshape(examples * nblocks, width)
    middle = examples // 2 * nblocks

    def features(blocks, first, count, other):
        start = offsets[ybit, width // 2][other]
        return lax.dynamic_slice(blocks, (first, start), (count, width // 2), allow_negative_indices=False)

    high = lax.reduce_precision(queries, 8, 7)
    low = (queries - high).astype(jnp.bfloat16)
    high = high.astype(jnp.bfloat16)
    left = jnp.concatenate([high, low, high], axis=1)
    blocks = after(blocks, left)
    early = features(blocks, 0, middle, 1)
    other_core, blocks = after((other_core, blocks), early)
    early = swap(early, ybit)

    *full, high, low = product(other_core, left, [precond], other_kernel, OTHER_VMEM)
    sent = [pack(value) for value in full]
    got = [swap(value, 0) for value in sent]
    mine = product(after(core, sent), left, [high, low], mine_kernel, MINE_VMEM)
    one = paths(mine[0], got[0])
    sent = messages(one, 0)
    two = paths(mine[1], after(got[1], sent))
    blocks = after(blocks, sent)
    near = features(blocks, 0, 2 * middle, 0)
    late = features(blocks, middle, middle, 1)
    sibling = swap(near, 0)
    one = exchange(one, sent, 0)
    sent = messages(one, 1)
    two = exchange(two, after(messages(two, 0), sent), 0)
    one = halve(exchange(one, sent, 1))
    got_one = swap(pack(one), rest[-1])
    two = exchange(two, after(messages(two, 1), sibling), 1)
    two = halve(two)
    sent = pack(two)
    one = (after(one, sent) + unpack(got_one)).astype(jnp.bfloat16)
    got_two = swap(sent, rest[-1])
    late, early = after((late, early), one)
    late = swap(late, ybit)
    one = gather(one)
    groups = [
        jnp.concatenate([near, sibling], axis=0),
        jnp.concatenate([early, late, swap(early, 0), swap(late, 0)], axis=0),
    ]
    raws = [scores(group, one) for group in groups]
    two = gather((two + unpack(got_two)).astype(jnp.bfloat16), raws)
    raws = raws + [scores(group, two) for group in groups]

    ordered = in_slot_order(raws, slot_block).reshape(n, owned, 2 * CORES * examples, nq // CORES)
    got = lax.all_to_all(ordered, "rows", split_axis=0, concat_axis=0, tiled=True)

    lists = (query_cluster, cand_blocks, cand_count, slot_block, first_slot)
    query_cluster, cand_blocks, cand_count, slot_block, first_slot = after(lists, ordered)
    allowed = listed_mask(query_cluster, cand_blocks, cand_count, nblocks)
    slots = lax.dynamic_slice(slot_block, (first_slot,), (owned,), allow_negative_indices=False)
    own_allowed = jnp.take(allowed, slots, axis=0, mode="clip")
    return finish(got.reshape(n, owned, 2 * CORES, examples, nq // CORES), own_allowed)


def solution(mesh):
    placed = (
        P("groups", "rows"),
        P("rows", None),
        P("rows", "groups", None),
        P("groups"),
        P("groups", None),
        P("groups"),
        P("groups"),
    )
    return jax.shard_map(
        shards,
        mesh=mesh,
        in_specs=placed,
        out_specs=P(None, ("groups", "rows"), None),
        check_vma=False,
    )
```

```python
import jax
import jax.numpy as jnp
from jax import lax
from jax.experimental import pallas as pl
from jax.experimental.pallas import tpu as pltpu
from jax.sharding import PartitionSpec as P

CORES = 2
CHUNKS = 2
PATHS = 2
UNIT = 4.0
LANES = 128
OTHER_VMEM = 44
MINE_VMEM = 16


def listed_mask(query_cluster, cand_blocks, cand_count, nblocks):
    nclusters = cand_blocks.shape[0]
    valid = jnp.arange(cand_blocks.shape[1])[None, :] < cand_count[:, None]
    hits = (cand_blocks[:, :, None] == jnp.arange(nblocks)[None, None, :]) & valid[:, :, None]
    listed = jnp.any(hits, axis=1).astype(jnp.float32)
    onehot = (query_cluster[:, None] == jnp.arange(nclusters)[None, :]).astype(jnp.float32)
    return jnp.dot(listed.T, onehot.T, preferred_element_type=jnp.float32)


def split(value):
    high = value.astype(jnp.bfloat16)
    return high, (value - high.astype(jnp.float32)).astype(jnp.bfloat16)


def rows_of(core_ref, rows_ref):
    half = rows_ref.shape[0] // CORES
    return rows_ref[pl.ds(pl.multiple_of(core_ref[0] * half, half), half), :]


def multiply(left, high, low, outs, columns):
    right = jnp.concatenate([high, high, low], axis=0)
    result = jnp.dot(left, right, preferred_element_type=jnp.float32)
    part = result.shape[0] // len(outs)
    for chunk, out_ref in enumerate(outs):
        out_ref[:, columns] = result[chunk * part:(chunk + 1) * part]


def other_kernel(core_ref, rows_ref, columns_hbm, *refs):
    outs, (high_ref, low_ref, columns_ref, sems) = refs[:-4], refs[-4:]
    steps, _, block = columns_ref.shape

    def load(i):
        return pltpu.make_async_copy(
            columns_hbm.at[:, i * block:(i + 1) * block], columns_ref.at[i], sems.at[i]
        )

    for i in range(steps):
        load(i).start()
    left = rows_of(core_ref, rows_ref)
    for i in range(steps):
        load(i).wait()
        columns = slice(i * block, (i + 1) * block)
        high, low = split(columns_ref[i])
        high_ref[:, columns] = high
        low_ref[:, columns] = low
        multiply(left, high, low, outs, columns)


def mine_kernel(core_ref, rows_ref, high_ref, low_ref, *outs):
    left = rows_of(core_ref, rows_ref)
    width = high_ref.shape[1]
    block = min(512, width)
    for i in range(width // block):
        columns = slice(i * block, (i + 1) * block)
        multiply(left, high_ref[:, columns], low_ref[:, columns], outs, columns)


def product(core, rows, columns, kernel, vmem):
    nrows = rows.shape[0]
    depth, width = columns[0].shape
    block = min(512, width)
    part = nrows // CORES // CHUNKS
    out = [jax.ShapeDtypeStruct((part, width), jnp.float32)] * CHUNKS
    in_vmem = pl.BlockSpec(memory_space=pltpu.VMEM)
    operand, scratch = in_vmem, []
    if kernel is other_kernel:
        out = out + [jax.ShapeDtypeStruct((depth, width), jnp.bfloat16)] * 2
        operand = pl.BlockSpec(memory_space=pltpu.HBM)
        scratch = [
            pltpu.VMEM((width // block, depth, block), jnp.float32),
            pltpu.SemaphoreType.DMA((width // block,)),
        ]
    return pl.pallas_call(
        kernel,
        in_specs=[pl.BlockSpec(memory_space=pltpu.SMEM), in_vmem] + [operand] * len(columns),
        out_specs=[in_vmem] * len(out),
        out_shape=out,
        scratch_shapes=scratch,
        compiler_params=pltpu.CompilerParams(vmem_limit_bytes=vmem * 1024 * 1024),
        cost_estimate=pl.CostEstimate(
            flops=3 * nrows * depth * width,
            bytes_accessed=4 * width * depth + 2 * width * nrows,
            transcendentals=0,
        ),
    )(core.reshape(1), rows, *columns)


def order_kernel(slots_ref, *refs):
    raws, out_ref = refs[:-1], refs[-1]
    nblocks = slots_ref.shape[0]
    groups = len(raws) // CHUNKS
    for slot in range(nblocks):
        for i, raw_ref in enumerate(raws):
            examples, width = raw_ref.shape[0] // nblocks, raw_ref.shape[1]
            chunk, group = divmod(i, groups)
            rows = pl.ds(slots_ref[slot], examples, stride=nblocks)
            out_ref[
                slot, group * examples:(group + 1) * examples, chunk * width:(chunk + 1) * width
            ] = raw_ref[rows, :].astype(out_ref.dtype)


def in_slot_order(raws, slots):
    nblocks = slots.shape[0]
    rows, width = raws[0].shape
    groups = len(raws) // CHUNKS
    return pl.pallas_call(
        order_kernel,
        in_specs=[pl.BlockSpec(memory_space=pltpu.SMEM)] + [pl.BlockSpec(memory_space=pltpu.VMEM)] * len(raws),
        out_specs=pl.BlockSpec(memory_space=pltpu.VMEM),
        out_shape=jax.ShapeDtypeStruct((nblocks, groups * rows // nblocks, CHUNKS * width), jnp.bfloat16),
        compiler_params=pltpu.CompilerParams(vmem_limit_bytes=4 * 1024 * 1024),
        cost_estimate=pl.CostEstimate(
            flops=rows * width, bytes_accessed=6 * len(raws) * rows * width, transcendentals=0
        ),
    )(slots, *raws)


def finish_kernel(got_ref, allowed_ref, out_ref):
    n, owned, quad, examples, half = got_ref.shape
    parts = half // LANES
    per_row = owned * CORES * parts
    for device in range(n):
        for core in range(CORES):
            sources = [(device & ~3) | (y << 1) | core for y in range(quad // CORES)]
            for slot in range(owned):
                scores = sum(got_ref[s, slot, s ^ device].astype(jnp.float32) for s in sources)
                scores = scores * allowed_ref[slot:slot + 1, core * half:(core + 1) * half]
                for i in range(parts):
                    first = device * examples * per_row + (slot * CORES + core) * parts + i
                    out_ref[pl.ds(first, examples, stride=per_row), :] = scores[:, i * LANES:(i + 1) * LANES]


def finish(got, allowed):
    n, owned, _, examples, half = got.shape
    flat = pl.pallas_call(
        finish_kernel,
        out_shape=jax.ShapeDtypeStruct((n * examples * owned * CORES * half // LANES, LANES), jnp.float32),
        compiler_params=pltpu.CompilerParams(vmem_limit_bytes=4 * 1024 * 1024),
        cost_estimate=pl.CostEstimate(flops=got.size, bytes_accessed=4 * got.size, transcendentals=0),
    )(got, allowed)
    return flat.reshape(n * examples, owned, CORES * half)


def shards(queries, precond, train, query_cluster, cand_blocks, cand_count, slot_block):
    n = lax.axis_size("rows")
    chips = n // CORES
    bits = chips.bit_length() - 1
    ybit, zbit = 1, 1 + bits // 2
    rest = [bit for bit in range(1, 1 + bits) if bit not in (ybit, zbit)]
    me = lax.axis_index("rows")
    core = me & 1

    examples, nblocks, width = train.shape
    nq = queries.shape[0]

    def swap(value, bit):
        return lax.ppermute(value, "rows", [(r, r ^ (1 << bit)) for r in range(n)])

    rows = nq // CORES // CHUNKS // PATHS
    sizes = {(ybit, width // 2), (zbit, rows // 2)} | {(bit, rows >> (i + 2)) for i, bit in enumerate(rest[:-1])}
    offsets = {}
    first_half = {}
    for bit, size in sorted(sizes):
        side = (me >> bit) & 1
        offsets[bit, size] = (side * size, (1 - side) * size)
        first_half[bit] = side == 0
    owned = nblocks // n
    first_slot = me * owned
    scalars = (core, 1 - core, first_slot, offsets, first_half)
    scalars, queries, train = lax.optimization_barrier((scalars, queries, train))
    core, other_core, first_slot, offsets, first_half = scalars

    def pack(value):
        return (value * UNIT).astype(jnp.float16)

    def unpack(value):
        return value.astype(jnp.float32) * (1.0 / UNIT)

    def part(value, bit, axis, other=0):
        shape = list(value.shape)
        shape[axis] //= 2
        starts = [0] * value.ndim
        starts[axis] = offsets[bit, shape[axis]][other]
        return lax.dynamic_slice(value, starts, shape, allow_negative_indices=False)

    def give(value, bit, axis):
        return pack(part(value, bit, axis, 1))

    def keep(value, got, bit, axis):
        return part(value, bit, axis) + unpack(got)

    def join(own, got, bit):
        mine_first = jnp.concatenate([own, got], axis=1)
        return jnp.where(first_half[bit], mine_first, jnp.concatenate([got, own], axis=1))

    def after(value, first):
        return lax.optimization_barrier((value, first))[0]

    def paths(value, other):
        value = value + unpack(other)
        return [value[i * rows:(i + 1) * rows] for i in range(PATHS)]

    levels = ((ybit, 1), (zbit, 0)), ((zbit, 0), (ybit, 1))

    def messages(values, step):
        return [give(value, *level[step]) for value, level in zip(values, levels)]

    def exchange(values, sent, step):
        got = [swap(message, level[step][0]) for message, level in zip(sent, levels)]
        return [keep(value, message, *level[step]) for value, message, level in zip(values, got, levels)]

    def halve(values):
        value = jnp.stack(values)
        for bit in rest[:-1]:
            value = keep(value, swap(give(value, bit, 1), bit), bit, 1)
        return value

    def gather(value, first=None):
        for bit in reversed([zbit] + rest[:-1]):
            got = swap(value, bit)
            if first is not None and bit == zbit:
                got = after(got, first)
            value = join(value, got, bit)
        return value.reshape(-1, value.shape[-1])

    def scores(group, value):
        return lax.dot_general(group, value, (((1,), (1,)), ((), ())), preferred_element_type=jnp.float32)

    blocks = train.reshape(examples * nblocks, width)
    middle = examples // 2 * nblocks

    def features(blocks, first, count, other):
        start = offsets[ybit, width // 2][other]
        return lax.dynamic_slice(blocks, (first, start), (count, width // 2), allow_negative_indices=False)

    high = lax.reduce_precision(queries, 8, 7)
    low = (queries - high).astype(jnp.bfloat16)
    high = high.astype(jnp.bfloat16)
    left = jnp.concatenate([high, low, high], axis=1)
    blocks = after(blocks, left)
    early = features(blocks, 0, middle, 1)
    other_core, blocks = after((other_core, blocks), early)
    early = swap(early, ybit)

    *full, high, low = product(other_core, left, [precond], other_kernel, OTHER_VMEM)
    sent = [pack(value) for value in full]
    got = [swap(value, 0) for value in sent]
    blocks = after(blocks, sent)
    near = features(blocks, 0, 2 * middle, 0)
    sibling = swap(near, 0)
    mine = product(after(core, sent), left, [high, low], mine_kernel, MINE_VMEM)
    one = paths(mine[0], got[0])
    sent = messages(one, 0)
    two = paths(mine[1], after(got[1], sent))
    one = exchange(one, sent, 0)
    sent = messages(one, 1)
    sent_two = after(messages(two, 0), (sent, sibling))
    one = halve(exchange(one, sent, 1))
    sent = pack(one)
    got_one = swap(sent, rest[-1])
    two = exchange(two, sent_two, 0)
    two = exchange(two, messages(two, 1), 1)
    two = halve(two)
    sent = pack(two)
    one = (after(one, sent) + unpack(got_one)).astype(jnp.bfloat16)
    got_two = swap(sent, rest[-1])
    blocks, early = after((blocks, early), one)
    late = swap(features(blocks, middle, middle, 1), ybit)
    one = gather(one)
    groups = [
        jnp.concatenate([near, sibling], axis=0),
        jnp.concatenate([early, late, swap(early, 0), swap(late, 0)], axis=0),
    ]
    raws = [scores(group, one) for group in groups]
    two = gather((two + unpack(got_two)).astype(jnp.bfloat16), raws)
    raws = raws + [scores(group, two) for group in groups]

    ordered = in_slot_order(raws, slot_block).reshape(n, owned, 2 * CORES * examples, nq // CORES)
    got = lax.all_to_all(ordered, "rows", split_axis=0, concat_axis=0, tiled=True)

    lists = (query_cluster, cand_blocks, cand_count, slot_block, first_slot)
    query_cluster, cand_blocks, cand_count, slot_block, first_slot = after(lists, ordered)
    allowed = listed_mask(query_cluster, cand_blocks, cand_count, nblocks)
    slots = lax.dynamic_slice(slot_block, (first_slot,), (owned,), allow_negative_indices=False)
    own_allowed = jnp.take(allowed, slots, axis=0, mode="clip")
    return finish(got.reshape(n, owned, 2 * CORES, examples, nq // CORES), own_allowed)


def solution(mesh):
    placed = (
        P("groups", "rows"),
        P("rows", None),
        P("rows", "groups", None),
        P("groups"),
        P("groups", None),
        P("groups"),
        P("groups"),
    )
    return jax.shard_map(
        shards,
        mesh=mesh,
        in_specs=placed,
        out_specs=P(None, ("groups", "rows"), None),
        check_vma=False,
    )
```

```python
import jax
import jax.numpy as jnp
from jax import lax
from jax.experimental import pallas as pl
from jax.experimental.pallas import tpu as pltpu
from jax.sharding import PartitionSpec as P

CORES = 2
CHUNKS = 2
PATHS = 2
UNIT = 4.0
LANES = 128
OTHER_VMEM = 44
MINE_VMEM = 16


def listed_mask(query_cluster, cand_blocks, cand_count, nblocks):
    nclusters = cand_blocks.shape[0]
    valid = jnp.arange(cand_blocks.shape[1])[None, :] < cand_count[:, None]
    hits = (cand_blocks[:, :, None] == jnp.arange(nblocks)[None, None, :]) & valid[:, :, None]
    listed = jnp.any(hits, axis=1).astype(jnp.float32)
    onehot = (query_cluster[:, None] == jnp.arange(nclusters)[None, :]).astype(jnp.float32)
    return jnp.dot(listed.T, onehot.T, preferred_element_type=jnp.float32)


def split(value):
    high = value.astype(jnp.bfloat16)
    return high, (value - high.astype(jnp.float32)).astype(jnp.bfloat16)


def rows_of(core_ref, rows_ref):
    half = rows_ref.shape[0] // CORES
    return rows_ref[pl.ds(pl.multiple_of(core_ref[0] * half, half), half), :]


def multiply(left, high, low, outs, columns):
    right = jnp.concatenate([high, high, low], axis=0)
    result = jnp.dot(left, right, preferred_element_type=jnp.float32)
    part = result.shape[0] // len(outs)
    for chunk, out_ref in enumerate(outs):
        out_ref[:, columns] = result[chunk * part:(chunk + 1) * part]


def other_kernel(core_ref, rows_ref, columns_hbm, *refs):
    outs, (high_ref, low_ref, columns_ref, sems) = refs[:-4], refs[-4:]
    steps, _, block = columns_ref.shape

    def load(i):
        return pltpu.make_async_copy(
            columns_hbm.at[:, i * block:(i + 1) * block], columns_ref.at[i], sems.at[i]
        )

    for i in range(steps):
        load(i).start()
    left = rows_of(core_ref, rows_ref)
    for i in range(steps):
        load(i).wait()
        columns = slice(i * block, (i + 1) * block)
        high, low = split(columns_ref[i])
        high_ref[:, columns] = high
        low_ref[:, columns] = low
        multiply(left, high, low, outs, columns)


def mine_kernel(core_ref, rows_ref, high_ref, low_ref, *outs):
    left = rows_of(core_ref, rows_ref)
    width = high_ref.shape[1]
    block = min(512, width)
    for i in range(width // block):
        columns = slice(i * block, (i + 1) * block)
        multiply(left, high_ref[:, columns], low_ref[:, columns], outs, columns)


def product(core, rows, columns, kernel, vmem):
    nrows = rows.shape[0]
    depth, width = columns[0].shape
    block = min(512, width)
    part = nrows // CORES // CHUNKS
    out = [jax.ShapeDtypeStruct((part, width), jnp.float32)] * CHUNKS
    in_vmem = pl.BlockSpec(memory_space=pltpu.VMEM)
    operand, scratch = in_vmem, []
    if kernel is other_kernel:
        out = out + [jax.ShapeDtypeStruct((depth, width), jnp.bfloat16)] * 2
        operand = pl.BlockSpec(memory_space=pltpu.HBM)
        scratch = [
            pltpu.VMEM((width // block, depth, block), jnp.float32),
            pltpu.SemaphoreType.DMA((width // block,)),
        ]
    return pl.pallas_call(
        kernel,
        in_specs=[pl.BlockSpec(memory_space=pltpu.SMEM), in_vmem] + [operand] * len(columns),
        out_specs=[in_vmem] * len(out),
        out_shape=out,
        scratch_shapes=scratch,
        compiler_params=pltpu.CompilerParams(vmem_limit_bytes=vmem * 1024 * 1024),
        cost_estimate=pl.CostEstimate(
            flops=3 * nrows * depth * width,
            bytes_accessed=4 * width * depth + 2 * width * nrows,
            transcendentals=0,
        ),
    )(core.reshape(1), rows, *columns)


def order_kernel(slots_ref, *refs):
    raws, out_ref = refs[:-1], refs[-1]
    nblocks = slots_ref.shape[0]
    groups = len(raws) // CHUNKS
    for slot in range(nblocks):
        for i, raw_ref in enumerate(raws):
            examples, width = raw_ref.shape[0] // nblocks, raw_ref.shape[1]
            chunk, group = divmod(i, groups)
            rows = pl.ds(slots_ref[slot], examples, stride=nblocks)
            out_ref[
                slot, group * examples:(group + 1) * examples, chunk * width:(chunk + 1) * width
            ] = raw_ref[rows, :].astype(out_ref.dtype)


def in_slot_order(raws, slots):
    nblocks = slots.shape[0]
    rows, width = raws[0].shape
    groups = len(raws) // CHUNKS
    return pl.pallas_call(
        order_kernel,
        in_specs=[pl.BlockSpec(memory_space=pltpu.SMEM)] + [pl.BlockSpec(memory_space=pltpu.VMEM)] * len(raws),
        out_specs=pl.BlockSpec(memory_space=pltpu.VMEM),
        out_shape=jax.ShapeDtypeStruct((nblocks, groups * rows // nblocks, CHUNKS * width), jnp.bfloat16),
        compiler_params=pltpu.CompilerParams(vmem_limit_bytes=4 * 1024 * 1024),
        cost_estimate=pl.CostEstimate(
            flops=rows * width, bytes_accessed=6 * len(raws) * rows * width, transcendentals=0
        ),
    )(slots, *raws)


def finish_kernel(got_ref, allowed_ref, out_ref):
    n, owned, quad, examples, half = got_ref.shape
    parts = half // LANES
    per_row = owned * CORES * parts
    for device in range(n):
        for core in range(CORES):
            sources = [(device & ~3) | (y << 1) | core for y in range(quad // CORES)]
            for slot in range(owned):
                scores = sum(got_ref[s, slot, s ^ device].astype(jnp.float32) for s in sources)
                scores = scores * allowed_ref[slot:slot + 1, core * half:(core + 1) * half]
                for i in range(parts):
                    first = device * examples * per_row + (slot * CORES + core) * parts + i
                    out_ref[pl.ds(first, examples, stride=per_row), :] = scores[:, i * LANES:(i + 1) * LANES]


def finish(got, allowed):
    n, owned, _, examples, half = got.shape
    flat = pl.pallas_call(
        finish_kernel,
        out_shape=jax.ShapeDtypeStruct((n * examples * owned * CORES * half // LANES, LANES), jnp.float32),
        compiler_params=pltpu.CompilerParams(vmem_limit_bytes=4 * 1024 * 1024),
        cost_estimate=pl.CostEstimate(flops=got.size, bytes_accessed=4 * got.size, transcendentals=0),
    )(got, allowed)
    return flat.reshape(n * examples, owned, CORES * half)


def shards(queries, precond, train, query_cluster, cand_blocks, cand_count, slot_block):
    n = lax.axis_size("rows")
    chips = n // CORES
    bits = chips.bit_length() - 1
    ybit, zbit = 1, 1 + bits // 2
    rest = [bit for bit in range(1, 1 + bits) if bit not in (ybit, zbit)]
    me = lax.axis_index("rows")
    core = me & 1

    examples, nblocks, width = train.shape
    nq = queries.shape[0]

    def swap(value, bit):
        return lax.ppermute(value, "rows", [(r, r ^ (1 << bit)) for r in range(n)])

    rows = nq // CORES // CHUNKS // PATHS
    sizes = {(ybit, width // 2), (zbit, rows // 2)} | {(bit, rows >> (i + 2)) for i, bit in enumerate(rest[:-1])}
    offsets = {}
    first_half = {}
    for bit, size in sorted(sizes):
        side = (me >> bit) & 1
        offsets[bit, size] = (side * size, (1 - side) * size)
        first_half[bit] = side == 0
    owned = nblocks // n
    first_slot = me * owned
    scalars = (core, 1 - core, first_slot, offsets, first_half)
    scalars, queries, train = lax.optimization_barrier((scalars, queries, train))
    core, other_core, first_slot, offsets, first_half = scalars

    def pack(value):
        return (value * UNIT).astype(jnp.float16)

    def unpack(value):
        return value.astype(jnp.float32) * (1.0 / UNIT)

    def part(value, bit, axis, other=0):
        shape = list(value.shape)
        shape[axis] //= 2
        starts = [0] * value.ndim
        starts[axis] = offsets[bit, shape[axis]][other]
        return lax.dynamic_slice(value, starts, shape, allow_negative_indices=False)

    def give(value, bit, axis):
        return pack(part(value, bit, axis, 1))

    def keep(value, got, bit, axis):
        return part(value, bit, axis) + unpack(got)

    def join(own, got, bit):
        mine_first = jnp.concatenate([own, got], axis=1)
        return jnp.where(first_half[bit], mine_first, jnp.concatenate([got, own], axis=1))

    def after(value, first):
        return lax.optimization_barrier((value, first))[0]

    def paths(value, other):
        value = value + unpack(other)
        return [value[i * rows:(i + 1) * rows] for i in range(PATHS)]

    levels = ((ybit, 1), (zbit, 0)), ((zbit, 0), (ybit, 1))

    def messages(values, step):
        return [give(value, *level[step]) for value, level in zip(values, levels)]

    def exchange(values, sent, step):
        got = [swap(message, level[step][0]) for message, level in zip(sent, levels)]
        return [keep(value, message, *level[step]) for value, message, level in zip(values, got, levels)]

    def halve(values):
        value = jnp.stack(values)
        for bit in rest[:-1]:
            value = keep(value, swap(give(value, bit, 1), bit), bit, 1)
        return value

    def gather(value, first=None):
        for bit in reversed([zbit] + rest[:-1]):
            got = swap(value, bit)
            if first is not None and bit == zbit:
                got = after(got, first)
            value = join(value, got, bit)
        return value.reshape(-1, value.shape[-1])

    def scores(group, value):
        return lax.dot_general(group, value, (((1,), (1,)), ((), ())), preferred_element_type=jnp.float32)

    blocks = train.reshape(examples * nblocks, width)
    total = examples * nblocks
    middle = max(1, examples * 3 // 8) * nblocks

    def features(blocks, first, count, other):
        start = offsets[ybit, width // 2][other]
        return lax.dynamic_slice(blocks, (first, start), (count, width // 2), allow_negative_indices=False)

    high = lax.reduce_precision(queries, 8, 7)
    low = (queries - high).astype(jnp.bfloat16)
    high = high.astype(jnp.bfloat16)
    left = jnp.concatenate([high, low, high], axis=1)
    blocks = after(blocks, left)
    early = features(blocks, 0, middle, 1)
    other_core, blocks = after((other_core, blocks), early)
    early = swap(early, ybit)

    *full, high, low = product(other_core, left, [precond], other_kernel, OTHER_VMEM)
    sent = [pack(value) for value in full]
    got = [swap(value, 0) for value in sent]
    blocks = after(blocks, sent)
    near = features(blocks, 0, total, 0)
    sibling = swap(near, 0)
    mine = product(after(core, sent), left, [high, low], mine_kernel, MINE_VMEM)
    one = paths(mine[0], got[0])
    sent = messages(one, 0)
    two = paths(mine[1], after(got[1], sent))
    one = exchange(one, sent, 0)
    sent = messages(one, 1)
    sent_two = after(messages(two, 0), (sent, sibling))
    one = halve(exchange(one, sent, 1))
    sent = pack(one)
    got_one = swap(sent, rest[-1])
    two = exchange(two, sent_two, 0)
    two = exchange(two, messages(two, 1), 1)
    two = halve(two)
    sent = pack(two)
    one = (after(one, sent) + unpack(got_one)).astype(jnp.bfloat16)
    got_two = swap(sent, rest[-1])
    blocks, early = after((blocks, early), one)
    late = swap(features(blocks, middle, total - middle, 1), ybit)
    one = gather(one)
    groups = [
        jnp.concatenate([near, sibling], axis=0),
        jnp.concatenate([early, late, swap(early, 0), swap(late, 0)], axis=0),
    ]
    raws = [scores(group, one) for group in groups]
    two = gather((two + unpack(got_two)).astype(jnp.bfloat16), raws)
    raws = raws + [scores(group, two) for group in groups]

    ordered = in_slot_order(raws, slot_block).reshape(n, owned, 2 * CORES * examples, nq // CORES)
    got = lax.all_to_all(ordered, "rows", split_axis=0, concat_axis=0, tiled=True)

    lists = (query_cluster, cand_blocks, cand_count, slot_block, first_slot)
    query_cluster, cand_blocks, cand_count, slot_block, first_slot = after(lists, ordered)
    allowed = listed_mask(query_cluster, cand_blocks, cand_count, nblocks)
    slots = lax.dynamic_slice(slot_block, (first_slot,), (owned,), allow_negative_indices=False)
    own_allowed = jnp.take(allowed, slots, axis=0, mode="clip")
    return finish(got.reshape(n, owned, 2 * CORES, examples, nq // CORES), own_allowed)


def solution(mesh):
    placed = (
        P("groups", "rows"),
        P("rows", None),
        P("rows", "groups", None),
        P("groups"),
        P("groups", None),
        P("groups"),
        P("groups"),
    )
    return jax.shard_map(
        shards,
        mesh=mesh,
        in_specs=placed,
        out_specs=P(None, ("groups", "rows"), None),
        check_vma=False,
    )
```

```python
import jax
import jax.numpy as jnp
from jax import lax
from jax.experimental import pallas as pl
from jax.experimental.pallas import tpu as pltpu
from jax.sharding import PartitionSpec as P

CORES = 2
CHUNKS = 2
PATHS = 2
TOP = 15.0
LEAST = -100.0
LANES = 128
LOAD_VMEM = 48
PRODUCT_VMEM = 16


def listed_mask(query_cluster, cand_blocks, cand_count, nblocks):
    nclusters = cand_blocks.shape[0]
    valid = jnp.arange(cand_blocks.shape[1])[None, :] < cand_count[:, None]
    hits = (cand_blocks[:, :, None] == jnp.arange(nblocks)[None, None, :]) & valid[:, :, None]
    listed = jnp.any(hits, axis=1).astype(jnp.float32)
    onehot = (query_cluster[:, None] == jnp.arange(nclusters)[None, :]).astype(jnp.float32)
    return jnp.dot(listed.T, onehot.T, preferred_element_type=jnp.float32)


def split(value):
    high = value.astype(jnp.bfloat16)
    return high, (value - high.astype(jnp.float32)).astype(jnp.bfloat16)


def rows_of(core_ref, rows_ref):
    half = rows_ref.shape[0] // CORES
    return rows_ref[pl.ds(pl.multiple_of(core_ref[0] * half, half), half), :]


def multiply(left, high, low, outs, columns):
    right = jnp.concatenate([high, high, low], axis=0)
    result = jnp.dot(left, right, preferred_element_type=jnp.float32)
    part = result.shape[0] // len(outs)
    for chunk, out_ref in enumerate(outs):
        out_ref[:, columns] = result[chunk * part:(chunk + 1) * part]


def load_kernel(rows_ref, columns_hbm, high_ref, low_ref, power_ref, columns_ref, sems):
    steps, depth, block = columns_ref.shape

    def load(i):
        return pltpu.make_async_copy(
            columns_hbm.at[:, i * block:(i + 1) * block], columns_ref.at[i], sems.at[i]
        )

    for i in range(steps):
        load(i).start()
    rows_peak = jnp.max(jnp.abs(rows_ref[:, :depth].astype(jnp.float32)), axis=0, keepdims=True)
    peak = jnp.zeros((1, block), jnp.float32)
    for i in range(steps):
        load(i).wait()
        columns = columns_ref[i]
        peak = jnp.maximum(peak, jnp.max(jnp.abs(columns), axis=0, keepdims=True))
        high, low = split(columns)
        high_ref[:, i * block:(i + 1) * block] = high
        low_ref[:, i * block:(i + 1) * block] = low
    bound = 1.02 * depth * jnp.max(rows_peak, axis=1, keepdims=True) * jnp.max(peak, axis=1, keepdims=True)
    power = jnp.maximum(jnp.ceil(jnp.log2(bound)), LEAST)
    power_ref[...] = jnp.broadcast_to(power, power_ref.shape)


def load_columns(rows, columns):
    depth, width = columns.shape
    block = min(512, width)
    in_vmem = pl.BlockSpec(memory_space=pltpu.VMEM)
    return pl.pallas_call(
        load_kernel,
        in_specs=[in_vmem, pl.BlockSpec(memory_space=pltpu.HBM)],
        out_specs=[in_vmem] * 3,
        out_shape=[jax.ShapeDtypeStruct((depth, width), jnp.bfloat16)] * 2
        + [jax.ShapeDtypeStruct((1, width), jnp.float32)],
        scratch_shapes=[
            pltpu.VMEM((width // block, depth, block), jnp.float32),
            pltpu.SemaphoreType.DMA((width // block,)),
        ],
        compiler_params=pltpu.CompilerParams(vmem_limit_bytes=LOAD_VMEM * 1024 * 1024),
        cost_estimate=pl.CostEstimate(
            flops=4 * depth * width, bytes_accessed=4 * depth * width, transcendentals=0
        ),
    )(rows, columns)


def product_kernel(core_ref, rows_ref, high_ref, low_ref, *outs):
    left = rows_of(core_ref, rows_ref)
    width = high_ref.shape[1]
    block = min(512, width)
    for i in range(width // block):
        columns = slice(i * block, (i + 1) * block)
        multiply(left, high_ref[:, columns], low_ref[:, columns], outs, columns)


def product(core, rows, high, low):
    nrows = rows.shape[0]
    depth, width = high.shape
    part = nrows // CORES // CHUNKS
    in_vmem = pl.BlockSpec(memory_space=pltpu.VMEM)
    return pl.pallas_call(
        product_kernel,
        in_specs=[pl.BlockSpec(memory_space=pltpu.SMEM)] + [in_vmem] * 3,
        out_specs=[in_vmem] * CHUNKS,
        out_shape=[jax.ShapeDtypeStruct((part, width), jnp.float32)] * CHUNKS,
        compiler_params=pltpu.CompilerParams(vmem_limit_bytes=PRODUCT_VMEM * 1024 * 1024),
        cost_estimate=pl.CostEstimate(
            flops=3 * nrows * depth * width,
            bytes_accessed=4 * width * depth + 2 * width * nrows,
            transcendentals=0,
        ),
    )(core.reshape(1), rows, high, low)


def order_kernel(slots_ref, *refs):
    raws, out_ref = refs[:-1], refs[-1]
    nblocks = slots_ref.shape[0]
    groups = len(raws) // CHUNKS
    for slot in range(nblocks):
        for i, raw_ref in enumerate(raws):
            examples, width = raw_ref.shape[0] // nblocks, raw_ref.shape[1]
            chunk, group = divmod(i, groups)
            rows = pl.ds(slots_ref[slot], examples, stride=nblocks)
            out_ref[
                slot, group * examples:(group + 1) * examples, chunk * width:(chunk + 1) * width
            ] = raw_ref[rows, :].astype(out_ref.dtype)


def in_slot_order(raws, slots):
    nblocks = slots.shape[0]
    rows, width = raws[0].shape
    groups = len(raws) // CHUNKS
    return pl.pallas_call(
        order_kernel,
        in_specs=[pl.BlockSpec(memory_space=pltpu.SMEM)] + [pl.BlockSpec(memory_space=pltpu.VMEM)] * len(raws),
        out_specs=pl.BlockSpec(memory_space=pltpu.VMEM),
        out_shape=jax.ShapeDtypeStruct((nblocks, groups * rows // nblocks, CHUNKS * width), jnp.bfloat16),
        compiler_params=pltpu.CompilerParams(vmem_limit_bytes=4 * 1024 * 1024),
        cost_estimate=pl.CostEstimate(
            flops=rows * width, bytes_accessed=6 * len(raws) * rows * width, transcendentals=0
        ),
    )(slots, *raws)


def finish_kernel(got_ref, allowed_ref, out_ref):
    n, owned, quad, examples, half = got_ref.shape
    parts = half // LANES
    per_row = owned * CORES * parts
    for device in range(n):
        for core in range(CORES):
            sources = [(device & ~3) | (y << 1) | core for y in range(quad // CORES)]
            for slot in range(owned):
                scores = sum(got_ref[s, slot, s ^ device].astype(jnp.float32) for s in sources)
                scores = scores * allowed_ref[slot:slot + 1, core * half:(core + 1) * half]
                for i in range(parts):
                    first = device * examples * per_row + (slot * CORES + core) * parts + i
                    out_ref[pl.ds(first, examples, stride=per_row), :] = scores[:, i * LANES:(i + 1) * LANES]


def finish(got, allowed):
    n, owned, _, examples, half = got.shape
    flat = pl.pallas_call(
        finish_kernel,
        out_shape=jax.ShapeDtypeStruct((n * examples * owned * CORES * half // LANES, LANES), jnp.float32),
        compiler_params=pltpu.CompilerParams(vmem_limit_bytes=4 * 1024 * 1024),
        cost_estimate=pl.CostEstimate(flops=got.size, bytes_accessed=4 * got.size, transcendentals=0),
    )(got, allowed)
    return flat.reshape(n * examples, owned, CORES * half)


def shards(queries, precond, train, query_cluster, cand_blocks, cand_count, slot_block):
    n = lax.axis_size("rows")
    chips = n // CORES
    bits = chips.bit_length() - 1
    ybit, zbit = 1, 1 + bits // 2
    rest = [bit for bit in range(1, 1 + bits) if bit not in (ybit, zbit)]
    me = lax.axis_index("rows")
    core = me & 1

    examples, nblocks, width = train.shape
    nq = queries.shape[0]

    def swap(value, bit):
        return lax.ppermute(value, "rows", [(r, r ^ (1 << bit)) for r in range(n)])

    rows = nq // CORES // CHUNKS // PATHS
    sizes = {(ybit, width // 2), (zbit, rows // 2)} | {(bit, rows >> (i + 2)) for i, bit in enumerate(rest[:-1])}
    offsets = {}
    first_half = {}
    for bit, size in sorted(sizes):
        side = (me >> bit) & 1
        offsets[bit, size] = (side * size, (1 - side) * size)
        first_half[bit] = side == 0
    owned = nblocks // n
    first_slot = me * owned
    scalars = (core, 1 - core, first_slot, offsets, first_half)
    scalars, queries, train = lax.optimization_barrier((scalars, queries, train))
    core, other_core, first_slot, offsets, first_half = scalars

    def pack(value, power):
        return (value * jnp.exp2(TOP - power[:, :value.shape[-1]])).astype(jnp.float16)

    def unpack(got, power):
        return got.astype(jnp.float32) * jnp.exp2(power[:, :got.shape[-1]] - TOP)

    def agree(power, bit, added):
        return jnp.maximum(power, swap(power, bit)) + added

    def part(value, bit, axis, other=0):
        shape = list(value.shape)
        shape[axis] //= 2
        starts = [0] * value.ndim
        starts[axis] = offsets[bit, shape[axis]][other]
        return lax.dynamic_slice(value, starts, shape, allow_negative_indices=False)

    def give(value, power, bit, axis):
        return pack(part(value, bit, axis, 1), power)

    def keep(value, got, power, bit, axis):
        return part(value, bit, axis) + unpack(got, power)

    def join(own, got, bit):
        mine_first = jnp.concatenate([own, got], axis=1)
        return jnp.where(first_half[bit], mine_first, jnp.concatenate([got, own], axis=1))

    def after(value, first):
        return lax.optimization_barrier((value, first))[0]

    def paths(value, got, power):
        value = value + unpack(got, power)
        return [value[i * rows:(i + 1) * rows] for i in range(PATHS)]

    levels = ((ybit, 1), (zbit, 0)), ((zbit, 0), (ybit, 1))

    def messages(values, powers, step):
        return [give(value, power, *level[step]) for value, power, level in zip(values, powers, levels)]

    def exchange(values, sent, powers, step):
        got = [swap(message, level[step][0]) for message, level in zip(sent, levels)]
        return [
            keep(value, message, power, *level[step])
            for value, message, power, level in zip(values, got, powers, levels)
        ]

    def halve(values, powers):
        value = jnp.stack(values)
        for bit, power in zip(rest[:-1], powers):
            value = keep(value, swap(give(value, power, bit, 1), bit), power, bit, 1)
        return value

    def total(value, got, power):
        return (value + unpack(got, power)).astype(jnp.bfloat16)

    def gather(value, first=None):
        for bit in reversed([zbit] + rest[:-1]):
            got = swap(value, bit)
            if first is not None and bit == zbit:
                got = after(got, first)
            value = join(value, got, bit)
        return value.reshape(-1, value.shape[-1])

    def scores(group, value):
        return lax.dot_general(group, value, (((1,), (1,)), ((), ())), preferred_element_type=jnp.float32)

    blocks = train.reshape(examples * nblocks, width)
    every = examples * nblocks
    middle = max(1, examples * 3 // 8) * nblocks

    def features(blocks, first, count, other):
        start = offsets[ybit, width // 2][other]
        return lax.dynamic_slice(blocks, (first, start), (count, width // 2), allow_negative_indices=False)

    high = lax.reduce_precision(queries, 8, 7)
    low = (queries - high).astype(jnp.bfloat16)
    high = high.astype(jnp.bfloat16)
    left = jnp.concatenate([high, low, high], axis=1)
    blocks = after(blocks, left)
    early = features(blocks, 0, middle, 1)
    other_core, blocks = after((other_core, blocks), early)
    early = swap(early, ybit)

    high, low, power = load_columns(after(left, other_core), precond)
    first_power = agree(power, 0, 0.0)
    full = product(other_core, left, high, low)
    sent = [pack(value, first_power) for value in full]
    got = [swap(value, 0) for value in sent]
    blocks = after(blocks, sent)
    near = features(blocks, 0, every, 0)
    sibling = swap(near, 0)
    power = after(first_power, sent)
    powers = [[agree(power, level[0][0], 1.0) for level in levels]]
    mine = product(after(core, sent), left, high, low)
    one = paths(mine[0], got[0], first_power)
    sent = messages(one, powers[0], 0)
    power = agree(after(powers[0][0], sent), levels[0][1][0], 1.0)
    powers.append([power] * PATHS)
    rest_powers = []
    for bit in rest:
        power = agree(power, bit, 1.0)
        rest_powers.append(power)
    two = paths(mine[1], after(got[1], sent), first_power)
    one = exchange(one, sent, powers[0], 0)
    sent = after(messages(one, powers[1], 1), (rest_powers, early))
    sent_two = after(messages(two, powers[0], 0), (sent, sibling))
    one = halve(exchange(one, sent, powers[1], 1), rest_powers)
    sent = pack(one, power)
    got_one = swap(sent, rest[-1])
    two = exchange(two, sent_two, powers[0], 0)
    two = halve(exchange(two, after(messages(two, powers[1], 1), sent), powers[1], 1), rest_powers)
    one = total(one, got_one, power)
    sent = after(pack(two, power), one)
    got_two = swap(sent, rest[-1])
    blocks, early = after((blocks, early), one)
    late = swap(features(blocks, middle, every - middle, 1), ybit)
    one = gather(one)
    groups = [
        jnp.concatenate([near, sibling], axis=0),
        jnp.concatenate([early, late, swap(early, 0), swap(late, 0)], axis=0),
    ]
    raws = [scores(group, one) for group in groups]
    two = gather(total(two, got_two, power), raws)
    raws = raws + [scores(group, two) for group in groups]

    ordered = in_slot_order(raws, slot_block).reshape(n, owned, 2 * CORES * examples, nq // CORES)
    got = lax.all_to_all(ordered, "rows", split_axis=0, concat_axis=0, tiled=True)

    lists = (query_cluster, cand_blocks, cand_count, slot_block, first_slot)
    query_cluster, cand_blocks, cand_count, slot_block, first_slot = after(lists, ordered)
    allowed = listed_mask(query_cluster, cand_blocks, cand_count, nblocks)
    slots = lax.dynamic_slice(slot_block, (first_slot,), (owned,), allow_negative_indices=False)
    own_allowed = jnp.take(allowed, slots, axis=0, mode="clip")
    return finish(got.reshape(n, owned, 2 * CORES, examples, nq // CORES), own_allowed)


def solution(mesh):
    placed = (
        P("groups", "rows"),
        P("rows", None),
        P("rows", "groups", None),
        P("groups"),
        P("groups", None),
        P("groups"),
        P("groups"),
    )
    return jax.shard_map(
        shards,
        mesh=mesh,
        in_specs=placed,
        out_specs=P(None, ("groups", "rows"), None),
        check_vma=False,
    )
```

```python
import jax
import jax.numpy as jnp
from jax import lax
from jax.experimental import pallas as pl
from jax.experimental.pallas import tpu as pltpu
from jax.sharding import PartitionSpec as P

CORES = 2
CHUNKS = 2
PATHS = 2
UNIT = 2.0 ** 18
LEAST = 2.0 ** -100
LANES = 128
OTHER_VMEM = 44
MINE_VMEM = 16


def listed_mask(query_cluster, cand_blocks, cand_count, nblocks):
    nclusters = cand_blocks.shape[0]
    valid = jnp.arange(cand_blocks.shape[1])[None, :] < cand_count[:, None]
    hits = (cand_blocks[:, :, None] == jnp.arange(nblocks)[None, None, :]) & valid[:, :, None]
    listed = jnp.any(hits, axis=1).astype(jnp.float32)
    onehot = (query_cluster[:, None] == jnp.arange(nclusters)[None, :]).astype(jnp.float32)
    return jnp.dot(listed.T, onehot.T, preferred_element_type=jnp.float32)


def split(value):
    high = value.astype(jnp.bfloat16)
    return high, (value - high.astype(jnp.float32)).astype(jnp.bfloat16)


def rows_of(core_ref, rows_ref):
    half = rows_ref.shape[0] // CORES
    return rows_ref[pl.ds(pl.multiple_of(core_ref[0] * half, half), half), :]


def multiply(left, high, low, outs, columns):
    right = jnp.concatenate([high, high, low], axis=0)
    result = jnp.dot(left, right, preferred_element_type=jnp.float32)
    part = result.shape[0] // len(outs)
    for chunk, out_ref in enumerate(outs):
        out_ref[:, columns] = result[chunk * part:(chunk + 1) * part]


def other_kernel(core_ref, rows_ref, columns_hbm, *refs):
    outs, (high_ref, low_ref, columns_ref, sems) = refs[:-4], refs[-4:]
    steps, _, block = columns_ref.shape

    def load(i):
        return pltpu.make_async_copy(
            columns_hbm.at[:, i * block:(i + 1) * block], columns_ref.at[i], sems.at[i]
        )

    for i in range(steps):
        load(i).start()
    left = rows_of(core_ref, rows_ref)
    for i in range(steps):
        load(i).wait()
        columns = slice(i * block, (i + 1) * block)
        high, low = split(columns_ref[i])
        high_ref[:, columns] = high
        low_ref[:, columns] = low
        multiply(left, high, low, outs, columns)


def mine_kernel(core_ref, rows_ref, high_ref, low_ref, *outs):
    left = rows_of(core_ref, rows_ref)
    width = high_ref.shape[1]
    block = min(512, width)
    for i in range(width // block):
        columns = slice(i * block, (i + 1) * block)
        multiply(left, high_ref[:, columns], low_ref[:, columns], outs, columns)


def product(core, rows, columns, kernel, vmem):
    nrows = rows.shape[0]
    depth, width = columns[0].shape
    block = min(512, width)
    part = nrows // CORES // CHUNKS
    out = [jax.ShapeDtypeStruct((part, width), jnp.float32)] * CHUNKS
    in_vmem = pl.BlockSpec(memory_space=pltpu.VMEM)
    operand, scratch = in_vmem, []
    if kernel is other_kernel:
        out = out + [jax.ShapeDtypeStruct((depth, width), jnp.bfloat16)] * 2
        operand = pl.BlockSpec(memory_space=pltpu.HBM)
        scratch = [
            pltpu.VMEM((width // block, depth, block), jnp.float32),
            pltpu.SemaphoreType.DMA((width // block,)),
        ]
    return pl.pallas_call(
        kernel,
        in_specs=[pl.BlockSpec(memory_space=pltpu.SMEM), in_vmem] + [operand] * len(columns),
        out_specs=[in_vmem] * len(out),
        out_shape=out,
        scratch_shapes=scratch,
        compiler_params=pltpu.CompilerParams(vmem_limit_bytes=vmem * 1024 * 1024),
        cost_estimate=pl.CostEstimate(
            flops=3 * nrows * depth * width,
            bytes_accessed=4 * width * depth + 2 * width * nrows,
            transcendentals=0,
        ),
    )(core.reshape(1), rows, *columns)


def order_kernel(slots_ref, *refs):
    raws, out_ref = refs[:-1], refs[-1]
    nblocks = slots_ref.shape[0]
    groups = len(raws) // CHUNKS
    for slot in range(nblocks):
        for i, raw_ref in enumerate(raws):
            examples, width = raw_ref.shape[0] // nblocks, raw_ref.shape[1]
            chunk, group = divmod(i, groups)
            rows = pl.ds(slots_ref[slot], examples, stride=nblocks)
            out_ref[
                slot, group * examples:(group + 1) * examples, chunk * width:(chunk + 1) * width
            ] = raw_ref[rows, :].astype(out_ref.dtype)


def in_slot_order(raws, slots):
    nblocks = slots.shape[0]
    rows, width = raws[0].shape
    groups = len(raws) // CHUNKS
    return pl.pallas_call(
        order_kernel,
        in_specs=[pl.BlockSpec(memory_space=pltpu.SMEM)] + [pl.BlockSpec(memory_space=pltpu.VMEM)] * len(raws),
        out_specs=pl.BlockSpec(memory_space=pltpu.VMEM),
        out_shape=jax.ShapeDtypeStruct((nblocks, groups * rows // nblocks, CHUNKS * width), jnp.bfloat16),
        compiler_params=pltpu.CompilerParams(vmem_limit_bytes=4 * 1024 * 1024),
        cost_estimate=pl.CostEstimate(
            flops=rows * width, bytes_accessed=6 * len(raws) * rows * width, transcendentals=0
        ),
    )(slots, *raws)


def finish_kernel(got_ref, allowed_ref, out_ref):
    n, owned, quad, examples, half = got_ref.shape
    parts = half // LANES
    per_row = owned * CORES * parts
    for device in range(n):
        for core in range(CORES):
            sources = [(device & ~3) | (y << 1) | core for y in range(quad // CORES)]
            for slot in range(owned):
                scores = sum(got_ref[s, slot, s ^ device].astype(jnp.float32) for s in sources)
                scores = scores * allowed_ref[slot:slot + 1, core * half:(core + 1) * half]
                for i in range(parts):
                    first = device * examples * per_row + (slot * CORES + core) * parts + i
                    out_ref[pl.ds(first, examples, stride=per_row), :] = scores[:, i * LANES:(i + 1) * LANES]


def finish(got, allowed):
    n, owned, _, examples, half = got.shape
    flat = pl.pallas_call(
        finish_kernel,
        out_shape=jax.ShapeDtypeStruct((n * examples * owned * CORES * half // LANES, LANES), jnp.float32),
        compiler_params=pltpu.CompilerParams(vmem_limit_bytes=4 * 1024 * 1024),
        cost_estimate=pl.CostEstimate(flops=got.size, bytes_accessed=4 * got.size, transcendentals=0),
    )(got, allowed)
    return flat.reshape(n * examples, owned, CORES * half)


def shards(queries, precond, train, query_cluster, cand_blocks, cand_count, slot_block):
    n = lax.axis_size("rows")
    chips = n // CORES
    bits = chips.bit_length() - 1
    ybit, zbit = 1, 1 + bits // 2
    rest = [bit for bit in range(1, 1 + bits) if bit not in (ybit, zbit)]
    me = lax.axis_index("rows")
    core = me & 1

    examples, nblocks, width = train.shape
    nq = queries.shape[0]

    def swap(value, bit):
        return lax.ppermute(value, "rows", [(r, r ^ (1 << bit)) for r in range(n)])

    rows = nq // CORES // CHUNKS // PATHS
    sizes = {(ybit, width // 2), (zbit, rows // 2)} | {(bit, rows >> (i + 2)) for i, bit in enumerate(rest[:-1])}
    offsets = {}
    first_half = {}
    for bit, size in sorted(sizes):
        side = (me >> bit) & 1
        offsets[bit, size] = (side * size, (1 - side) * size)
        first_half[bit] = side == 0
    owned = nblocks // n
    first_slot = me * owned
    scalars = (core, 1 - core, first_slot, offsets, first_half)
    scalars, queries, train = lax.optimization_barrier((scalars, queries, train))
    core, other_core, first_slot, offsets, first_half = scalars

    def pack(value):
        value = value * UNIT
        return (value * lax.rsqrt(jnp.abs(value) + LEAST)).astype(jnp.float16)

    def unpack(value):
        value = value.astype(jnp.float32)
        return value * jnp.abs(value) * (1.0 / UNIT)

    def part(value, bit, axis, other=0):
        shape = list(value.shape)
        shape[axis] //= 2
        starts = [0] * value.ndim
        starts[axis] = offsets[bit, shape[axis]][other]
        return lax.dynamic_slice(value, starts, shape, allow_negative_indices=False)

    def give(value, bit, axis):
        return pack(part(value, bit, axis, 1))

    def keep(value, got, bit, axis):
        return part(value, bit, axis) + unpack(got)

    def join(own, got, bit):
        mine_first = jnp.concatenate([own, got], axis=1)
        return jnp.where(first_half[bit], mine_first, jnp.concatenate([got, own], axis=1))

    def after(value, first):
        return lax.optimization_barrier((value, first))[0]

    def paths(value, other):
        value = value + unpack(other)
        return [value[i * rows:(i + 1) * rows] for i in range(PATHS)]

    levels = ((ybit, 1), (zbit, 0)), ((zbit, 0), (ybit, 1))

    def messages(values, step):
        return [give(value, *level[step]) for value, level in zip(values, levels)]

    def exchange(values, sent, step):
        got = [swap(message, level[step][0]) for message, level in zip(sent, levels)]
        return [keep(value, message, *level[step]) for value, message, level in zip(values, got, levels)]

    def halve(values):
        value = jnp.stack(values)
        for bit in rest[:-1]:
            value = keep(value, swap(give(value, bit, 1), bit), bit, 1)
        return value

    def gather(value, first=None):
        for bit in reversed([zbit] + rest[:-1]):
            got = swap(value, bit)
            if first is not None and bit == zbit:
                got = after(got, first)
            value = join(value, got, bit)
        return value.reshape(-1, value.shape[-1])

    def scores(group, value):
        return lax.dot_general(group, value, (((1,), (1,)), ((), ())), preferred_element_type=jnp.float32)

    blocks = train.reshape(examples * nblocks, width)
    total = examples * nblocks
    middle = max(1, examples * 3 // 8) * nblocks

    def features(blocks, first, count, other):
        start = offsets[ybit, width // 2][other]
        return lax.dynamic_slice(blocks, (first, start), (count, width // 2), allow_negative_indices=False)

    high = lax.reduce_precision(queries, 8, 7)
    low = (queries - high).astype(jnp.bfloat16)
    high = high.astype(jnp.bfloat16)
    left = jnp.concatenate([high, low, high], axis=1)
    blocks = after(blocks, left)
    early = features(blocks, 0, middle, 1)
    other_core, blocks = after((other_core, blocks), early)
    early = swap(early, ybit)

    *full, high, low = product(other_core, left, [precond], other_kernel, OTHER_VMEM)
    sent = [pack(value) for value in full]
    got = [swap(value, 0) for value in sent]
    blocks = after(blocks, sent)
    near = features(blocks, 0, total, 0)
    sibling = swap(near, 0)
    mine = product(after(core, sent), left, [high, low], mine_kernel, MINE_VMEM)
    one = paths(mine[0], got[0])
    sent = messages(one, 0)
    two = paths(mine[1], after(got[1], sent))
    one = exchange(one, sent, 0)
    sent = messages(one, 1)
    sent_two = after(messages(two, 0), (sent, sibling))
    one = halve(exchange(one, sent, 1))
    sent = pack(one)
    got_one = swap(sent, rest[-1])
    two = exchange(two, sent_two, 0)
    two = exchange(two, messages(two, 1), 1)
    two = halve(two)
    sent = pack(two)
    one = (after(one, sent) + unpack(got_one)).astype(jnp.bfloat16)
    got_two = swap(sent, rest[-1])
    blocks, early = after((blocks, early), one)
    late = swap(features(blocks, middle, total - middle, 1), ybit)
    one = gather(one)
    groups = [
        jnp.concatenate([near, sibling], axis=0),
        jnp.concatenate([early, late, swap(early, 0), swap(late, 0)], axis=0),
    ]
    raws = [scores(group, one) for group in groups]
    two = gather((two + unpack(got_two)).astype(jnp.bfloat16), raws)
    raws = raws + [scores(group, two) for group in groups]

    ordered = in_slot_order(raws, slot_block).reshape(n, owned, 2 * CORES * examples, nq // CORES)
    got = lax.all_to_all(ordered, "rows", split_axis=0, concat_axis=0, tiled=True)

    lists = (query_cluster, cand_blocks, cand_count, slot_block, first_slot)
    query_cluster, cand_blocks, cand_count, slot_block, first_slot = after(lists, ordered)
    allowed = listed_mask(query_cluster, cand_blocks, cand_count, nblocks)
    slots = lax.dynamic_slice(slot_block, (first_slot,), (owned,), allow_negative_indices=False)
    own_allowed = jnp.take(allowed, slots, axis=0, mode="clip")
    return finish(got.reshape(n, owned, 2 * CORES, examples, nq // CORES), own_allowed)


def solution(mesh):
    placed = (
        P("groups", "rows"),
        P("rows", None),
        P("rows", "groups", None),
        P("groups"),
        P("groups", None),
        P("groups"),
        P("groups"),
    )
    return jax.shard_map(
        shards,
        mesh=mesh,
        in_specs=placed,
        out_specs=P(None, ("groups", "rows"), None),
        check_vma=False,
    )
```

```python
import jax
import jax.numpy as jnp
from jax import lax
from jax.experimental import pallas as pl
from jax.experimental.pallas import tpu as pltpu
from jax.sharding import PartitionSpec as P

CORES = 2
CHUNKS = 2
PATHS = 2
UNIT = 2.0 ** 18
LEAST = 2.0 ** -100
LANES = 128
OTHER_VMEM = 44
MINE_VMEM = 16


def listed_mask(query_cluster, cand_blocks, cand_count, nblocks):
    nclusters = cand_blocks.shape[0]
    valid = jnp.arange(cand_blocks.shape[1])[None, :] < cand_count[:, None]
    hits = (cand_blocks[:, :, None] == jnp.arange(nblocks)[None, None, :]) & valid[:, :, None]
    listed = jnp.any(hits, axis=1).astype(jnp.float32)
    onehot = (query_cluster[:, None] == jnp.arange(nclusters)[None, :]).astype(jnp.float32)
    return jnp.dot(listed.T, onehot.T, preferred_element_type=jnp.float32)


def split(value):
    high = value.astype(jnp.bfloat16)
    return high, (value - high.astype(jnp.float32)).astype(jnp.bfloat16)


def rows_of(core_ref, rows_ref):
    half = rows_ref.shape[0] // CORES
    return rows_ref[pl.ds(pl.multiple_of(core_ref[0] * half, half), half), :]


def multiply(left, high, low, outs, columns):
    right = jnp.concatenate([high, high, low], axis=0)
    result = jnp.dot(left, right, preferred_element_type=jnp.float32)
    part = result.shape[0] // len(outs)
    for chunk, out_ref in enumerate(outs):
        out_ref[:, columns] = result[chunk * part:(chunk + 1) * part]


def other_kernel(core_ref, rows_ref, columns_hbm, *refs):
    outs, (high_ref, low_ref, columns_ref, sems) = refs[:-4], refs[-4:]
    steps, _, block = columns_ref.shape

    def load(i):
        return pltpu.make_async_copy(
            columns_hbm.at[:, i * block:(i + 1) * block], columns_ref.at[i], sems.at[i]
        )

    for i in range(steps):
        load(i).start()
    left = rows_of(core_ref, rows_ref)
    for i in range(steps):
        load(i).wait()
        columns = slice(i * block, (i + 1) * block)
        high, low = split(columns_ref[i])
        high_ref[:, columns] = high
        low_ref[:, columns] = low
        multiply(left, high, low, outs, columns)


def mine_kernel(core_ref, rows_ref, high_ref, low_ref, *outs):
    left = rows_of(core_ref, rows_ref)
    width = high_ref.shape[1]
    block = min(512, width)
    for i in range(width // block):
        columns = slice(i * block, (i + 1) * block)
        multiply(left, high_ref[:, columns], low_ref[:, columns], outs, columns)


def product(core, rows, columns, kernel, vmem):
    nrows = rows.shape[0]
    depth, width = columns[0].shape
    block = min(512, width)
    part = nrows // CORES // CHUNKS
    out = [jax.ShapeDtypeStruct((part, width), jnp.float32)] * CHUNKS
    in_vmem = pl.BlockSpec(memory_space=pltpu.VMEM)
    operand, scratch = in_vmem, []
    if kernel is other_kernel:
        out = out + [jax.ShapeDtypeStruct((depth, width), jnp.bfloat16)] * 2
        operand = pl.BlockSpec(memory_space=pltpu.HBM)
        scratch = [
            pltpu.VMEM((width // block, depth, block), jnp.float32),
            pltpu.SemaphoreType.DMA((width // block,)),
        ]
    return pl.pallas_call(
        kernel,
        in_specs=[pl.BlockSpec(memory_space=pltpu.SMEM), in_vmem] + [operand] * len(columns),
        out_specs=[in_vmem] * len(out),
        out_shape=out,
        scratch_shapes=scratch,
        compiler_params=pltpu.CompilerParams(vmem_limit_bytes=vmem * 1024 * 1024),
        cost_estimate=pl.CostEstimate(
            flops=3 * nrows * depth * width,
            bytes_accessed=4 * width * depth + 2 * width * nrows,
            transcendentals=0,
        ),
    )(core.reshape(1), rows, *columns)


def order_kernel(slots_ref, *refs):
    raws, out_ref = refs[:-1], refs[-1]
    nblocks = slots_ref.shape[0]
    groups = len(raws) // CHUNKS
    for slot in range(nblocks):
        for i, raw_ref in enumerate(raws):
            examples, width = raw_ref.shape[0] // nblocks, raw_ref.shape[1]
            chunk, group = divmod(i, groups)
            rows = pl.ds(slots_ref[slot], examples, stride=nblocks)
            out_ref[
                slot, group * examples:(group + 1) * examples, chunk * width:(chunk + 1) * width
            ] = raw_ref[rows, :].astype(out_ref.dtype)


def in_slot_order(raws, slots):
    nblocks = slots.shape[0]
    rows, width = raws[0].shape
    groups = len(raws) // CHUNKS
    return pl.pallas_call(
        order_kernel,
        in_specs=[pl.BlockSpec(memory_space=pltpu.SMEM)] + [pl.BlockSpec(memory_space=pltpu.VMEM)] * len(raws),
        out_specs=pl.BlockSpec(memory_space=pltpu.VMEM),
        out_shape=jax.ShapeDtypeStruct((nblocks, groups * rows // nblocks, CHUNKS * width), jnp.bfloat16),
        compiler_params=pltpu.CompilerParams(vmem_limit_bytes=4 * 1024 * 1024),
        cost_estimate=pl.CostEstimate(
            flops=rows * width, bytes_accessed=6 * len(raws) * rows * width, transcendentals=0
        ),
    )(slots, *raws)


def finish_kernel(got_ref, allowed_ref, out_ref):
    n, owned, quad, examples, half = got_ref.shape
    parts = half // LANES
    per_row = owned * CORES * parts
    for device in range(n):
        for core in range(CORES):
            sources = [(device & ~3) | (y << 1) | core for y in range(quad // CORES)]
            for slot in range(owned):
                scores = sum(got_ref[s, slot, s ^ device].astype(jnp.float32) for s in sources)
                scores = scores * allowed_ref[slot:slot + 1, core * half:(core + 1) * half]
                for i in range(parts):
                    first = device * examples * per_row + (slot * CORES + core) * parts + i
                    out_ref[pl.ds(first, examples, stride=per_row), :] = scores[:, i * LANES:(i + 1) * LANES]


def finish(got, allowed):
    n, owned, _, examples, half = got.shape
    flat = pl.pallas_call(
        finish_kernel,
        out_shape=jax.ShapeDtypeStruct((n * examples * owned * CORES * half // LANES, LANES), jnp.float32),
        compiler_params=pltpu.CompilerParams(vmem_limit_bytes=4 * 1024 * 1024),
        cost_estimate=pl.CostEstimate(flops=got.size, bytes_accessed=4 * got.size, transcendentals=0),
    )(got, allowed)
    return flat.reshape(n * examples, owned, CORES * half)


def shards(queries, precond, train, query_cluster, cand_blocks, cand_count, slot_block):
    n = lax.axis_size("rows")
    chips = n // CORES
    bits = chips.bit_length() - 1
    ybit, zbit = 1, 1 + bits // 2
    rest = [bit for bit in range(1, 1 + bits) if bit not in (ybit, zbit)]
    me = lax.axis_index("rows")
    core = me & 1

    examples, nblocks, width = train.shape
    nq = queries.shape[0]

    def swap(value, bit):
        return lax.ppermute(value, "rows", [(r, r ^ (1 << bit)) for r in range(n)])

    rows = nq // CORES // CHUNKS // PATHS
    sizes = {(ybit, width // 2), (zbit, rows // 2)} | {(bit, rows >> (i + 2)) for i, bit in enumerate(rest[:-1])}
    offsets = {}
    first_half = {}
    for bit, size in sorted(sizes):
        side = (me >> bit) & 1
        offsets[bit, size] = (side * size, (1 - side) * size)
        first_half[bit] = side == 0
    owned = nblocks // n
    first_slot = me * owned
    scalars = (core, 1 - core, first_slot, offsets, first_half)
    scalars, queries, train = lax.optimization_barrier((scalars, queries, train))
    core, other_core, first_slot, offsets, first_half = scalars

    def pack(value):
        value = value * UNIT
        return (value * lax.rsqrt(jnp.abs(value) + LEAST)).astype(jnp.float16)

    def unpack(value):
        value = value.astype(jnp.float32)
        return value * jnp.abs(value) * (1.0 / UNIT)

    def part(value, bit, axis, other=0):
        shape = list(value.shape)
        shape[axis] //= 2
        starts = [0] * value.ndim
        starts[axis] = offsets[bit, shape[axis]][other]
        return lax.dynamic_slice(value, starts, shape, allow_negative_indices=False)

    def give(value, bit, axis):
        return pack(part(value, bit, axis, 1))

    def keep(value, got, bit, axis):
        return part(value, bit, axis) + unpack(got)

    def join(own, got, bit):
        mine_first = jnp.concatenate([own, got], axis=1)
        return jnp.where(first_half[bit], mine_first, jnp.concatenate([got, own], axis=1))

    def after(value, first):
        return lax.optimization_barrier((value, first))[0]

    def paths(value, other):
        value = value + unpack(other)
        return [value[i * rows:(i + 1) * rows] for i in range(PATHS)]

    levels = ((ybit, 1), (zbit, 0)), ((zbit, 0), (ybit, 1))

    def messages(values, step):
        return [give(value, *level[step]) for value, level in zip(values, levels)]

    def exchange(values, sent, step):
        got = [swap(message, level[step][0]) for message, level in zip(sent, levels)]
        return [keep(value, message, *level[step]) for value, message, level in zip(values, got, levels)]

    def halve(values):
        value = jnp.stack(values)
        for bit in rest[:-1]:
            value = keep(value, swap(give(value, bit, 1), bit), bit, 1)
        return value

    def gather(value, first=None):
        for bit in reversed([zbit] + rest[:-1]):
            got = swap(value, bit)
            if first is not None and bit == zbit:
                got = after(got, first)
            value = join(value, got, bit)
        return value.reshape(-1, value.shape[-1])

    def scores(group, value):
        return lax.dot_general(group, value, (((1,), (1,)), ((), ())), preferred_element_type=jnp.float32)

    blocks = train.reshape(examples * nblocks, width)
    every = examples * nblocks
    middle = max(1, examples * 3 // 8) * nblocks

    def features(blocks, first, count, other):
        start = offsets[ybit, width // 2][other]
        return lax.dynamic_slice(blocks, (first, start), (count, width // 2), allow_negative_indices=False)

    high = lax.reduce_precision(queries, 8, 7)
    low = (queries - high).astype(jnp.bfloat16)
    high = high.astype(jnp.bfloat16)
    left = jnp.concatenate([high, low, high], axis=1)
    blocks = after(blocks, left)
    early = features(blocks, 0, middle, 1)
    other_core, blocks = after((other_core, blocks), early)
    early = swap(early, ybit)

    *full, high, low = product(other_core, left, [precond], other_kernel, OTHER_VMEM)
    sent = [pack(value) for value in full]
    got = [swap(value, 0) for value in sent]
    blocks = after(blocks, sent)
    near = features(blocks, 0, every, 0)
    sibling = swap(near, 0)
    mine = product(after(core, sent), left, [high, low], mine_kernel, MINE_VMEM)
    one = paths(mine[0], got[0])
    sent = messages(one, 0)
    two = paths(mine[1], after(got[1], sent))
    one = exchange(one, sent, 0)
    sent = messages(one, 1)
    sent_two = after(messages(two, 0), (sent, sibling))
    one = halve(exchange(one, sent, 1))
    sent = pack(one)
    got_one = swap(sent, rest[-1])
    two = exchange(two, sent_two, 0)
    two = exchange(two, messages(two, 1), 1)
    late = swap(features(after(blocks, two[0]), middle, every - middle, 1), ybit)
    two = halve(two)
    sent = pack(two)
    one = (after(one, sent) + unpack(got_one)).astype(jnp.bfloat16)
    got_two = swap(sent, rest[-1])
    early = after(early, one)
    one = gather(one)
    groups = [
        jnp.concatenate([near, sibling], axis=0),
        jnp.concatenate([early, late, swap(early, 0), swap(late, 0)], axis=0),
    ]
    raws = [scores(group, one) for group in groups]
    two = gather((two + unpack(got_two)).astype(jnp.bfloat16), raws)
    raws = raws + [scores(group, two) for group in groups]

    ordered = in_slot_order(raws, slot_block).reshape(n, owned, 2 * CORES * examples, nq // CORES)
    got = lax.all_to_all(ordered, "rows", split_axis=0, concat_axis=0, tiled=True)

    lists = (query_cluster, cand_blocks, cand_count, slot_block, first_slot)
    query_cluster, cand_blocks, cand_count, slot_block, first_slot = after(lists, ordered)
    allowed = listed_mask(query_cluster, cand_blocks, cand_count, nblocks)
    slots = lax.dynamic_slice(slot_block, (first_slot,), (owned,), allow_negative_indices=False)
    own_allowed = jnp.take(allowed, slots, axis=0, mode="clip")
    return finish(got.reshape(n, owned, 2 * CORES, examples, nq // CORES), own_allowed)


def solution(mesh):
    placed = (
        P("groups", "rows"),
        P("rows", None),
        P("rows", "groups", None),
        P("groups"),
        P("groups", None),
        P("groups"),
        P("groups"),
    )
    return jax.shard_map(
        shards,
        mesh=mesh,
        in_specs=placed,
        out_specs=P(None, ("groups", "rows"), None),
        check_vma=False,
    )
```

```python
import jax
import jax.numpy as jnp
from jax import lax
from jax.experimental import pallas as pl
from jax.experimental.pallas import tpu as pltpu
from jax.sharding import PartitionSpec as P

CORES = 2
CHUNKS = 2
PATHS = 2
UNIT = 2.0 ** 18
LEAST = 2.0 ** -100
LANES = 128
OTHER_VMEM = 44
MINE_VMEM = 16


def listed_mask(query_cluster, cand_blocks, cand_count, nblocks):
    nclusters = cand_blocks.shape[0]
    valid = jnp.arange(cand_blocks.shape[1])[None, :] < cand_count[:, None]
    hits = (cand_blocks[:, :, None] == jnp.arange(nblocks)[None, None, :]) & valid[:, :, None]
    listed = jnp.any(hits, axis=1).astype(jnp.float32)
    onehot = (query_cluster[:, None] == jnp.arange(nclusters)[None, :]).astype(jnp.float32)
    return jnp.dot(listed.T, onehot.T, preferred_element_type=jnp.float32)


def split(value):
    high = value.astype(jnp.bfloat16)
    return high, (value - high.astype(jnp.float32)).astype(jnp.bfloat16)


def rows_of(core_ref, rows_ref):
    half = rows_ref.shape[0] // CORES
    return rows_ref[pl.ds(pl.multiple_of(core_ref[0] * half, half), half), :]


def multiply(left, high, low, outs, columns):
    right = jnp.concatenate([high, high, low], axis=0)
    result = jnp.dot(left, right, preferred_element_type=jnp.float32)
    part = result.shape[0] // len(outs)
    for chunk, out_ref in enumerate(outs):
        out_ref[:, columns] = result[chunk * part:(chunk + 1) * part]


def other_kernel(core_ref, rows_ref, columns_hbm, *refs):
    outs, (high_ref, low_ref, columns_ref, sems) = refs[:-4], refs[-4:]
    steps, _, block = columns_ref.shape

    def load(i):
        return pltpu.make_async_copy(
            columns_hbm.at[:, i * block:(i + 1) * block], columns_ref.at[i], sems.at[i]
        )

    for i in range(steps):
        load(i).start()
    left = rows_of(core_ref, rows_ref)
    for i in range(steps):
        load(i).wait()
        columns = slice(i * block, (i + 1) * block)
        high, low = split(columns_ref[i])
        high_ref[:, columns] = high
        low_ref[:, columns] = low
        multiply(left, high, low, outs, columns)


def mine_kernel(core_ref, rows_ref, high_ref, low_ref, *outs):
    left = rows_of(core_ref, rows_ref)
    width = high_ref.shape[1]
    block = min(512, width)
    for i in range(width // block):
        columns = slice(i * block, (i + 1) * block)
        multiply(left, high_ref[:, columns], low_ref[:, columns], outs, columns)


def product(core, rows, columns, kernel, vmem, pieces):
    nrows = rows.shape[0]
    depth, width = columns[0].shape
    block = min(512, width)
    out = [jax.ShapeDtypeStruct((nrows // CORES // pieces, width), jnp.float32)] * pieces
    in_vmem = pl.BlockSpec(memory_space=pltpu.VMEM)
    operand, scratch = in_vmem, []
    if kernel is other_kernel:
        out = out + [jax.ShapeDtypeStruct((depth, width), jnp.bfloat16)] * 2
        operand = pl.BlockSpec(memory_space=pltpu.HBM)
        scratch = [
            pltpu.VMEM((width // block, depth, block), jnp.float32),
            pltpu.SemaphoreType.DMA((width // block,)),
        ]
    return pl.pallas_call(
        kernel,
        in_specs=[pl.BlockSpec(memory_space=pltpu.SMEM), in_vmem] + [operand] * len(columns),
        out_specs=[in_vmem] * len(out),
        out_shape=out,
        scratch_shapes=scratch,
        compiler_params=pltpu.CompilerParams(vmem_limit_bytes=vmem * 1024 * 1024),
        cost_estimate=pl.CostEstimate(
            flops=3 * nrows * depth * width,
            bytes_accessed=4 * width * depth + 2 * width * nrows,
            transcendentals=0,
        ),
    )(core.reshape(1), rows, *columns)


def order_kernel(slots_ref, *refs):
    raws, (out_hbm, staged_ref, sems) = refs[:-3], refs[-3:]
    nblocks = slots_ref.shape[0]
    groups = len(raws) // CHUNKS
    parts = sems.shape[0]
    size = nblocks // parts

    def send(part):
        slots = pl.ds(part * size, size)
        return pltpu.make_async_copy(staged_ref.at[slots], out_hbm.at[slots], sems.at[part])

    for part in range(parts):
        for slot in range(part * size, (part + 1) * size):
            for i, raw_ref in enumerate(raws):
                examples, width = raw_ref.shape[0] // nblocks, raw_ref.shape[1]
                chunk, group = divmod(i, groups)
                rows = pl.ds(slots_ref[slot], examples, stride=nblocks)
                staged_ref[
                    slot, group * examples:(group + 1) * examples, chunk * width:(chunk + 1) * width
                ] = raw_ref[rows, :].astype(staged_ref.dtype)
        send(part).start()
    for part in range(parts):
        send(part).wait()


def in_slot_order(raws, slots):
    nblocks = slots.shape[0]
    rows, width = raws[0].shape
    groups = len(raws) // CHUNKS
    shape = (nblocks, groups * rows // nblocks, CHUNKS * width)
    return pl.pallas_call(
        order_kernel,
        in_specs=[pl.BlockSpec(memory_space=pltpu.SMEM)] + [pl.BlockSpec(memory_space=pltpu.VMEM)] * len(raws),
        out_specs=pl.BlockSpec(memory_space=pltpu.HBM),
        out_shape=jax.ShapeDtypeStruct(shape, jnp.bfloat16),
        scratch_shapes=[pltpu.VMEM(shape, jnp.bfloat16), pltpu.SemaphoreType.DMA((4,))],
        compiler_params=pltpu.CompilerParams(vmem_limit_bytes=4 * 1024 * 1024),
        cost_estimate=pl.CostEstimate(
            flops=rows * width, bytes_accessed=6 * len(raws) * rows * width, transcendentals=0
        ),
    )(slots, *raws)


def finish_kernel(got_ref, allowed_ref, out_ref):
    n, owned, quad, examples, half = got_ref.shape
    parts = half // LANES
    per_row = owned * CORES * parts
    for device in range(n):
        for core in range(CORES):
            sources = [(device & ~3) | (y << 1) | core for y in range(quad // CORES)]
            for slot in range(owned):
                scores = sum(got_ref[s, slot, s ^ device].astype(jnp.float32) for s in sources)
                scores = scores * allowed_ref[slot:slot + 1, core * half:(core + 1) * half]
                for i in range(parts):
                    first = device * examples * per_row + (slot * CORES + core) * parts + i
                    out_ref[pl.ds(first, examples, stride=per_row), :] = scores[:, i * LANES:(i + 1) * LANES]


def finish(got, allowed):
    n, owned, _, examples, half = got.shape
    flat = pl.pallas_call(
        finish_kernel,
        out_shape=jax.ShapeDtypeStruct((n * examples * owned * CORES * half // LANES, LANES), jnp.float32),
        compiler_params=pltpu.CompilerParams(vmem_limit_bytes=4 * 1024 * 1024),
        cost_estimate=pl.CostEstimate(flops=got.size, bytes_accessed=4 * got.size, transcendentals=0),
    )(got, allowed)
    return flat.reshape(n * examples, owned, CORES * half)


def shards(queries, precond, train, query_cluster, cand_blocks, cand_count, slot_block):
    n = lax.axis_size("rows")
    chips = n // CORES
    bits = chips.bit_length() - 1
    ybit, zbit = 1, 1 + bits // 2
    rest = [bit for bit in range(1, 1 + bits) if bit not in (ybit, zbit)]
    me = lax.axis_index("rows")
    core = me & 1

    examples, nblocks, width = train.shape
    nq = queries.shape[0]

    def swap(value, bit):
        return lax.ppermute(value, "rows", [(r, r ^ (1 << bit)) for r in range(n)])

    rows = nq // CORES // CHUNKS // PATHS
    sizes = {(ybit, width // 2), (zbit, rows // 2)} | {(bit, rows >> (i + 2)) for i, bit in enumerate(rest[:-1])}
    offsets = {}
    first_half = {}
    for bit, size in sorted(sizes):
        side = (me >> bit) & 1
        offsets[bit, size] = (side * size, (1 - side) * size)
        first_half[bit] = side == 0
    owned = nblocks // n
    first_slot = me * owned
    scalars = (core, 1 - core, first_slot, offsets, first_half)
    scalars, queries, train = lax.optimization_barrier((scalars, queries, train))
    core, other_core, first_slot, offsets, first_half = scalars

    def pack(value):
        value = value * UNIT
        return (value * lax.rsqrt(jnp.abs(value) + LEAST)).astype(jnp.float16)

    def unpack(value):
        value = value.astype(jnp.float32)
        return value * jnp.abs(value) * (1.0 / UNIT)

    def part(value, bit, axis, other=0):
        shape = list(value.shape)
        shape[axis] //= 2
        starts = [0] * value.ndim
        starts[axis] = offsets[bit, shape[axis]][other]
        return lax.dynamic_slice(value, starts, shape, allow_negative_indices=False)

    def give(value, bit, axis):
        return pack(part(value, bit, axis, 1))

    def keep(value, got, bit, axis):
        return part(value, bit, axis) + unpack(got)

    def join(own, got, bit):
        mine_first = jnp.concatenate([own, got], axis=1)
        return jnp.where(first_half[bit], mine_first, jnp.concatenate([got, own], axis=1))

    def after(value, first):
        return lax.optimization_barrier((value, first))[0]

    def paths(values, other):
        return [value + unpack(other[i * rows:(i + 1) * rows]) for i, value in enumerate(values)]

    levels = ((ybit, 1), (zbit, 0)), ((zbit, 0), (ybit, 1))

    def messages(values, step):
        return [give(value, *level[step]) for value, level in zip(values, levels)]

    def exchange(values, sent, step):
        got = [swap(message, level[step][0]) for message, level in zip(sent, levels)]
        return [keep(value, message, *level[step]) for value, message, level in zip(values, got, levels)]

    def halve(values):
        value = jnp.stack(values)
        for bit in rest[:-1]:
            value = keep(value, swap(give(value, bit, 1), bit), bit, 1)
        return value

    def gather(value, first=None):
        for bit in reversed([zbit] + rest[:-1]):
            got = swap(value, bit)
            if first is not None and bit == zbit:
                got = after(got, first)
            value = join(value, got, bit)
        return value.reshape(-1, value.shape[-1])

    def scores(group, value):
        return lax.dot_general(group, value, (((1,), (1,)), ((), ())), preferred_element_type=jnp.float32)

    blocks = train.reshape(examples * nblocks, width)
    every = examples * nblocks
    middle = max(1, examples * 3 // 8) * nblocks

    def features(blocks, first, count, other):
        start = offsets[ybit, width // 2][other]
        return lax.dynamic_slice(blocks, (first, start), (count, width // 2), allow_negative_indices=False)

    high = lax.reduce_precision(queries, 8, 7)
    low = (queries - high).astype(jnp.bfloat16)
    high = high.astype(jnp.bfloat16)
    left = jnp.concatenate([high, low, high], axis=1)
    blocks = after(blocks, left)
    early = features(blocks, 0, middle, 1)
    other_core, blocks = after((other_core, blocks), early)
    early = swap(early, ybit)

    *full, high, low = product(other_core, left, [precond], other_kernel, OTHER_VMEM, CHUNKS)
    sent = pack(full[0])
    got = swap(sent, 0)
    mine = product(after(core, sent), left, [high, low], mine_kernel, MINE_VMEM, CHUNKS * PATHS)
    one = paths(mine[:PATHS], got)
    sent = messages(one, 0)
    got = swap(pack(after(full[1], mine[0])), 0)
    two = paths(mine[PATHS:], after(got, sent))
    blocks = after(blocks, sent)
    near = features(blocks, 0, every, 0)
    sibling = swap(near, 0)
    one = exchange(one, sent, 0)
    sent = messages(one, 1)
    sent_two = after(messages(two, 0), (sent, early))
    one = halve(exchange(one, sent, 1))
    sent = pack(one)
    got_one = swap(sent, rest[-1])
    two = exchange(two, sent_two, 0)
    two = exchange(two, messages(two, 1), 1)
    late = swap(features(after(blocks, two[0]), middle, every - middle, 1), ybit)
    two = halve(two)
    sent = pack(two)
    one = (after(one, sent) + unpack(got_one)).astype(jnp.bfloat16)
    got_two = swap(sent, rest[-1])
    early = after(early, one)
    one = gather(one)
    groups = [
        jnp.concatenate([near, sibling], axis=0),
        jnp.concatenate([early, late, swap(early, 0), swap(late, 0)], axis=0),
    ]
    raws = [scores(group, one) for group in groups]
    two = gather((two + unpack(got_two)).astype(jnp.bfloat16), raws)
    raws = raws + [scores(group, two) for group in groups]

    ordered = in_slot_order(raws, slot_block).reshape(n, owned, 2 * CORES * examples, nq // CORES)
    got = lax.all_to_all(ordered, "rows", split_axis=0, concat_axis=0, tiled=True)

    lists = (query_cluster, cand_blocks, cand_count, slot_block, first_slot)
    query_cluster, cand_blocks, cand_count, slot_block, first_slot = after(lists, ordered)
    allowed = listed_mask(query_cluster, cand_blocks, cand_count, nblocks)
    slots = lax.dynamic_slice(slot_block, (first_slot,), (owned,), allow_negative_indices=False)
    own_allowed = jnp.take(allowed, slots, axis=0, mode="clip")
    return finish(got.reshape(n, owned, 2 * CORES, examples, nq // CORES), own_allowed)


def solution(mesh):
    placed = (
        P("groups", "rows"),
        P("rows", None),
        P("rows", "groups", None),
        P("groups"),
        P("groups", None),
        P("groups"),
        P("groups"),
    )
    return jax.shard_map(
        shards,
        mesh=mesh,
        in_specs=placed,
        out_specs=P(None, ("groups", "rows"), None),
        check_vma=False,
    )
```

```python
import jax
import jax.numpy as jnp
from jax import lax
from jax.experimental import pallas as pl
from jax.experimental.pallas import tpu as pltpu
from jax.sharding import PartitionSpec as P

CORES = 2
CHUNKS = 2
PATHS = 2
UNIT = 2.0 ** 18
LEAST = 2.0 ** -100
LANES = 128
OTHER_VMEM = 44
MINE_VMEM = 16


def listed_mask(query_cluster, cand_blocks, cand_count, nblocks):
    nclusters = cand_blocks.shape[0]
    valid = jnp.arange(cand_blocks.shape[1])[None, :] < cand_count[:, None]
    hits = (cand_blocks[:, :, None] == jnp.arange(nblocks)[None, None, :]) & valid[:, :, None]
    listed = jnp.any(hits, axis=1).astype(jnp.float32)
    onehot = (query_cluster[:, None] == jnp.arange(nclusters)[None, :]).astype(jnp.float32)
    return jnp.dot(listed.T, onehot.T, preferred_element_type=jnp.float32)


def split(value):
    high = value.astype(jnp.bfloat16)
    return high, (value - high.astype(jnp.float32)).astype(jnp.bfloat16)


def rows_of(core_ref, rows_ref):
    half = rows_ref.shape[0] // CORES
    return rows_ref[pl.ds(pl.multiple_of(core_ref[0] * half, half), half), :]


def multiply(left, high, low, outs, columns):
    right = jnp.concatenate([high, high, low], axis=0)
    result = jnp.dot(left, right, preferred_element_type=jnp.float32)
    part = result.shape[0] // len(outs)
    for chunk, out_ref in enumerate(outs):
        out_ref[:, columns] = result[chunk * part:(chunk + 1) * part]


def other_kernel(core_ref, rows_ref, columns_hbm, *refs):
    outs, (high_ref, low_ref, columns_ref, sems) = refs[:-4], refs[-4:]
    steps, _, block = columns_ref.shape

    def load(i):
        return pltpu.make_async_copy(
            columns_hbm.at[:, i * block:(i + 1) * block], columns_ref.at[i], sems.at[i]
        )

    for i in range(steps):
        load(i).start()
    left = rows_of(core_ref, rows_ref)
    for i in range(steps):
        load(i).wait()
        columns = slice(i * block, (i + 1) * block)
        high, low = split(columns_ref[i])
        high_ref[:, columns] = high
        low_ref[:, columns] = low
        multiply(left, high, low, outs, columns)


def mine_kernel(core_ref, rows_ref, high_ref, low_ref, *outs):
    left = rows_of(core_ref, rows_ref)
    width = high_ref.shape[1]
    block = min(512, width)
    for i in range(width // block):
        columns = slice(i * block, (i + 1) * block)
        multiply(left, high_ref[:, columns], low_ref[:, columns], outs, columns)


def product(core, rows, columns, kernel, vmem, pieces):
    nrows = rows.shape[0]
    depth, width = columns[0].shape
    block = min(512, width)
    out = [jax.ShapeDtypeStruct((nrows // CORES // pieces, width), jnp.float32)] * pieces
    in_vmem = pl.BlockSpec(memory_space=pltpu.VMEM)
    operand, scratch = in_vmem, []
    if kernel is other_kernel:
        out = out + [jax.ShapeDtypeStruct((depth, width), jnp.bfloat16)] * 2
        operand = pl.BlockSpec(memory_space=pltpu.HBM)
        scratch = [
            pltpu.VMEM((width // block, depth, block), jnp.float32),
            pltpu.SemaphoreType.DMA((width // block,)),
        ]
    return pl.pallas_call(
        kernel,
        in_specs=[pl.BlockSpec(memory_space=pltpu.SMEM), in_vmem] + [operand] * len(columns),
        out_specs=[in_vmem] * len(out),
        out_shape=out,
        scratch_shapes=scratch,
        compiler_params=pltpu.CompilerParams(vmem_limit_bytes=vmem * 1024 * 1024),
        cost_estimate=pl.CostEstimate(
            flops=3 * nrows * depth * width,
            bytes_accessed=4 * width * depth + 2 * width * nrows,
            transcendentals=0,
        ),
    )(core.reshape(1), rows, *columns)


def order_kernel(slots_ref, *refs):
    raws, (out_hbm, staged_ref, sems) = refs[:-3], refs[-3:]
    nblocks = slots_ref.shape[0]
    groups = len(raws) // CHUNKS
    parts = sems.shape[0]
    size = nblocks // parts

    def send(part):
        slots = pl.ds(part * size, size)
        return pltpu.make_async_copy(staged_ref.at[slots], out_hbm.at[slots], sems.at[part])

    for part in range(parts):
        for slot in range(part * size, (part + 1) * size):
            for i, raw_ref in enumerate(raws):
                examples, width = raw_ref.shape[0] // nblocks, raw_ref.shape[1]
                chunk, group = divmod(i, groups)
                rows = pl.ds(slots_ref[slot], examples, stride=nblocks)
                staged_ref[
                    slot, group * examples:(group + 1) * examples, chunk * width:(chunk + 1) * width
                ] = raw_ref[rows, :].astype(staged_ref.dtype)
        send(part).start()
    for part in range(parts):
        send(part).wait()


def in_slot_order(raws, slots):
    nblocks = slots.shape[0]
    rows, width = raws[0].shape
    groups = len(raws) // CHUNKS
    shape = (nblocks, groups * rows // nblocks, CHUNKS * width)
    return pl.pallas_call(
        order_kernel,
        in_specs=[pl.BlockSpec(memory_space=pltpu.SMEM)] + [pl.BlockSpec(memory_space=pltpu.VMEM)] * len(raws),
        out_specs=pl.BlockSpec(memory_space=pltpu.HBM),
        out_shape=jax.ShapeDtypeStruct(shape, jnp.bfloat16),
        scratch_shapes=[pltpu.VMEM(shape, jnp.bfloat16), pltpu.SemaphoreType.DMA((4,))],
        compiler_params=pltpu.CompilerParams(vmem_limit_bytes=4 * 1024 * 1024),
        cost_estimate=pl.CostEstimate(
            flops=rows * width, bytes_accessed=6 * len(raws) * rows * width, transcendentals=0
        ),
    )(slots, *raws)


def finish_kernel(got_ref, allowed_ref, out_ref):
    n, owned, quad, examples, half = got_ref.shape
    parts = half // LANES
    per_row = owned * CORES * parts
    for device in range(n):
        for core in range(CORES):
            sources = [(device & ~3) | (y << 1) | core for y in range(quad // CORES)]
            for slot in range(owned):
                scores = sum(got_ref[s, slot, s ^ device].astype(jnp.float32) for s in sources)
                scores = scores * allowed_ref[slot:slot + 1, core * half:(core + 1) * half]
                for i in range(parts):
                    first = device * examples * per_row + (slot * CORES + core) * parts + i
                    out_ref[pl.ds(first, examples, stride=per_row), :] = scores[:, i * LANES:(i + 1) * LANES]


def finish(got, allowed):
    n, owned, _, examples, half = got.shape
    flat = pl.pallas_call(
        finish_kernel,
        out_shape=jax.ShapeDtypeStruct((n * examples * owned * CORES * half // LANES, LANES), jnp.float32),
        compiler_params=pltpu.CompilerParams(vmem_limit_bytes=4 * 1024 * 1024),
        cost_estimate=pl.CostEstimate(flops=got.size, bytes_accessed=4 * got.size, transcendentals=0),
    )(got, allowed)
    return flat.reshape(n * examples, owned, CORES * half)


def shards(queries, precond, train, query_cluster, cand_blocks, cand_count, slot_block):
    n = lax.axis_size("rows")
    chips = n // CORES
    bits = chips.bit_length() - 1
    ybit, zbit = 1, 1 + bits // 2
    rest = [bit for bit in range(1, 1 + bits) if bit not in (ybit, zbit)]
    me = lax.axis_index("rows")
    core = me & 1

    examples, nblocks, width = train.shape
    nq = queries.shape[0]

    def swap(value, bit):
        return lax.ppermute(value, "rows", [(r, r ^ (1 << bit)) for r in range(n)])

    rows = nq // CORES // CHUNKS // PATHS
    sizes = {(ybit, width // 2), (zbit, rows // 2)} | {(bit, rows >> (i + 2)) for i, bit in enumerate(rest[:-1])}
    offsets = {}
    first_half = {}
    for bit, size in sorted(sizes):
        side = (me >> bit) & 1
        offsets[bit, size] = (side * size, (1 - side) * size)
        first_half[bit] = side == 0
    owned = nblocks // n
    first_slot = me * owned
    scalars = (core, 1 - core, first_slot, offsets, first_half)
    scalars, queries, train = lax.optimization_barrier((scalars, queries, train))
    core, other_core, first_slot, offsets, first_half = scalars

    def pack(value):
        value = value * UNIT
        return (value * lax.rsqrt(jnp.abs(value) + LEAST)).astype(jnp.float16)

    def unpack(value):
        value = value.astype(jnp.float32)
        return value * jnp.abs(value) * (1.0 / UNIT)

    def part(value, bit, axis, other=0):
        shape = list(value.shape)
        shape[axis] //= 2
        starts = [0] * value.ndim
        starts[axis] = offsets[bit, shape[axis]][other]
        return lax.dynamic_slice(value, starts, shape, allow_negative_indices=False)

    def give(value, bit, axis):
        return pack(part(value, bit, axis, 1))

    def keep(value, got, bit, axis):
        return part(value, bit, axis) + unpack(got)

    def join(own, got, bit):
        mine_first = jnp.concatenate([own, got], axis=1)
        return jnp.where(first_half[bit], mine_first, jnp.concatenate([got, own], axis=1))

    def after(value, first):
        return lax.optimization_barrier((value, first))[0]

    def paths(values, other):
        return [value + unpack(other[i * rows:(i + 1) * rows]) for i, value in enumerate(values)]

    levels = ((ybit, 1), (zbit, 0)), ((zbit, 0), (ybit, 1))

    def messages(values, step):
        return [give(value, *level[step]) for value, level in zip(values, levels)]

    def exchange(values, sent, step):
        got = [swap(message, level[step][0]) for message, level in zip(sent, levels)]
        return [keep(value, message, *level[step]) for value, message, level in zip(values, got, levels)]

    def halve(values):
        value = jnp.stack(values)
        for bit in rest[:-1]:
            value = keep(value, swap(give(value, bit, 1), bit), bit, 1)
        return value

    def gather(value, first=None):
        for bit in reversed([zbit] + rest[:-1]):
            got = swap(value, bit)
            if first is not None and bit == zbit:
                got = after(got, first)
            value = join(value, got, bit)
        return value.reshape(-1, value.shape[-1])

    def scores(group, value):
        return lax.dot_general(group, value, (((1,), (1,)), ((), ())), preferred_element_type=jnp.float32)

    blocks = train.reshape(examples * nblocks, width)
    every = examples * nblocks
    middle = max(1, examples * 7 // 16) * nblocks

    def features(blocks, first, count, other):
        start = offsets[ybit, width // 2][other]
        return lax.dynamic_slice(blocks, (first, start), (count, width // 2), allow_negative_indices=False)

    high = lax.reduce_precision(queries, 8, 7)
    low = (queries - high).astype(jnp.bfloat16)
    high = high.astype(jnp.bfloat16)
    left = jnp.concatenate([high, low, high], axis=1)
    blocks = after(blocks, left)
    early = features(blocks, 0, middle, 1)
    other_core, blocks = after((other_core, blocks), early)
    early = swap(early, ybit)

    *full, high, low = product(other_core, left, [precond], other_kernel, OTHER_VMEM, CHUNKS)
    sent = pack(full[0])
    got = swap(sent, 0)
    mine = product(after(core, sent), left, [high, low], mine_kernel, MINE_VMEM, CHUNKS * PATHS)
    one = paths(mine[:PATHS], got)
    sent = messages(one, 0)
    got = swap(pack(after(full[1], mine[0])), 0)
    two = paths(mine[PATHS:], after(got, sent))
    blocks = after(blocks, sent)
    near = features(blocks, 0, every, 0)
    sibling = swap(near, 0)
    one = exchange(one, sent, 0)
    sent = messages(one, 1)
    sent_two = after(messages(two, 0), (sent, early))
    one = halve(exchange(one, sent, 1))
    sent = pack(one)
    got_one = swap(sent, rest[-1])
    two = exchange(two, sent_two, 0)
    two = exchange(two, messages(two, 1), 1)
    late = swap(features(after(blocks, two[0]), middle, every - middle, 1), ybit)
    two = halve(two)
    sent = pack(two)
    one = (after(one, sent) + unpack(got_one)).astype(jnp.bfloat16)
    got_two = swap(sent, rest[-1])
    early = after(early, one)
    one = gather(one)
    groups = [
        jnp.concatenate([near, sibling], axis=0),
        jnp.concatenate([early, late, swap(early, 0), swap(late, 0)], axis=0),
    ]
    raws = [scores(group, one) for group in groups]
    two = gather((two + unpack(got_two)).astype(jnp.bfloat16), raws)
    raws = raws + [scores(group, two) for group in groups]

    ordered = in_slot_order(raws, slot_block).reshape(n, owned, 2 * CORES * examples, nq // CORES)
    got = lax.all_to_all(ordered, "rows", split_axis=0, concat_axis=0, tiled=True)

    lists = (query_cluster, cand_blocks, cand_count, slot_block, first_slot)
    query_cluster, cand_blocks, cand_count, slot_block, first_slot = after(lists, ordered)
    allowed = listed_mask(query_cluster, cand_blocks, cand_count, nblocks)
    slots = lax.dynamic_slice(slot_block, (first_slot,), (owned,), allow_negative_indices=False)
    own_allowed = jnp.take(allowed, slots, axis=0, mode="clip")
    return finish(got.reshape(n, owned, 2 * CORES, examples, nq // CORES), own_allowed)


def solution(mesh):
    placed = (
        P("groups", "rows"),
        P("rows", None),
        P("rows", "groups", None),
        P("groups"),
        P("groups", None),
        P("groups"),
        P("groups"),
    )
    return jax.shard_map(
        shards,
        mesh=mesh,
        in_specs=placed,
        out_specs=P(None, ("groups", "rows"), None),
        check_vma=False,
    )
```

```python
import jax
import jax.numpy as jnp
from jax import lax
from jax.experimental import pallas as pl
from jax.experimental.pallas import tpu as pltpu
from jax.sharding import PartitionSpec as P

CORES = 2
CHUNKS = 2
PATHS = 2
UNIT = 2.0 ** 18
LEAST = 2.0 ** -100
LANES = 128
OTHER_VMEM = 44
MINE_VMEM = 16


def listed_mask(query_cluster, cand_blocks, cand_count, nblocks):
    nclusters = cand_blocks.shape[0]
    valid = jnp.arange(cand_blocks.shape[1])[None, :] < cand_count[:, None]
    hits = (cand_blocks[:, :, None] == jnp.arange(nblocks)[None, None, :]) & valid[:, :, None]
    listed = jnp.any(hits, axis=1).astype(jnp.float32)
    onehot = (query_cluster[:, None] == jnp.arange(nclusters)[None, :]).astype(jnp.float32)
    return jnp.dot(listed.T, onehot.T, preferred_element_type=jnp.float32)


def split(value):
    high = value.astype(jnp.bfloat16)
    return high, (value - high.astype(jnp.float32)).astype(jnp.bfloat16)


def rows_of(core_ref, rows_ref):
    half = rows_ref.shape[0] // CORES
    return rows_ref[pl.ds(pl.multiple_of(core_ref[0] * half, half), half), :]


def multiply(left, high, low, outs, columns):
    right = jnp.concatenate([high, high, low], axis=0)
    result = jnp.dot(left, right, preferred_element_type=jnp.float32)
    part = result.shape[0] // len(outs)
    for chunk, out_ref in enumerate(outs):
        out_ref[:, columns] = result[chunk * part:(chunk + 1) * part]


def other_kernel(core_ref, rows_ref, columns_hbm, *refs):
    outs, (high_ref, low_ref, columns_ref, sems) = refs[:-4], refs[-4:]
    steps, _, block = columns_ref.shape

    def load(i):
        return pltpu.make_async_copy(
            columns_hbm.at[:, i * block:(i + 1) * block], columns_ref.at[i], sems.at[i]
        )

    for i in range(steps):
        load(i).start()
    left = rows_of(core_ref, rows_ref)
    for i in range(steps):
        load(i).wait()
        columns = slice(i * block, (i + 1) * block)
        high, low = split(columns_ref[i])
        high_ref[:, columns] = high
        low_ref[:, columns] = low
        multiply(left, high, low, outs, columns)


def mine_kernel(core_ref, rows_ref, high_ref, low_ref, *outs):
    left = rows_of(core_ref, rows_ref)
    width = high_ref.shape[1]
    block = min(512, width)
    for i in range(width // block):
        columns = slice(i * block, (i + 1) * block)
        multiply(left, high_ref[:, columns], low_ref[:, columns], outs, columns)


def product(core, rows, columns, kernel, vmem, pieces):
    nrows = rows.shape[0]
    depth, width = columns[0].shape
    block = min(512, width)
    out = [jax.ShapeDtypeStruct((nrows // CORES // pieces, width), jnp.float32)] * pieces
    in_vmem = pl.BlockSpec(memory_space=pltpu.VMEM)
    operand, scratch = in_vmem, []
    if kernel is other_kernel:
        out = out + [jax.ShapeDtypeStruct((depth, width), jnp.bfloat16)] * 2
        operand = pl.BlockSpec(memory_space=pltpu.HBM)
        scratch = [
            pltpu.VMEM((width // block, depth, block), jnp.float32),
            pltpu.SemaphoreType.DMA((width // block,)),
        ]
    return pl.pallas_call(
        kernel,
        in_specs=[pl.BlockSpec(memory_space=pltpu.SMEM), in_vmem] + [operand] * len(columns),
        out_specs=[in_vmem] * len(out),
        out_shape=out,
        scratch_shapes=scratch,
        compiler_params=pltpu.CompilerParams(vmem_limit_bytes=vmem * 1024 * 1024),
        cost_estimate=pl.CostEstimate(
            flops=3 * nrows * depth * width,
            bytes_accessed=4 * width * depth + 2 * width * nrows,
            transcendentals=0,
        ),
    )(core.reshape(1), rows, *columns)


def order_kernel(slots_ref, *refs):
    raws, (out_hbm, staged_ref, sems) = refs[:-3], refs[-3:]
    nblocks = slots_ref.shape[0]
    parts = sems.shape[0]
    size = nblocks // parts

    def send(part):
        slots = pl.ds(part * size, size)
        return pltpu.make_async_copy(staged_ref.at[slots], out_hbm.at[slots], sems.at[part])

    for part in range(parts):
        for slot in range(part * size, (part + 1) * size):
            for group, raw_ref in enumerate(raws):
                examples = raw_ref.shape[0] // nblocks
                rows = pl.ds(slots_ref[slot], examples, stride=nblocks)
                staged_ref[slot, group * examples:(group + 1) * examples, :] = (
                    raw_ref[rows, :].astype(staged_ref.dtype)
                )
        send(part).start()
    for part in range(parts):
        send(part).wait()


def in_slot_order(raws, slots):
    nblocks = slots.shape[0]
    rows, width = raws[0].shape
    shape = (nblocks, len(raws) * rows // nblocks, width)
    return pl.pallas_call(
        order_kernel,
        in_specs=[pl.BlockSpec(memory_space=pltpu.SMEM)] + [pl.BlockSpec(memory_space=pltpu.VMEM)] * len(raws),
        out_specs=pl.BlockSpec(memory_space=pltpu.HBM),
        out_shape=jax.ShapeDtypeStruct(shape, jnp.bfloat16),
        scratch_shapes=[pltpu.VMEM(shape, jnp.bfloat16), pltpu.SemaphoreType.DMA((4,))],
        compiler_params=pltpu.CompilerParams(vmem_limit_bytes=4 * 1024 * 1024),
        cost_estimate=pl.CostEstimate(
            flops=rows * width, bytes_accessed=6 * len(raws) * rows * width, transcendentals=0
        ),
    )(slots, *raws)


def finish_kernel(allowed_ref, *refs):
    got, out_ref = refs[:-1], refs[-1]
    n, owned, quad, examples, width = got[0].shape
    parts = width // LANES
    per_row = owned * CORES * len(got) * parts
    for device in range(n):
        for core in range(CORES):
            sources = [(device & ~3) | (y << 1) | core for y in range(quad // CORES)]
            for slot in range(owned):
                for chunk, got_ref in enumerate(got):
                    scores = sum(got_ref[s, slot, s ^ device].astype(jnp.float32) for s in sources)
                    for i in range(parts):
                        place = (core * len(got) + chunk) * parts + i
                        allowed = allowed_ref[slot:slot + 1, place * LANES:(place + 1) * LANES]
                        first = device * examples * per_row + slot * CORES * len(got) * parts + place
                        out_ref[pl.ds(first, examples, stride=per_row), :] = (
                            scores[:, i * LANES:(i + 1) * LANES] * allowed
                        )


def finish(got, allowed):
    n, owned, _, examples, width = got[0].shape
    nq = allowed.shape[1]
    flat = pl.pallas_call(
        finish_kernel,
        out_shape=jax.ShapeDtypeStruct((n * examples * owned * nq // LANES, LANES), jnp.float32),
        compiler_params=pltpu.CompilerParams(vmem_limit_bytes=4 * 1024 * 1024),
        cost_estimate=pl.CostEstimate(
            flops=len(got) * got[0].size, bytes_accessed=4 * len(got) * got[0].size, transcendentals=0
        ),
    )(allowed, *got)
    return flat.reshape(n * examples, owned, nq)


def shards(queries, precond, train, query_cluster, cand_blocks, cand_count, slot_block):
    n = lax.axis_size("rows")
    chips = n // CORES
    bits = chips.bit_length() - 1
    ybit, zbit = 1, 1 + bits // 2
    rest = [bit for bit in range(1, 1 + bits) if bit not in (ybit, zbit)]
    me = lax.axis_index("rows")
    core = me & 1

    examples, nblocks, width = train.shape
    nq = queries.shape[0]

    def swap(value, bit):
        return lax.ppermute(value, "rows", [(r, r ^ (1 << bit)) for r in range(n)])

    rows = nq // CORES // CHUNKS // PATHS
    sizes = {(ybit, width // 2), (zbit, rows // 2)} | {(bit, rows >> (i + 2)) for i, bit in enumerate(rest[:-1])}
    offsets = {}
    first_half = {}
    for bit, size in sorted(sizes):
        side = (me >> bit) & 1
        offsets[bit, size] = (side * size, (1 - side) * size)
        first_half[bit] = side == 0
    owned = nblocks // n
    first_slot = me * owned
    scalars = (core, 1 - core, first_slot, offsets, first_half)
    scalars, queries, train = lax.optimization_barrier((scalars, queries, train))
    core, other_core, first_slot, offsets, first_half = scalars

    def pack(value):
        value = value * UNIT
        return (value * lax.rsqrt(jnp.abs(value) + LEAST)).astype(jnp.float16)

    def unpack(value):
        value = value.astype(jnp.float32)
        return value * jnp.abs(value) * (1.0 / UNIT)

    def part(value, bit, axis, other=0):
        shape = list(value.shape)
        shape[axis] //= 2
        starts = [0] * value.ndim
        starts[axis] = offsets[bit, shape[axis]][other]
        return lax.dynamic_slice(value, starts, shape, allow_negative_indices=False)

    def give(value, bit, axis):
        return pack(part(value, bit, axis, 1))

    def keep(value, got, bit, axis):
        return part(value, bit, axis) + unpack(got)

    def join(own, got, bit):
        mine_first = jnp.concatenate([own, got], axis=1)
        return jnp.where(first_half[bit], mine_first, jnp.concatenate([got, own], axis=1))

    def after(value, first):
        return lax.optimization_barrier((value, first))[0]

    def paths(values, other):
        return [value + unpack(other[i * rows:(i + 1) * rows]) for i, value in enumerate(values)]

    levels = ((ybit, 1), (zbit, 0)), ((zbit, 0), (ybit, 1))

    def messages(values, step):
        return [give(value, *level[step]) for value, level in zip(values, levels)]

    def exchange(values, sent, step):
        got = [swap(message, level[step][0]) for message, level in zip(sent, levels)]
        return [keep(value, message, *level[step]) for value, message, level in zip(values, got, levels)]

    def halve(values):
        value = jnp.stack(values)
        for bit in rest[:-1]:
            value = keep(value, swap(give(value, bit, 1), bit), bit, 1)
        return value

    def gather(value, first=None):
        for bit in reversed([zbit] + rest[:-1]):
            got = swap(value, bit)
            if first is not None and bit == zbit:
                got = after(got, first)
            value = join(value, got, bit)
        return value.reshape(-1, value.shape[-1])

    def scores(group, value):
        return lax.dot_general(group, value, (((1,), (1,)), ((), ())), preferred_element_type=jnp.float32)

    blocks = train.reshape(examples * nblocks, width)
    every = examples * nblocks
    middle = max(1, examples * 7 // 16) * nblocks

    def features(blocks, first, count, other):
        start = offsets[ybit, width // 2][other]
        return lax.dynamic_slice(blocks, (first, start), (count, width // 2), allow_negative_indices=False)

    high = lax.reduce_precision(queries, 8, 7)
    low = (queries - high).astype(jnp.bfloat16)
    high = high.astype(jnp.bfloat16)
    left = jnp.concatenate([high, low, high], axis=1)
    blocks = after(blocks, left)
    early = features(blocks, 0, middle, 1)
    other_core, blocks = after((other_core, blocks), early)
    early = swap(early, ybit)

    *full, high, low = product(other_core, left, [precond], other_kernel, OTHER_VMEM, CHUNKS)
    sent = pack(full[0])
    got = swap(sent, 0)
    mine = product(after(core, sent), left, [high, low], mine_kernel, MINE_VMEM, CHUNKS * PATHS)
    one = paths(mine[:PATHS], got)
    sent = messages(one, 0)
    got = swap(pack(after(full[1], mine[0])), 0)
    two = paths(mine[PATHS:], after(got, sent))
    blocks = after(blocks, sent)
    near = features(blocks, 0, every, 0)
    sibling = swap(near, 0)
    one = exchange(one, sent, 0)
    sent = messages(one, 1)
    sent_two = after(messages(two, 0), (sent, early))
    one = halve(exchange(one, sent, 1))
    sent = pack(one)
    got_one = swap(sent, rest[-1])
    two = exchange(two, sent_two, 0)
    two = exchange(two, messages(two, 1), 1)
    late = swap(features(after(blocks, two[0]), middle, every - middle, 1), ybit)
    two = halve(two)
    sent = pack(two)
    one = (after(one, sent) + unpack(got_one)).astype(jnp.bfloat16)
    got_two = swap(sent, rest[-1])
    early = after(early, one)
    one = gather(one)
    groups = [
        jnp.concatenate([near, sibling], axis=0),
        jnp.concatenate([early, late, swap(early, 0), swap(late, 0)], axis=0),
    ]
    def deliver(value):
        ordered = in_slot_order([scores(group, value) for group in groups], slot_block)
        ordered = ordered.reshape(n, owned, 2 * CORES * examples, value.shape[0])
        return ordered, lax.all_to_all(ordered, "rows", split_axis=0, concat_axis=0, tiled=True)

    ordered, got_one = deliver(one)
    two = gather((two + unpack(got_two)).astype(jnp.bfloat16), ordered)
    ordered, got_two = deliver(two)

    lists = (query_cluster, cand_blocks, cand_count, slot_block, first_slot)
    query_cluster, cand_blocks, cand_count, slot_block, first_slot = after(lists, ordered)
    allowed = listed_mask(query_cluster, cand_blocks, cand_count, nblocks)
    slots = lax.dynamic_slice(slot_block, (first_slot,), (owned,), allow_negative_indices=False)
    own_allowed = jnp.take(allowed, slots, axis=0, mode="clip")
    got = [value.reshape(n, owned, 2 * CORES, examples, -1) for value in (got_one, got_two)]
    return finish(got, own_allowed)


def solution(mesh):
    placed = (
        P("groups", "rows"),
        P("rows", None),
        P("rows", "groups", None),
        P("groups"),
        P("groups", None),
        P("groups"),
        P("groups"),
    )
    return jax.shard_map(
        shards,
        mesh=mesh,
        in_specs=placed,
        out_specs=P(None, ("groups", "rows"), None),
        check_vma=False,
    )
```

```python
import jax
import jax.numpy as jnp
from jax import lax
from jax.experimental import pallas as pl
from jax.experimental.pallas import tpu as pltpu
from jax.sharding import PartitionSpec as P

CORES = 2
CHUNKS = 2
PATHS = 2
UNIT = 2.0 ** 18
LEAST = 2.0 ** -100
LANES = 128
AHEAD = 3
OTHER_VMEM = 44
MINE_VMEM = 16


def listed_mask(query_cluster, cand_blocks, cand_count, nblocks):
    nclusters = cand_blocks.shape[0]
    valid = jnp.arange(cand_blocks.shape[1])[None, :] < cand_count[:, None]
    hits = (cand_blocks[:, :, None] == jnp.arange(nblocks)[None, None, :]) & valid[:, :, None]
    listed = jnp.any(hits, axis=1).astype(jnp.float32)
    onehot = (query_cluster[:, None] == jnp.arange(nclusters)[None, :]).astype(jnp.float32)
    return jnp.dot(listed.T, onehot.T, preferred_element_type=jnp.float32)


def split(value):
    high = value.astype(jnp.bfloat16)
    return high, (value - high.astype(jnp.float32)).astype(jnp.bfloat16)


def rows_of(core_ref, rows_ref):
    half = rows_ref.shape[0] // CORES
    return rows_ref[pl.ds(pl.multiple_of(core_ref[0] * half, half), half), :]


def multiply(left, high, low, outs, columns):
    right = jnp.concatenate([high, high, low], axis=0)
    result = jnp.dot(left, right, preferred_element_type=jnp.float32)
    part = result.shape[0] // len(outs)
    for chunk, out_ref in enumerate(outs):
        out_ref[:, columns] = result[chunk * part:(chunk + 1) * part]


def other_kernel(core_ref, rows_ref, columns_hbm, *refs):
    outs, (high_ref, low_ref, columns_ref, sems) = refs[:-4], refs[-4:]
    steps, _, block = columns_ref.shape

    def load(i):
        return pltpu.make_async_copy(
            columns_hbm.at[:, i * block:(i + 1) * block], columns_ref.at[i], sems.at[i]
        )

    for i in range(min(AHEAD, steps)):
        load(i).start()
    left = rows_of(core_ref, rows_ref)
    for i in range(steps):
        load(i).wait()
        if i + AHEAD < steps:
            load(i + AHEAD).start()
        columns = slice(i * block, (i + 1) * block)
        high, low = split(columns_ref[i])
        high_ref[:, columns] = high
        low_ref[:, columns] = low
        multiply(left, high, low, outs, columns)


def mine_kernel(core_ref, rows_ref, high_ref, low_ref, *outs):
    left = rows_of(core_ref, rows_ref)
    width = high_ref.shape[1]
    block = min(512, width)
    for i in range(width // block):
        columns = slice(i * block, (i + 1) * block)
        multiply(left, high_ref[:, columns], low_ref[:, columns], outs, columns)


def product(core, rows, columns, kernel, vmem, pieces):
    nrows = rows.shape[0]
    depth, width = columns[0].shape
    block = min(512, width)
    out = [jax.ShapeDtypeStruct((nrows // CORES // pieces, width), jnp.float32)] * pieces
    in_vmem = pl.BlockSpec(memory_space=pltpu.VMEM)
    operand, scratch = in_vmem, []
    if kernel is other_kernel:
        out = out + [jax.ShapeDtypeStruct((depth, width), jnp.bfloat16)] * 2
        operand = pl.BlockSpec(memory_space=pltpu.HBM)
        scratch = [
            pltpu.VMEM((width // block, depth, block), jnp.float32),
            pltpu.SemaphoreType.DMA((width // block,)),
        ]
    return pl.pallas_call(
        kernel,
        in_specs=[pl.BlockSpec(memory_space=pltpu.SMEM), in_vmem] + [operand] * len(columns),
        out_specs=[in_vmem] * len(out),
        out_shape=out,
        scratch_shapes=scratch,
        compiler_params=pltpu.CompilerParams(vmem_limit_bytes=vmem * 1024 * 1024),
        cost_estimate=pl.CostEstimate(
            flops=3 * nrows * depth * width,
            bytes_accessed=4 * width * depth + 2 * width * nrows,
            transcendentals=0,
        ),
    )(core.reshape(1), rows, *columns)


def order_kernel(slots_ref, *refs):
    raws, (out_hbm, staged_ref, sems) = refs[:-3], refs[-3:]
    nblocks = slots_ref.shape[0]
    groups = len(raws) // CHUNKS
    parts = sems.shape[0]
    size = nblocks // parts

    def send(part):
        slots = pl.ds(part * size, size)
        return pltpu.make_async_copy(staged_ref.at[slots], out_hbm.at[slots], sems.at[part])

    for part in range(parts):
        for slot in range(part * size, (part + 1) * size):
            for i, raw_ref in enumerate(raws):
                examples, width = raw_ref.shape[0] // nblocks, raw_ref.shape[1]
                chunk, group = divmod(i, groups)
                rows = pl.ds(slots_ref[slot], examples, stride=nblocks)
                staged_ref[
                    slot, group * examples:(group + 1) * examples, chunk * width:(chunk + 1) * width
                ] = raw_ref[rows, :].astype(staged_ref.dtype)
        send(part).start()
    for part in range(parts):
        send(part).wait()


def in_slot_order(raws, slots):
    nblocks = slots.shape[0]
    rows, width = raws[0].shape
    groups = len(raws) // CHUNKS
    shape = (nblocks, groups * rows // nblocks, CHUNKS * width)
    return pl.pallas_call(
        order_kernel,
        in_specs=[pl.BlockSpec(memory_space=pltpu.SMEM)] + [pl.BlockSpec(memory_space=pltpu.VMEM)] * len(raws),
        out_specs=pl.BlockSpec(memory_space=pltpu.HBM),
        out_shape=jax.ShapeDtypeStruct(shape, jnp.bfloat16),
        scratch_shapes=[pltpu.VMEM(shape, jnp.bfloat16), pltpu.SemaphoreType.DMA((4,))],
        compiler_params=pltpu.CompilerParams(vmem_limit_bytes=4 * 1024 * 1024),
        cost_estimate=pl.CostEstimate(
            flops=rows * width, bytes_accessed=6 * len(raws) * rows * width, transcendentals=0
        ),
    )(slots, *raws)


def finish_kernel(got_ref, allowed_ref, out_ref):
    n, owned, quad, examples, half = got_ref.shape
    parts = half // LANES
    per_row = owned * CORES * parts
    for device in range(n):
        for core in range(CORES):
            sources = [(device & ~3) | (y << 1) | core for y in range(quad // CORES)]
            for slot in range(owned):
                scores = sum(got_ref[s, slot, s ^ device].astype(jnp.float32) for s in sources)
                scores = scores * allowed_ref[slot:slot + 1, core * half:(core + 1) * half]
                for i in range(parts):
                    first = device * examples * per_row + (slot * CORES + core) * parts + i
                    out_ref[pl.ds(first, examples, stride=per_row), :] = scores[:, i * LANES:(i + 1) * LANES]


def finish(got, allowed):
    n, owned, _, examples, half = got.shape
    flat = pl.pallas_call(
        finish_kernel,
        out_shape=jax.ShapeDtypeStruct((n * examples * owned * CORES * half // LANES, LANES), jnp.float32),
        compiler_params=pltpu.CompilerParams(vmem_limit_bytes=4 * 1024 * 1024),
        cost_estimate=pl.CostEstimate(flops=got.size, bytes_accessed=4 * got.size, transcendentals=0),
    )(got, allowed)
    return flat.reshape(n * examples, owned, CORES * half)


def shards(queries, precond, train, query_cluster, cand_blocks, cand_count, slot_block):
    n = lax.axis_size("rows")
    chips = n // CORES
    bits = chips.bit_length() - 1
    ybit, zbit = 1, 1 + bits // 2
    rest = [bit for bit in range(1, 1 + bits) if bit not in (ybit, zbit)]
    me = lax.axis_index("rows")
    core = me & 1

    examples, nblocks, width = train.shape
    nq = queries.shape[0]

    def swap(value, bit):
        return lax.ppermute(value, "rows", [(r, r ^ (1 << bit)) for r in range(n)])

    rows = nq // CORES // CHUNKS // PATHS
    sizes = {(ybit, width // 2), (zbit, rows // 2)} | {(bit, rows >> (i + 2)) for i, bit in enumerate(rest[:-1])}
    offsets = {}
    first_half = {}
    for bit, size in sorted(sizes):
        side = (me >> bit) & 1
        offsets[bit, size] = (side * size, (1 - side) * size)
        first_half[bit] = side == 0
    owned = nblocks // n
    first_slot = me * owned
    scalars = (core, 1 - core, first_slot, offsets, first_half)
    scalars, queries, train = lax.optimization_barrier((scalars, queries, train))
    core, other_core, first_slot, offsets, first_half = scalars

    def pack(value):
        value = value * UNIT
        return (value * lax.rsqrt(jnp.abs(value) + LEAST)).astype(jnp.float16)

    def unpack(value):
        value = value.astype(jnp.float32)
        return value * jnp.abs(value) * (1.0 / UNIT)

    def part(value, bit, axis, other=0):
        shape = list(value.shape)
        shape[axis] //= 2
        starts = [0] * value.ndim
        starts[axis] = offsets[bit, shape[axis]][other]
        return lax.dynamic_slice(value, starts, shape, allow_negative_indices=False)

    def give(value, bit, axis):
        return pack(part(value, bit, axis, 1))

    def keep(value, got, bit, axis):
        return part(value, bit, axis) + unpack(got)

    def join(own, got, bit):
        mine_first = jnp.concatenate([own, got], axis=1)
        return jnp.where(first_half[bit], mine_first, jnp.concatenate([got, own], axis=1))

    def after(value, first):
        return lax.optimization_barrier((value, first))[0]

    def paths(values, other):
        return [value + unpack(other[i * rows:(i + 1) * rows]) for i, value in enumerate(values)]

    levels = ((ybit, 1), (zbit, 0)), ((zbit, 0), (ybit, 1))

    def messages(values, step):
        return [give(value, *level[step]) for value, level in zip(values, levels)]

    def exchange(values, sent, step):
        got = [swap(message, level[step][0]) for message, level in zip(sent, levels)]
        return [keep(value, message, *level[step]) for value, message, level in zip(values, got, levels)]

    def halve(values):
        value = jnp.stack(values)
        for bit in rest[:-1]:
            value = keep(value, swap(give(value, bit, 1), bit), bit, 1)
        return value

    def gather(value, first=None):
        for bit in reversed([zbit] + rest[:-1]):
            got = swap(value, bit)
            if first is not None and bit == zbit:
                got = after(got, first)
            value = join(value, got, bit)
        return value.reshape(-1, value.shape[-1])

    def scores(group, value):
        return lax.dot_general(group, value, (((1,), (1,)), ((), ())), preferred_element_type=jnp.float32)

    blocks = train.reshape(examples * nblocks, width)
    every = examples * nblocks
    middle = max(1, examples * 3 // 8) * nblocks

    def features(blocks, first, count, other):
        start = offsets[ybit, width // 2][other]
        return lax.dynamic_slice(blocks, (first, start), (count, width // 2), allow_negative_indices=False)

    high = lax.reduce_precision(queries, 8, 7)
    low = (queries - high).astype(jnp.bfloat16)
    high = high.astype(jnp.bfloat16)
    left = jnp.concatenate([high, low, high], axis=1)
    blocks = after(blocks, left)
    early = features(blocks, 0, middle, 1)
    other_core, blocks = after((other_core, blocks), early)
    early = swap(early, ybit)

    *full, high, low = product(other_core, left, [precond], other_kernel, OTHER_VMEM, CHUNKS)
    sent = pack(full[0])
    got = swap(sent, 0)
    mine = product(after(core, sent), left, [high, low], mine_kernel, MINE_VMEM, CHUNKS * PATHS)
    one = paths(mine[:PATHS], got)
    sent = messages(one, 0)
    got = swap(pack(after(full[1], mine[0])), 0)
    two = paths(mine[PATHS:], after(got, sent))
    blocks = after(blocks, sent)
    near = features(blocks, 0, every, 0)
    sibling = swap(near, 0)
    one = exchange(one, sent, 0)
    sent = messages(one, 1)
    sent_two = after(messages(two, 0), (sent, early))
    one = halve(exchange(one, sent, 1))
    sent = pack(one)
    got_one = swap(sent, rest[-1])
    two = exchange(two, sent_two, 0)
    two = exchange(two, messages(two, 1), 1)
    late = swap(features(after(blocks, two[0]), middle, every - middle, 1), ybit)
    two = halve(two)
    sent = pack(two)
    one = (after(one, sent) + unpack(got_one)).astype(jnp.bfloat16)
    got_two = swap(sent, rest[-1])
    early = after(early, one)
    one = gather(one)
    groups = [
        jnp.concatenate([near, sibling], axis=0),
        jnp.concatenate([early, late, swap(early, 0), swap(late, 0)], axis=0),
    ]
    raws = [scores(group, one) for group in groups]
    two = gather((two + unpack(got_two)).astype(jnp.bfloat16), raws)
    raws = raws + [scores(group, two) for group in groups]

    ordered = in_slot_order(raws, slot_block).reshape(n, owned, 2 * CORES * examples, nq // CORES)
    got = lax.all_to_all(ordered, "rows", split_axis=0, concat_axis=0, tiled=True)

    lists = (query_cluster, cand_blocks, cand_count, slot_block, first_slot)
    query_cluster, cand_blocks, cand_count, slot_block, first_slot = after(lists, ordered)
    allowed = listed_mask(query_cluster, cand_blocks, cand_count, nblocks)
    slots = lax.dynamic_slice(slot_block, (first_slot,), (owned,), allow_negative_indices=False)
    own_allowed = jnp.take(allowed, slots, axis=0, mode="clip")
    return finish(got.reshape(n, owned, 2 * CORES, examples, nq // CORES), own_allowed)


def solution(mesh):
    placed = (
        P("groups", "rows"),
        P("rows", None),
        P("rows", "groups", None),
        P("groups"),
        P("groups", None),
        P("groups"),
        P("groups"),
    )
    return jax.shard_map(
        shards,
        mesh=mesh,
        in_specs=placed,
        out_specs=P(None, ("groups", "rows"), None),
        check_vma=False,
    )
```

```python
import jax
import jax.numpy as jnp
from jax import lax
from jax.experimental import pallas as pl
from jax.experimental.pallas import tpu as pltpu
from jax.sharding import PartitionSpec as P

CORES = 2
CHUNKS = 2
PATHS = 2
UNIT = 2.0 ** 18
LEAST = 2.0 ** -100
LANES = 128
AHEAD = 6
LOAD_COLUMNS = 256
OTHER_VMEM = 44
MINE_VMEM = 16


def listed_mask(query_cluster, cand_blocks, cand_count, nblocks):
    nclusters = cand_blocks.shape[0]
    valid = jnp.arange(cand_blocks.shape[1])[None, :] < cand_count[:, None]
    hits = (cand_blocks[:, :, None] == jnp.arange(nblocks)[None, None, :]) & valid[:, :, None]
    listed = jnp.any(hits, axis=1).astype(jnp.float32)
    onehot = (query_cluster[:, None] == jnp.arange(nclusters)[None, :]).astype(jnp.float32)
    return jnp.dot(listed.T, onehot.T, preferred_element_type=jnp.float32)


def split(value):
    high = value.astype(jnp.bfloat16)
    return high, (value - high.astype(jnp.float32)).astype(jnp.bfloat16)


def rows_of(core_ref, rows_ref):
    half = rows_ref.shape[0] // CORES
    return rows_ref[pl.ds(pl.multiple_of(core_ref[0] * half, half), half), :]


def multiply(left, high, low, outs, columns):
    right = jnp.concatenate([high, high, low], axis=0)
    result = jnp.dot(left, right, preferred_element_type=jnp.float32)
    part = result.shape[0] // len(outs)
    for chunk, out_ref in enumerate(outs):
        out_ref[:, columns] = result[chunk * part:(chunk + 1) * part]


def other_kernel(core_ref, rows_ref, columns_hbm, *refs):
    outs, (high_ref, low_ref, columns_ref, sems) = refs[:-4], refs[-4:]
    steps, _, block = columns_ref.shape

    def load(i):
        return pltpu.make_async_copy(
            columns_hbm.at[:, i * block:(i + 1) * block], columns_ref.at[i], sems.at[i]
        )

    for i in range(min(AHEAD, steps)):
        load(i).start()
    left = rows_of(core_ref, rows_ref)
    for i in range(steps):
        load(i).wait()
        if i + AHEAD < steps:
            load(i + AHEAD).start()
        columns = slice(i * block, (i + 1) * block)
        high, low = split(columns_ref[i])
        high_ref[:, columns] = high
        low_ref[:, columns] = low
        multiply(left, high, low, outs, columns)


def mine_kernel(core_ref, rows_ref, high_ref, low_ref, *outs):
    left = rows_of(core_ref, rows_ref)
    width = high_ref.shape[1]
    block = min(512, width)
    for i in range(width // block):
        columns = slice(i * block, (i + 1) * block)
        multiply(left, high_ref[:, columns], low_ref[:, columns], outs, columns)


def product(core, rows, columns, kernel, vmem, pieces):
    nrows = rows.shape[0]
    depth, width = columns[0].shape
    block = min(LOAD_COLUMNS, width)
    out = [jax.ShapeDtypeStruct((nrows // CORES // pieces, width), jnp.float32)] * pieces
    in_vmem = pl.BlockSpec(memory_space=pltpu.VMEM)
    operand, scratch = in_vmem, []
    if kernel is other_kernel:
        out = out + [jax.ShapeDtypeStruct((depth, width), jnp.bfloat16)] * 2
        operand = pl.BlockSpec(memory_space=pltpu.HBM)
        scratch = [
            pltpu.VMEM((width // block, depth, block), jnp.float32),
            pltpu.SemaphoreType.DMA((width // block,)),
        ]
    return pl.pallas_call(
        kernel,
        in_specs=[pl.BlockSpec(memory_space=pltpu.SMEM), in_vmem] + [operand] * len(columns),
        out_specs=[in_vmem] * len(out),
        out_shape=out,
        scratch_shapes=scratch,
        compiler_params=pltpu.CompilerParams(vmem_limit_bytes=vmem * 1024 * 1024),
        cost_estimate=pl.CostEstimate(
            flops=3 * nrows * depth * width,
            bytes_accessed=4 * width * depth + 2 * width * nrows,
            transcendentals=0,
        ),
    )(core.reshape(1), rows, *columns)


def order_kernel(slots_ref, *refs):
    raws, (out_hbm, staged_ref, sems) = refs[:-3], refs[-3:]
    nblocks = slots_ref.shape[0]
    groups = len(raws) // CHUNKS
    parts = sems.shape[0]
    size = nblocks // parts

    def send(part):
        slots = pl.ds(part * size, size)
        return pltpu.make_async_copy(staged_ref.at[slots], out_hbm.at[slots], sems.at[part])

    for part in range(parts):
        for slot in range(part * size, (part + 1) * size):
            for i, raw_ref in enumerate(raws):
                examples, width = raw_ref.shape[0] // nblocks, raw_ref.shape[1]
                chunk, group = divmod(i, groups)
                rows = pl.ds(slots_ref[slot], examples, stride=nblocks)
                staged_ref[
                    slot, group * examples:(group + 1) * examples, chunk * width:(chunk + 1) * width
                ] = raw_ref[rows, :].astype(staged_ref.dtype)
        send(part).start()
    for part in range(parts):
        send(part).wait()


def in_slot_order(raws, slots):
    nblocks = slots.shape[0]
    rows, width = raws[0].shape
    groups = len(raws) // CHUNKS
    shape = (nblocks, groups * rows // nblocks, CHUNKS * width)
    return pl.pallas_call(
        order_kernel,
        in_specs=[pl.BlockSpec(memory_space=pltpu.SMEM)] + [pl.BlockSpec(memory_space=pltpu.VMEM)] * len(raws),
        out_specs=pl.BlockSpec(memory_space=pltpu.HBM),
        out_shape=jax.ShapeDtypeStruct(shape, jnp.bfloat16),
        scratch_shapes=[pltpu.VMEM(shape, jnp.bfloat16), pltpu.SemaphoreType.DMA((4,))],
        compiler_params=pltpu.CompilerParams(vmem_limit_bytes=4 * 1024 * 1024),
        cost_estimate=pl.CostEstimate(
            flops=rows * width, bytes_accessed=6 * len(raws) * rows * width, transcendentals=0
        ),
    )(slots, *raws)


def finish_kernel(got_ref, allowed_ref, out_ref):
    n, owned, quad, examples, half = got_ref.shape
    parts = half // LANES
    per_row = owned * CORES * parts
    for device in range(n):
        for core in range(CORES):
            sources = [(device & ~3) | (y << 1) | core for y in range(quad // CORES)]
            for slot in range(owned):
                scores = sum(got_ref[s, slot, s ^ device].astype(jnp.float32) for s in sources)
                scores = scores * allowed_ref[slot:slot + 1, core * half:(core + 1) * half]
                for i in range(parts):
                    first = device * examples * per_row + (slot * CORES + core) * parts + i
                    out_ref[pl.ds(first, examples, stride=per_row), :] = scores[:, i * LANES:(i + 1) * LANES]


def finish(got, allowed):
    n, owned, _, examples, half = got.shape
    flat = pl.pallas_call(
        finish_kernel,
        out_shape=jax.ShapeDtypeStruct((n * examples * owned * CORES * half // LANES, LANES), jnp.float32),
        compiler_params=pltpu.CompilerParams(vmem_limit_bytes=4 * 1024 * 1024),
        cost_estimate=pl.CostEstimate(flops=got.size, bytes_accessed=4 * got.size, transcendentals=0),
    )(got, allowed)
    return flat.reshape(n * examples, owned, CORES * half)


def shards(queries, precond, train, query_cluster, cand_blocks, cand_count, slot_block):
    n = lax.axis_size("rows")
    chips = n // CORES
    bits = chips.bit_length() - 1
    ybit, zbit = 1, 1 + bits // 2
    rest = [bit for bit in range(1, 1 + bits) if bit not in (ybit, zbit)]
    me = lax.axis_index("rows")
    core = me & 1

    examples, nblocks, width = train.shape
    nq = queries.shape[0]

    def swap(value, bit):
        return lax.ppermute(value, "rows", [(r, r ^ (1 << bit)) for r in range(n)])

    rows = nq // CORES // CHUNKS // PATHS
    sizes = {(ybit, width // 2), (zbit, rows // 2)} | {(bit, rows >> (i + 2)) for i, bit in enumerate(rest[:-1])}
    offsets = {}
    first_half = {}
    for bit, size in sorted(sizes):
        side = (me >> bit) & 1
        offsets[bit, size] = (side * size, (1 - side) * size)
        first_half[bit] = side == 0
    owned = nblocks // n
    first_slot = me * owned
    scalars = (core, 1 - core, first_slot, offsets, first_half)
    scalars, queries, train = lax.optimization_barrier((scalars, queries, train))
    core, other_core, first_slot, offsets, first_half = scalars

    def pack(value):
        value = value * UNIT
        return (value * lax.rsqrt(jnp.abs(value) + LEAST)).astype(jnp.float16)

    def unpack(value):
        value = value.astype(jnp.float32)
        return value * jnp.abs(value) * (1.0 / UNIT)

    def part(value, bit, axis, other=0):
        shape = list(value.shape)
        shape[axis] //= 2
        starts = [0] * value.ndim
        starts[axis] = offsets[bit, shape[axis]][other]
        return lax.dynamic_slice(value, starts, shape, allow_negative_indices=False)

    def give(value, bit, axis):
        return pack(part(value, bit, axis, 1))

    def keep(value, got, bit, axis):
        return part(value, bit, axis) + unpack(got)

    def join(own, got, bit):
        mine_first = jnp.concatenate([own, got], axis=1)
        return jnp.where(first_half[bit], mine_first, jnp.concatenate([got, own], axis=1))

    def after(value, first):
        return lax.optimization_barrier((value, first))[0]

    def paths(values, other):
        return [value + unpack(other[i * rows:(i + 1) * rows]) for i, value in enumerate(values)]

    levels = ((ybit, 1), (zbit, 0)), ((zbit, 0), (ybit, 1))

    def messages(values, step):
        return [give(value, *level[step]) for value, level in zip(values, levels)]

    def exchange(values, sent, step):
        got = [swap(message, level[step][0]) for message, level in zip(sent, levels)]
        return [keep(value, message, *level[step]) for value, message, level in zip(values, got, levels)]

    def halve(values):
        value = jnp.stack(values)
        for bit in rest[:-1]:
            value = keep(value, swap(give(value, bit, 1), bit), bit, 1)
        return value

    def gather(value, first=None):
        for bit in reversed([zbit] + rest[:-1]):
            got = swap(value, bit)
            if first is not None and bit == zbit:
                got = after(got, first)
            value = join(value, got, bit)
        return value.reshape(-1, value.shape[-1])

    def scores(group, value):
        return lax.dot_general(group, value, (((1,), (1,)), ((), ())), preferred_element_type=jnp.float32)

    blocks = train.reshape(examples * nblocks, width)
    every = examples * nblocks
    middle = max(1, examples * 3 // 8) * nblocks

    def features(blocks, first, count, other):
        start = offsets[ybit, width // 2][other]
        return lax.dynamic_slice(blocks, (first, start), (count, width // 2), allow_negative_indices=False)

    high = lax.reduce_precision(queries, 8, 7)
    low = (queries - high).astype(jnp.bfloat16)
    high = high.astype(jnp.bfloat16)
    left = jnp.concatenate([high, low, high], axis=1)
    blocks = after(blocks, left)
    early = features(blocks, 0, middle, 1)
    other_core, blocks = after((other_core, blocks), early)
    early = swap(early, ybit)

    *full, high, low = product(other_core, left, [precond], other_kernel, OTHER_VMEM, CHUNKS)
    sent = pack(full[0])
    got = swap(sent, 0)
    mine = product(after(core, sent), left, [high, low], mine_kernel, MINE_VMEM, CHUNKS * PATHS)
    one = paths(mine[:PATHS], got)
    sent = messages(one, 0)
    got = swap(pack(after(full[1], mine[0])), 0)
    two = paths(mine[PATHS:], after(got, sent))
    blocks = after(blocks, sent)
    near = features(blocks, 0, every, 0)
    sibling = swap(near, 0)
    one = exchange(one, sent, 0)
    sent = messages(one, 1)
    sent_two = after(messages(two, 0), (sent, early))
    one = halve(exchange(one, sent, 1))
    sent = pack(one)
    got_one = swap(sent, rest[-1])
    two = exchange(two, sent_two, 0)
    two = exchange(two, messages(two, 1), 1)
    late = swap(features(after(blocks, two[0]), middle, every - middle, 1), ybit)
    two = halve(two)
    sent = pack(two)
    one = (after(one, sent) + unpack(got_one)).astype(jnp.bfloat16)
    got_two = swap(sent, rest[-1])
    early = after(early, one)
    one = gather(one)
    groups = [
        jnp.concatenate([near, sibling], axis=0),
        jnp.concatenate([early, late, swap(early, 0), swap(late, 0)], axis=0),
    ]
    raws = [scores(group, one) for group in groups]
    two = gather((two + unpack(got_two)).astype(jnp.bfloat16), raws)
    raws = raws + [scores(group, two) for group in groups]

    ordered = in_slot_order(raws, slot_block).reshape(n, owned, 2 * CORES * examples, nq // CORES)
    got = lax.all_to_all(ordered, "rows", split_axis=0, concat_axis=0, tiled=True)

    lists = (query_cluster, cand_blocks, cand_count, slot_block, first_slot)
    query_cluster, cand_blocks, cand_count, slot_block, first_slot = after(lists, ordered)
    allowed = listed_mask(query_cluster, cand_blocks, cand_count, nblocks)
    slots = lax.dynamic_slice(slot_block, (first_slot,), (owned,), allow_negative_indices=False)
    own_allowed = jnp.take(allowed, slots, axis=0, mode="clip")
    return finish(got.reshape(n, owned, 2 * CORES, examples, nq // CORES), own_allowed)


def solution(mesh):
    placed = (
        P("groups", "rows"),
        P("rows", None),
        P("rows", "groups", None),
        P("groups"),
        P("groups", None),
        P("groups"),
        P("groups"),
    )
    return jax.shard_map(
        shards,
        mesh=mesh,
        in_specs=placed,
        out_specs=P(None, ("groups", "rows"), None),
        check_vma=False,
    )
```

```python
import jax
import jax.numpy as jnp
from jax import lax
from jax.experimental import pallas as pl
from jax.experimental.pallas import tpu as pltpu
from jax.sharding import PartitionSpec as P

CORES = 2
CHUNKS = 2
PATHS = 2
UNIT = 2.0 ** 18
LEAST = 2.0 ** -100
LANES = 128
OTHER_VMEM = 44
MINE_VMEM = 16


def listed_mask(query_cluster, cand_blocks, cand_count, nblocks):
    nclusters = cand_blocks.shape[0]
    valid = jnp.arange(cand_blocks.shape[1])[None, :] < cand_count[:, None]
    hits = (cand_blocks[:, :, None] == jnp.arange(nblocks)[None, None, :]) & valid[:, :, None]
    listed = jnp.any(hits, axis=1).astype(jnp.float32)
    onehot = (query_cluster[:, None] == jnp.arange(nclusters)[None, :]).astype(jnp.float32)
    return jnp.dot(listed.T, onehot.T, preferred_element_type=jnp.float32)


def split(value):
    high = value.astype(jnp.bfloat16)
    return high, (value - high.astype(jnp.float32)).astype(jnp.bfloat16)


def rows_of(core_ref, rows_ref):
    half = rows_ref.shape[0] // CORES
    return rows_ref[pl.ds(pl.multiple_of(core_ref[0] * half, half), half), :]


def multiply(left, high, low, outs, columns):
    right = jnp.concatenate([high, high, low], axis=0)
    result = jnp.dot(left, right, preferred_element_type=jnp.float32)
    part = result.shape[0] // len(outs)
    for chunk, out_ref in enumerate(outs):
        out_ref[:, columns] = result[chunk * part:(chunk + 1) * part]


def other_kernel(core_ref, rows_ref, columns_hbm, *refs):
    outs, (high_ref, low_ref, columns_ref, sems) = refs[:-4], refs[-4:]
    steps, _, block = columns_ref.shape

    def load(i):
        return pltpu.make_async_copy(
            columns_hbm.at[:, i * block:(i + 1) * block], columns_ref.at[i], sems.at[i]
        )

    for i in range(steps):
        load(i).start()
    left = rows_of(core_ref, rows_ref)

    def take(i):
        columns = slice(i * block, (i + 1) * block)
        multiply(left, high_ref[:, columns], low_ref[:, columns], outs, columns)

    for i in range(steps):
        load(i).wait()
        columns = slice(i * block, (i + 1) * block)
        high, low = split(columns_ref[i])
        high_ref[:, columns] = high
        low_ref[:, columns] = low
        if i:
            take(i - 1)
    take(steps - 1)


def mine_kernel(core_ref, rows_ref, high_ref, low_ref, *outs):
    left = rows_of(core_ref, rows_ref)
    width = high_ref.shape[1]
    block = min(512, width)
    for i in range(width // block):
        columns = slice(i * block, (i + 1) * block)
        multiply(left, high_ref[:, columns], low_ref[:, columns], outs, columns)


def product(core, rows, columns, kernel, vmem, pieces):
    nrows = rows.shape[0]
    depth, width = columns[0].shape
    block = min(512, width)
    out = [jax.ShapeDtypeStruct((nrows // CORES // pieces, width), jnp.float32)] * pieces
    in_vmem = pl.BlockSpec(memory_space=pltpu.VMEM)
    operand, scratch = in_vmem, []
    if kernel is other_kernel:
        out = out + [jax.ShapeDtypeStruct((depth, width), jnp.bfloat16)] * 2
        operand = pl.BlockSpec(memory_space=pltpu.HBM)
        scratch = [
            pltpu.VMEM((width // block, depth, block), jnp.float32),
            pltpu.SemaphoreType.DMA((width // block,)),
        ]
    return pl.pallas_call(
        kernel,
        in_specs=[pl.BlockSpec(memory_space=pltpu.SMEM), in_vmem] + [operand] * len(columns),
        out_specs=[in_vmem] * len(out),
        out_shape=out,
        scratch_shapes=scratch,
        compiler_params=pltpu.CompilerParams(vmem_limit_bytes=vmem * 1024 * 1024),
        cost_estimate=pl.CostEstimate(
            flops=3 * nrows * depth * width,
            bytes_accessed=4 * width * depth + 2 * width * nrows,
            transcendentals=0,
        ),
    )(core.reshape(1), rows, *columns)


def order_kernel(slots_ref, *refs):
    raws, (out_hbm, staged_ref, sems) = refs[:-3], refs[-3:]
    nblocks = slots_ref.shape[0]
    groups = len(raws) // CHUNKS
    parts = sems.shape[0]
    size = nblocks // parts

    def send(part):
        slots = pl.ds(part * size, size)
        return pltpu.make_async_copy(staged_ref.at[slots], out_hbm.at[slots], sems.at[part])

    for part in range(parts):
        for slot in range(part * size, (part + 1) * size):
            for i, raw_ref in enumerate(raws):
                examples, width = raw_ref.shape[0] // nblocks, raw_ref.shape[1]
                chunk, group = divmod(i, groups)
                rows = pl.ds(slots_ref[slot], examples, stride=nblocks)
                staged_ref[
                    slot, group * examples:(group + 1) * examples, chunk * width:(chunk + 1) * width
                ] = raw_ref[rows, :].astype(staged_ref.dtype)
        send(part).start()
    for part in range(parts):
        send(part).wait()


def in_slot_order(raws, slots):
    nblocks = slots.shape[0]
    rows, width = raws[0].shape
    groups = len(raws) // CHUNKS
    shape = (nblocks, groups * rows // nblocks, CHUNKS * width)
    return pl.pallas_call(
        order_kernel,
        in_specs=[pl.BlockSpec(memory_space=pltpu.SMEM)] + [pl.BlockSpec(memory_space=pltpu.VMEM)] * len(raws),
        out_specs=pl.BlockSpec(memory_space=pltpu.HBM),
        out_shape=jax.ShapeDtypeStruct(shape, jnp.bfloat16),
        scratch_shapes=[pltpu.VMEM(shape, jnp.bfloat16), pltpu.SemaphoreType.DMA((4,))],
        compiler_params=pltpu.CompilerParams(vmem_limit_bytes=4 * 1024 * 1024),
        cost_estimate=pl.CostEstimate(
            flops=rows * width, bytes_accessed=6 * len(raws) * rows * width, transcendentals=0
        ),
    )(slots, *raws)


def finish_kernel(got_ref, allowed_ref, out_ref):
    n, owned, quad, examples, half = got_ref.shape
    parts = half // LANES
    per_row = owned * CORES * parts
    for device in range(n):
        for core in range(CORES):
            sources = [(device & ~3) | (y << 1) | core for y in range(quad // CORES)]
            for slot in range(owned):
                scores = sum(got_ref[s, slot, s ^ device].astype(jnp.float32) for s in sources)
                scores = scores * allowed_ref[slot:slot + 1, core * half:(core + 1) * half]
                for i in range(parts):
                    first = device * examples * per_row + (slot * CORES + core) * parts + i
                    out_ref[pl.ds(first, examples, stride=per_row), :] = scores[:, i * LANES:(i + 1) * LANES]


def finish(got, allowed):
    n, owned, _, examples, half = got.shape
    flat = pl.pallas_call(
        finish_kernel,
        out_shape=jax.ShapeDtypeStruct((n * examples * owned * CORES * half // LANES, LANES), jnp.float32),
        compiler_params=pltpu.CompilerParams(vmem_limit_bytes=4 * 1024 * 1024),
        cost_estimate=pl.CostEstimate(flops=got.size, bytes_accessed=4 * got.size, transcendentals=0),
    )(got, allowed)
    return flat.reshape(n * examples, owned, CORES * half)


def shards(queries, precond, train, query_cluster, cand_blocks, cand_count, slot_block):
    n = lax.axis_size("rows")
    chips = n // CORES
    bits = chips.bit_length() - 1
    ybit, zbit = 1, 1 + bits // 2
    rest = [bit for bit in range(1, 1 + bits) if bit not in (ybit, zbit)]
    me = lax.axis_index("rows")
    core = me & 1

    examples, nblocks, width = train.shape
    nq = queries.shape[0]

    def swap(value, bit):
        return lax.ppermute(value, "rows", [(r, r ^ (1 << bit)) for r in range(n)])

    rows = nq // CORES // CHUNKS // PATHS
    sizes = {(ybit, width // 2), (zbit, rows // 2)} | {(bit, rows >> (i + 2)) for i, bit in enumerate(rest[:-1])}
    offsets = {}
    first_half = {}
    for bit, size in sorted(sizes):
        side = (me >> bit) & 1
        offsets[bit, size] = (side * size, (1 - side) * size)
        first_half[bit] = side == 0
    owned = nblocks // n
    first_slot = me * owned
    scalars = (core, 1 - core, first_slot, offsets, first_half)
    scalars, queries, train = lax.optimization_barrier((scalars, queries, train))
    core, other_core, first_slot, offsets, first_half = scalars

    def pack(value):
        value = value * UNIT
        return (value * lax.rsqrt(jnp.abs(value) + LEAST)).astype(jnp.float16)

    def unpack(value):
        value = value.astype(jnp.float32)
        return value * jnp.abs(value) * (1.0 / UNIT)

    def part(value, bit, axis, other=0):
        shape = list(value.shape)
        shape[axis] //= 2
        starts = [0] * value.ndim
        starts[axis] = offsets[bit, shape[axis]][other]
        return lax.dynamic_slice(value, starts, shape, allow_negative_indices=False)

    def give(value, bit, axis):
        return pack(part(value, bit, axis, 1))

    def keep(value, got, bit, axis):
        return part(value, bit, axis) + unpack(got)

    def join(own, got, bit):
        mine_first = jnp.concatenate([own, got], axis=1)
        return jnp.where(first_half[bit], mine_first, jnp.concatenate([got, own], axis=1))

    def after(value, first):
        return lax.optimization_barrier((value, first))[0]

    def paths(values, other):
        return [value + unpack(other[i * rows:(i + 1) * rows]) for i, value in enumerate(values)]

    levels = ((ybit, 1), (zbit, 0)), ((zbit, 0), (ybit, 1))

    def messages(values, step):
        return [give(value, *level[step]) for value, level in zip(values, levels)]

    def exchange(values, sent, step):
        got = [swap(message, level[step][0]) for message, level in zip(sent, levels)]
        return [keep(value, message, *level[step]) for value, message, level in zip(values, got, levels)]

    def halve(values):
        value = jnp.stack(values)
        for bit in rest[:-1]:
            value = keep(value, swap(give(value, bit, 1), bit), bit, 1)
        return value

    def gather(value, first=None):
        for bit in reversed([zbit] + rest[:-1]):
            got = swap(value, bit)
            if first is not None and bit == zbit:
                got = after(got, first)
            value = join(value, got, bit)
        return value.reshape(-1, value.shape[-1])

    def scores(group, value):
        return lax.dot_general(group, value, (((1,), (1,)), ((), ())), preferred_element_type=jnp.float32)

    blocks = train.reshape(examples * nblocks, width)
    every = examples * nblocks
    middle = max(1, examples * 3 // 8) * nblocks

    def features(blocks, first, count, other):
        start = offsets[ybit, width // 2][other]
        return lax.dynamic_slice(blocks, (first, start), (count, width // 2), allow_negative_indices=False)

    high = lax.reduce_precision(queries, 8, 7)
    low = (queries - high).astype(jnp.bfloat16)
    high = high.astype(jnp.bfloat16)
    left = jnp.concatenate([high, low, high], axis=1)
    blocks = after(blocks, left)
    early = features(blocks, 0, middle, 1)
    other_core, blocks = after((other_core, blocks), early)
    early = swap(early, ybit)

    *full, high, low = product(other_core, left, [precond], other_kernel, OTHER_VMEM, CHUNKS)
    sent = pack(full[0])
    got = swap(sent, 0)
    mine = product(after(core, sent), left, [high, low], mine_kernel, MINE_VMEM, CHUNKS * PATHS)
    one = paths(mine[:PATHS], got)
    sent = messages(one, 0)
    got = swap(pack(after(full[1], mine[0])), 0)
    two = paths(mine[PATHS:], after(got, sent))
    blocks = after(blocks, sent)
    near = features(blocks, 0, every, 0)
    sibling = swap(near, 0)
    one = exchange(one, sent, 0)
    sent = messages(one, 1)
    sent_two = after(messages(two, 0), (sent, early))
    one = halve(exchange(one, sent, 1))
    sent = pack(one)
    got_one = swap(sent, rest[-1])
    two = exchange(two, sent_two, 0)
    two = exchange(two, messages(two, 1), 1)
    late = swap(features(after(blocks, two[0]), middle, every - middle, 1), ybit)
    two = halve(two)
    sent = pack(two)
    one = (after(one, sent) + unpack(got_one)).astype(jnp.bfloat16)
    got_two = swap(sent, rest[-1])
    early = after(early, one)
    one = gather(one)
    groups = [
        jnp.concatenate([near, sibling], axis=0),
        jnp.concatenate([early, late, swap(early, 0), swap(late, 0)], axis=0),
    ]
    raws = [scores(group, one) for group in groups]
    two = gather((two + unpack(got_two)).astype(jnp.bfloat16), raws)
    raws = raws + [scores(group, two) for group in groups]

    ordered = in_slot_order(raws, slot_block).reshape(n, owned, 2 * CORES * examples, nq // CORES)
    got = lax.all_to_all(ordered, "rows", split_axis=0, concat_axis=0, tiled=True)

    lists = (query_cluster, cand_blocks, cand_count, slot_block, first_slot)
    query_cluster, cand_blocks, cand_count, slot_block, first_slot = after(lists, ordered)
    allowed = listed_mask(query_cluster, cand_blocks, cand_count, nblocks)
    slots = lax.dynamic_slice(slot_block, (first_slot,), (owned,), allow_negative_indices=False)
    own_allowed = jnp.take(allowed, slots, axis=0, mode="clip")
    return finish(got.reshape(n, owned, 2 * CORES, examples, nq // CORES), own_allowed)


def solution(mesh):
    placed = (
        P("groups", "rows"),
        P("rows", None),
        P("rows", "groups", None),
        P("groups"),
        P("groups", None),
        P("groups"),
        P("groups"),
    )
    return jax.shard_map(
        shards,
        mesh=mesh,
        in_specs=placed,
        out_specs=P(None, ("groups", "rows"), None),
        check_vma=False,
    )
```

```python
import jax
import jax.numpy as jnp
from jax import lax
from jax.experimental import pallas as pl
from jax.experimental.pallas import tpu as pltpu
from jax.sharding import PartitionSpec as P

CORES = 2
CHUNKS = 2
PATHS = 2
UNIT = 2.0 ** 18
LEAST = 2.0 ** -100
LANES = 128
OTHER_VMEM = 44
MINE_VMEM = 16


def listed_mask(query_cluster, cand_blocks, cand_count, nblocks):
    nclusters = cand_blocks.shape[0]
    valid = jnp.arange(cand_blocks.shape[1])[None, :] < cand_count[:, None]
    hits = (cand_blocks[:, :, None] == jnp.arange(nblocks)[None, None, :]) & valid[:, :, None]
    listed = jnp.any(hits, axis=1).astype(jnp.float32)
    onehot = (query_cluster[:, None] == jnp.arange(nclusters)[None, :]).astype(jnp.float32)
    return jnp.dot(listed.T, onehot.T, preferred_element_type=jnp.float32)


def split(value):
    high = value.astype(jnp.bfloat16)
    return high, (value - high.astype(jnp.float32)).astype(jnp.bfloat16)


def rows_of(core_ref, rows_ref):
    half = rows_ref.shape[0] // CORES
    return rows_ref[pl.ds(pl.multiple_of(core_ref[0] * half, half), half), :]


def multiply(left, high, low, outs, columns):
    right = jnp.concatenate([high, high, low], axis=0)
    result = jnp.dot(left, right, preferred_element_type=jnp.float32)
    part = result.shape[0] // len(outs)
    for chunk, out_ref in enumerate(outs):
        out_ref[:, columns] = result[chunk * part:(chunk + 1) * part]


def other_kernel(core_ref, rows_ref, columns_hbm, *refs):
    outs, (high_ref, low_ref, columns_ref, sems) = refs[:-4], refs[-4:]
    steps, _, block = columns_ref.shape

    def load(i):
        return pltpu.make_async_copy(
            columns_hbm.at[:, i * block:(i + 1) * block], columns_ref.at[i], sems.at[i]
        )

    for i in range(steps):
        load(i).start()
    left = rows_of(core_ref, rows_ref)
    for i in range(steps):
        load(i).wait()
        columns = slice(i * block, (i + 1) * block)
        high, low = split(columns_ref[i])
        high_ref[:, columns] = high
        low_ref[:, columns] = low
        multiply(left, high, low, outs, columns)


def mine_kernel(core_ref, rows_ref, high_ref, low_ref, *outs):
    chunks = len(outs) // PATHS
    half = rows_ref.shape[0] // CORES
    count = half // CHUNKS * chunks
    first = core_ref[0] * half + core_ref[1] * (half // CHUNKS)
    left = rows_ref[pl.ds(pl.multiple_of(first, half // CHUNKS), count), :]
    width = high_ref.shape[1]
    block = min(512, width)
    for i in range(width // block):
        columns = slice(i * block, (i + 1) * block)
        multiply(left, high_ref[:, columns], low_ref[:, columns], outs, columns)


def product(core, rows, columns, kernel, vmem, pieces):
    nrows = rows.shape[0]
    depth, width = columns[0].shape
    block = min(512, width)
    whole = CHUNKS if kernel is other_kernel else CHUNKS * PATHS
    out = [jax.ShapeDtypeStruct((nrows // CORES // whole, width), jnp.float32)] * pieces
    in_vmem = pl.BlockSpec(memory_space=pltpu.VMEM)
    operand, scratch = in_vmem, []
    if kernel is other_kernel:
        out = out + [jax.ShapeDtypeStruct((depth, width), jnp.bfloat16)] * 2
        operand = pl.BlockSpec(memory_space=pltpu.HBM)
        scratch = [
            pltpu.VMEM((width // block, depth, block), jnp.float32),
            pltpu.SemaphoreType.DMA((width // block,)),
        ]
    return pl.pallas_call(
        kernel,
        in_specs=[pl.BlockSpec(memory_space=pltpu.SMEM), in_vmem] + [operand] * len(columns),
        out_specs=[in_vmem] * len(out),
        out_shape=out,
        scratch_shapes=scratch,
        compiler_params=pltpu.CompilerParams(vmem_limit_bytes=vmem * 1024 * 1024),
        cost_estimate=pl.CostEstimate(
            flops=3 * nrows * depth * width,
            bytes_accessed=4 * width * depth + 2 * width * nrows,
            transcendentals=0,
        ),
    )(core, rows, *columns)


def order_kernel(slots_ref, *refs):
    raws, (out_hbm, staged_ref, sems) = refs[:-3], refs[-3:]
    nblocks = slots_ref.shape[0]
    groups = len(raws) // CHUNKS
    parts = sems.shape[0]
    size = nblocks // parts

    def send(part):
        slots = pl.ds(part * size, size)
        return pltpu.make_async_copy(staged_ref.at[slots], out_hbm.at[slots], sems.at[part])

    for part in range(parts):
        for slot in range(part * size, (part + 1) * size):
            for i, raw_ref in enumerate(raws):
                examples, width = raw_ref.shape[0] // nblocks, raw_ref.shape[1]
                chunk, group = divmod(i, groups)
                rows = pl.ds(slots_ref[slot], examples, stride=nblocks)
                staged_ref[
                    slot, group * examples:(group + 1) * examples, chunk * width:(chunk + 1) * width
                ] = raw_ref[rows, :].astype(staged_ref.dtype)
        send(part).start()
    for part in range(parts):
        send(part).wait()


def in_slot_order(raws, slots):
    nblocks = slots.shape[0]
    rows, width = raws[0].shape
    groups = len(raws) // CHUNKS
    shape = (nblocks, groups * rows // nblocks, CHUNKS * width)
    return pl.pallas_call(
        order_kernel,
        in_specs=[pl.BlockSpec(memory_space=pltpu.SMEM)] + [pl.BlockSpec(memory_space=pltpu.VMEM)] * len(raws),
        out_specs=pl.BlockSpec(memory_space=pltpu.HBM),
        out_shape=jax.ShapeDtypeStruct(shape, jnp.bfloat16),
        scratch_shapes=[pltpu.VMEM(shape, jnp.bfloat16), pltpu.SemaphoreType.DMA((4,))],
        compiler_params=pltpu.CompilerParams(vmem_limit_bytes=4 * 1024 * 1024),
        cost_estimate=pl.CostEstimate(
            flops=rows * width, bytes_accessed=6 * len(raws) * rows * width, transcendentals=0
        ),
    )(slots, *raws)


def finish_kernel(got_ref, allowed_ref, out_ref):
    n, owned, quad, examples, half = got_ref.shape
    parts = half // LANES
    per_row = owned * CORES * parts
    for device in range(n):
        for core in range(CORES):
            sources = [(device & ~3) | (y << 1) | core for y in range(quad // CORES)]
            for slot in range(owned):
                scores = sum(got_ref[s, slot, s ^ device].astype(jnp.float32) for s in sources)
                scores = scores * allowed_ref[slot:slot + 1, core * half:(core + 1) * half]
                for i in range(parts):
                    first = device * examples * per_row + (slot * CORES + core) * parts + i
                    out_ref[pl.ds(first, examples, stride=per_row), :] = scores[:, i * LANES:(i + 1) * LANES]


def finish(got, allowed):
    n, owned, _, examples, half = got.shape
    flat = pl.pallas_call(
        finish_kernel,
        out_shape=jax.ShapeDtypeStruct((n * examples * owned * CORES * half // LANES, LANES), jnp.float32),
        compiler_params=pltpu.CompilerParams(vmem_limit_bytes=4 * 1024 * 1024),
        cost_estimate=pl.CostEstimate(flops=got.size, bytes_accessed=4 * got.size, transcendentals=0),
    )(got, allowed)
    return flat.reshape(n * examples, owned, CORES * half)


def shards(queries, precond, train, query_cluster, cand_blocks, cand_count, slot_block):
    n = lax.axis_size("rows")
    chips = n // CORES
    bits = chips.bit_length() - 1
    ybit, zbit = 1, 1 + bits // 2
    rest = [bit for bit in range(1, 1 + bits) if bit not in (ybit, zbit)]
    me = lax.axis_index("rows")
    core = me & 1

    examples, nblocks, width = train.shape
    nq = queries.shape[0]

    def swap(value, bit):
        return lax.ppermute(value, "rows", [(r, r ^ (1 << bit)) for r in range(n)])

    rows = nq // CORES // CHUNKS // PATHS
    sizes = {(ybit, width // 2), (zbit, rows // 2)} | {(bit, rows >> (i + 2)) for i, bit in enumerate(rest[:-1])}
    offsets = {}
    first_half = {}
    for bit, size in sorted(sizes):
        side = (me >> bit) & 1
        offsets[bit, size] = (side * size, (1 - side) * size)
        first_half[bit] = side == 0
    owned = nblocks // n
    first_slot = me * owned
    starts = [jnp.stack([core, jnp.int32(chunk)]) for chunk in range(CHUNKS)]
    scalars = (starts, 1 - core, first_slot, offsets, first_half)
    scalars, queries, train = lax.optimization_barrier((scalars, queries, train))
    starts, other_core, first_slot, offsets, first_half = scalars

    def pack(value):
        value = value * UNIT
        return (value * lax.rsqrt(jnp.abs(value) + LEAST)).astype(jnp.float16)

    def unpack(value):
        value = value.astype(jnp.float32)
        return value * jnp.abs(value) * (1.0 / UNIT)

    def part(value, bit, axis, other=0):
        shape = list(value.shape)
        shape[axis] //= 2
        starts = [0] * value.ndim
        starts[axis] = offsets[bit, shape[axis]][other]
        return lax.dynamic_slice(value, starts, shape, allow_negative_indices=False)

    def give(value, bit, axis):
        return pack(part(value, bit, axis, 1))

    def keep(value, got, bit, axis):
        return part(value, bit, axis) + unpack(got)

    def join(own, got, bit):
        mine_first = jnp.concatenate([own, got], axis=1)
        return jnp.where(first_half[bit], mine_first, jnp.concatenate([got, own], axis=1))

    def after(value, first):
        return lax.optimization_barrier((value, first))[0]

    def paths(values, other):
        return [value + unpack(other[i * rows:(i + 1) * rows]) for i, value in enumerate(values)]

    levels = ((ybit, 1), (zbit, 0)), ((zbit, 0), (ybit, 1))

    def messages(values, step):
        return [give(value, *level[step]) for value, level in zip(values, levels)]

    def exchange(values, sent, step):
        got = [swap(message, level[step][0]) for message, level in zip(sent, levels)]
        return [keep(value, message, *level[step]) for value, message, level in zip(values, got, levels)]

    def halve(values):
        value = jnp.stack(values)
        for bit in rest[:-1]:
            value = keep(value, swap(give(value, bit, 1), bit), bit, 1)
        return value

    def gather(value, first=None):
        for bit in reversed([zbit] + rest[:-1]):
            got = swap(value, bit)
            if first is not None and bit == zbit:
                got = after(got, first)
            value = join(value, got, bit)
        return value.reshape(-1, value.shape[-1])

    def scores(group, value):
        return lax.dot_general(group, value, (((1,), (1,)), ((), ())), preferred_element_type=jnp.float32)

    blocks = train.reshape(examples * nblocks, width)
    every = examples * nblocks
    middle = max(1, examples * 3 // 8) * nblocks

    def features(blocks, first, count, other):
        start = offsets[ybit, width // 2][other]
        return lax.dynamic_slice(blocks, (first, start), (count, width // 2), allow_negative_indices=False)

    high = lax.reduce_precision(queries, 8, 7)
    low = (queries - high).astype(jnp.bfloat16)
    high = high.astype(jnp.bfloat16)
    left = jnp.concatenate([high, low, high], axis=1)
    blocks = after(blocks, left)
    early = features(blocks, 0, middle, 1)
    other_core, blocks = after((other_core, blocks), early)
    early = swap(early, ybit)

    *full, high, low = product(other_core.reshape(1), left, [precond], other_kernel, OTHER_VMEM, CHUNKS)
    sent = pack(full[0])
    got = swap(sent, 0)
    mine = product(after(starts[0], sent), left, [high, low], mine_kernel, MINE_VMEM, PATHS)
    one = paths(mine, got)
    sent = messages(one, 0)
    got = swap(pack(after(full[1], mine[0])), 0)
    mine = product(after(starts[1], sent), left, [high, low], mine_kernel, MINE_VMEM, PATHS)
    two = paths(mine, got)
    blocks = after(blocks, sent)
    near = features(blocks, 0, every, 0)
    sibling = swap(near, 0)
    one = exchange(one, sent, 0)
    sent = messages(one, 1)
    sent_two = after(messages(two, 0), (sent, early))
    one = halve(exchange(one, sent, 1))
    sent = pack(one)
    got_one = swap(sent, rest[-1])
    two = exchange(two, sent_two, 0)
    two = exchange(two, messages(two, 1), 1)
    late = swap(features(after(blocks, two[0]), middle, every - middle, 1), ybit)
    two = halve(two)
    sent = pack(two)
    one = (after(one, sent) + unpack(got_one)).astype(jnp.bfloat16)
    got_two = swap(sent, rest[-1])
    early = after(early, one)
    one = gather(one)
    groups = [
        jnp.concatenate([near, sibling], axis=0),
        jnp.concatenate([early, late, swap(early, 0), swap(late, 0)], axis=0),
    ]
    raws = [scores(group, one) for group in groups]
    two = gather((two + unpack(got_two)).astype(jnp.bfloat16), raws)
    raws = raws + [scores(group, two) for group in groups]

    ordered = in_slot_order(raws, slot_block).reshape(n, owned, 2 * CORES * examples, nq // CORES)
    got = lax.all_to_all(ordered, "rows", split_axis=0, concat_axis=0, tiled=True)

    lists = (query_cluster, cand_blocks, cand_count, slot_block, first_slot)
    query_cluster, cand_blocks, cand_count, slot_block, first_slot = after(lists, ordered)
    allowed = listed_mask(query_cluster, cand_blocks, cand_count, nblocks)
    slots = lax.dynamic_slice(slot_block, (first_slot,), (owned,), allow_negative_indices=False)
    own_allowed = jnp.take(allowed, slots, axis=0, mode="clip")
    return finish(got.reshape(n, owned, 2 * CORES, examples, nq // CORES), own_allowed)


def solution(mesh):
    placed = (
        P("groups", "rows"),
        P("rows", None),
        P("rows", "groups", None),
        P("groups"),
        P("groups", None),
        P("groups"),
        P("groups"),
    )
    return jax.shard_map(
        shards,
        mesh=mesh,
        in_specs=placed,
        out_specs=P(None, ("groups", "rows"), None),
        check_vma=False,
    )
```

```python
import jax
import jax.numpy as jnp
from jax import lax
from jax.experimental import pallas as pl
from jax.experimental.pallas import tpu as pltpu
from jax.sharding import PartitionSpec as P

CORES = 2
CHUNKS = 2
PATHS = 2
UNIT = 2.0 ** 18
LEAST = 2.0 ** -100
LANES = 128
OTHER_VMEM = 44
MINE_VMEM = 16


def listed_mask(query_cluster, cand_blocks, cand_count, nblocks):
    nclusters = cand_blocks.shape[0]
    valid = jnp.arange(cand_blocks.shape[1])[None, :] < cand_count[:, None]
    hits = (cand_blocks[:, :, None] == jnp.arange(nblocks)[None, None, :]) & valid[:, :, None]
    listed = jnp.any(hits, axis=1).astype(jnp.float32)
    onehot = (query_cluster[:, None] == jnp.arange(nclusters)[None, :]).astype(jnp.float32)
    return jnp.dot(listed.T, onehot.T, preferred_element_type=jnp.float32)


def split(value):
    high = value.astype(jnp.bfloat16)
    return high, (value - high.astype(jnp.float32)).astype(jnp.bfloat16)


def rows_of(core_ref, rows_ref):
    half = rows_ref.shape[0] // CORES
    return rows_ref[pl.ds(pl.multiple_of(core_ref[0] * half, half), half), :]


def multiply(left, high, low, outs, columns):
    right = jnp.concatenate([high, high, low], axis=0)
    result = jnp.dot(left, right, preferred_element_type=jnp.float32)
    part = result.shape[0] // len(outs)
    for chunk, out_ref in enumerate(outs):
        out_ref[:, columns] = result[chunk * part:(chunk + 1) * part]


def other_kernel(core_ref, rows_ref, columns_hbm, *refs):
    outs, (high_ref, low_ref, columns_ref, sems) = refs[:-4], refs[-4:]
    steps, _, block = columns_ref.shape

    def load(i):
        return pltpu.make_async_copy(
            columns_hbm.at[:, i * block:(i + 1) * block], columns_ref.at[i], sems.at[i]
        )

    for i in range(steps):
        load(i).start()
    left = rows_of(core_ref, rows_ref)
    for i in range(steps):
        load(i).wait()
        columns = slice(i * block, (i + 1) * block)
        high, low = split(columns_ref[i])
        high_ref[:, columns] = high
        low_ref[:, columns] = low
        multiply(left, high, low, outs, columns)


def mine_kernel(core_ref, rows_ref, high_ref, low_ref, *outs):
    chunks = len(outs) // PATHS
    half = rows_ref.shape[0] // CORES
    count = half // CHUNKS * chunks
    first = core_ref[0] * half + core_ref[1] * (half // CHUNKS)
    left = rows_ref[pl.ds(pl.multiple_of(first, half // CHUNKS), count), :]
    width = high_ref.shape[1]
    block = min(512, width)
    for i in range(width // block):
        columns = slice(i * block, (i + 1) * block)
        multiply(left, high_ref[:, columns], low_ref[:, columns], outs, columns)


def product(core, rows, columns, kernel, vmem, pieces):
    nrows = rows.shape[0]
    depth, width = columns[0].shape
    block = min(512, width)
    whole = CHUNKS if kernel is other_kernel else CHUNKS * PATHS
    out = [jax.ShapeDtypeStruct((nrows // CORES // whole, width), jnp.float32)] * pieces
    in_vmem = pl.BlockSpec(memory_space=pltpu.VMEM)
    operand, scratch = in_vmem, []
    if kernel is other_kernel:
        out = out + [jax.ShapeDtypeStruct((depth, width), jnp.bfloat16)] * 2
        operand = pl.BlockSpec(memory_space=pltpu.HBM)
        scratch = [
            pltpu.VMEM((width // block, depth, block), jnp.float32),
            pltpu.SemaphoreType.DMA((width // block,)),
        ]
    return pl.pallas_call(
        kernel,
        in_specs=[pl.BlockSpec(memory_space=pltpu.SMEM), in_vmem] + [operand] * len(columns),
        out_specs=[in_vmem] * len(out),
        out_shape=out,
        scratch_shapes=scratch,
        compiler_params=pltpu.CompilerParams(vmem_limit_bytes=vmem * 1024 * 1024),
        cost_estimate=pl.CostEstimate(
            flops=3 * nrows * depth * width,
            bytes_accessed=4 * width * depth + 2 * width * nrows,
            transcendentals=0,
        ),
    )(core, rows, *columns)


def order_kernel(slots_ref, *refs):
    raws, (out_hbm, staged_ref, sems) = refs[:-3], refs[-3:]
    nblocks = slots_ref.shape[0]
    groups = len(raws) // CHUNKS
    parts = sems.shape[0]
    size = nblocks // parts

    def send(part):
        slots = pl.ds(part * size, size)
        return pltpu.make_async_copy(staged_ref.at[slots], out_hbm.at[slots], sems.at[part])

    for part in range(parts):
        for slot in range(part * size, (part + 1) * size):
            for i, raw_ref in enumerate(raws):
                examples, width = raw_ref.shape[0] // nblocks, raw_ref.shape[1]
                chunk, group = divmod(i, groups)
                rows = pl.ds(slots_ref[slot], examples, stride=nblocks)
                staged_ref[
                    slot, group * examples:(group + 1) * examples, chunk * width:(chunk + 1) * width
                ] = raw_ref[rows, :].astype(staged_ref.dtype)
        send(part).start()
    for part in range(parts):
        send(part).wait()


def in_slot_order(raws, slots):
    nblocks = slots.shape[0]
    rows, width = raws[0].shape
    groups = len(raws) // CHUNKS
    shape = (nblocks, groups * rows // nblocks, CHUNKS * width)
    return pl.pallas_call(
        order_kernel,
        in_specs=[pl.BlockSpec(memory_space=pltpu.SMEM)] + [pl.BlockSpec(memory_space=pltpu.VMEM)] * len(raws),
        out_specs=pl.BlockSpec(memory_space=pltpu.HBM),
        out_shape=jax.ShapeDtypeStruct(shape, jnp.bfloat16),
        scratch_shapes=[pltpu.VMEM(shape, jnp.bfloat16), pltpu.SemaphoreType.DMA((4,))],
        compiler_params=pltpu.CompilerParams(vmem_limit_bytes=4 * 1024 * 1024),
        cost_estimate=pl.CostEstimate(
            flops=rows * width, bytes_accessed=6 * len(raws) * rows * width, transcendentals=0
        ),
    )(slots, *raws)


def finish_kernel(got_ref, allowed_ref, out_ref):
    n, owned, quad, examples, half = got_ref.shape
    parts = half // LANES
    per_row = owned * CORES * parts
    for device in range(n):
        for core in range(CORES):
            sources = [(device & ~3) | (y << 1) | core for y in range(quad // CORES)]
            for slot in range(owned):
                scores = sum(got_ref[s, slot, s ^ device].astype(jnp.float32) for s in sources)
                scores = scores * allowed_ref[slot:slot + 1, core * half:(core + 1) * half]
                for i in range(parts):
                    first = device * examples * per_row + (slot * CORES + core) * parts + i
                    out_ref[pl.ds(first, examples, stride=per_row), :] = scores[:, i * LANES:(i + 1) * LANES]


def finish(got, allowed):
    n, owned, _, examples, half = got.shape
    flat = pl.pallas_call(
        finish_kernel,
        out_shape=jax.ShapeDtypeStruct((n * examples * owned * CORES * half // LANES, LANES), jnp.float32),
        compiler_params=pltpu.CompilerParams(vmem_limit_bytes=4 * 1024 * 1024),
        cost_estimate=pl.CostEstimate(flops=got.size, bytes_accessed=4 * got.size, transcendentals=0),
    )(got, allowed)
    return flat.reshape(n * examples, owned, CORES * half)


def shards(queries, precond, train, query_cluster, cand_blocks, cand_count, slot_block):
    n = lax.axis_size("rows")
    chips = n // CORES
    bits = chips.bit_length() - 1
    ybit, zbit = 1, 1 + bits // 2
    rest = [bit for bit in range(1, 1 + bits) if bit not in (ybit, zbit)]
    me = lax.axis_index("rows")
    core = me & 1

    examples, nblocks, width = train.shape
    nq = queries.shape[0]

    def swap(value, bit):
        return lax.ppermute(value, "rows", [(r, r ^ (1 << bit)) for r in range(n)])

    rows = nq // CORES // CHUNKS // PATHS
    sizes = {(ybit, width // 2), (zbit, rows // 2)} | {(bit, rows >> (i + 2)) for i, bit in enumerate(rest[:-1])}
    offsets = {}
    first_half = {}
    for bit, size in sorted(sizes):
        side = (me >> bit) & 1
        offsets[bit, size] = (side * size, (1 - side) * size)
        first_half[bit] = side == 0
    owned = nblocks // n
    first_slot = me * owned
    starts = [jnp.stack([core, jnp.int32(chunk)]) for chunk in range(CHUNKS)]
    scalars = (starts, 1 - core, first_slot, offsets, first_half)
    scalars, queries, train = lax.optimization_barrier((scalars, queries, train))
    starts, other_core, first_slot, offsets, first_half = scalars

    def pack(value):
        value = value * UNIT
        return (value * lax.rsqrt(jnp.abs(value) + LEAST)).astype(jnp.float16)

    def unpack(value):
        value = value.astype(jnp.float32)
        return value * jnp.abs(value) * (1.0 / UNIT)

    def part(value, bit, axis, other=0):
        shape = list(value.shape)
        shape[axis] //= 2
        starts = [0] * value.ndim
        starts[axis] = offsets[bit, shape[axis]][other]
        return lax.dynamic_slice(value, starts, shape, allow_negative_indices=False)

    def give(value, bit, axis):
        return pack(part(value, bit, axis, 1))

    def keep(value, got, bit, axis):
        return part(value, bit, axis) + unpack(got)

    def join(own, got, bit):
        mine_first = jnp.concatenate([own, got], axis=1)
        return jnp.where(first_half[bit], mine_first, jnp.concatenate([got, own], axis=1))

    def after(value, first):
        return lax.optimization_barrier((value, first))[0]

    def paths(values, other):
        return [value + unpack(other[i * rows:(i + 1) * rows]) for i, value in enumerate(values)]

    levels = ((ybit, 1), (zbit, 0)), ((zbit, 0), (ybit, 1))

    def messages(values, step):
        return [give(value, *level[step]) for value, level in zip(values, levels)]

    def exchange(values, sent, step):
        got = [swap(message, level[step][0]) for message, level in zip(sent, levels)]
        return [keep(value, message, *level[step]) for value, message, level in zip(values, got, levels)]

    def halve(values):
        value = jnp.stack(values)
        for bit in rest[:-1]:
            value = keep(value, swap(give(value, bit, 1), bit), bit, 1)
        return value

    def gather(value, first=None):
        for bit in reversed([zbit] + rest[:-1]):
            got = swap(value, bit)
            if first is not None and bit == zbit:
                got = after(got, first)
            value = join(value, got, bit)
        return value.reshape(-1, value.shape[-1])

    def scores(group, value):
        return lax.dot_general(group, value, (((1,), (1,)), ((), ())), preferred_element_type=jnp.float32)

    blocks = train.reshape(examples * nblocks, width)
    every = examples * nblocks
    middle = max(1, examples * 7 // 16) * nblocks

    def features(blocks, first, count, other):
        start = offsets[ybit, width // 2][other]
        return lax.dynamic_slice(blocks, (first, start), (count, width // 2), allow_negative_indices=False)

    high = lax.reduce_precision(queries, 8, 7)
    low = (queries - high).astype(jnp.bfloat16)
    high = high.astype(jnp.bfloat16)
    left = jnp.concatenate([high, low, high], axis=1)
    blocks = after(blocks, left)
    early = features(blocks, 0, middle, 1)
    other_core, blocks = after((other_core, blocks), early)
    early = swap(early, ybit)

    *full, high, low = product(other_core.reshape(1), left, [precond], other_kernel, OTHER_VMEM, CHUNKS)
    sent = pack(full[0])
    got = swap(sent, 0)
    mine = product(after(starts[0], sent), left, [high, low], mine_kernel, MINE_VMEM, PATHS)
    one = paths(mine, got)
    sent = messages(one, 0)
    got = swap(pack(after(full[1], mine[0])), 0)
    mine = product(after(starts[1], sent), left, [high, low], mine_kernel, MINE_VMEM, PATHS)
    two = paths(mine, got)
    blocks = after(blocks, sent)
    near = features(blocks, 0, every, 0)
    sibling = swap(near, 0)
    one = exchange(one, sent, 0)
    sent = messages(one, 1)
    sent_two = after(messages(two, 0), (sent, early))
    one = halve(exchange(one, sent, 1))
    sent = pack(one)
    got_one = swap(sent, rest[-1])
    two = exchange(two, sent_two, 0)
    two = exchange(two, messages(two, 1), 1)
    late = swap(features(after(blocks, two[0]), middle, every - middle, 1), ybit)
    two = halve(two)
    sent = pack(two)
    one = (after(one, sent) + unpack(got_one)).astype(jnp.bfloat16)
    got_two = swap(sent, rest[-1])
    early = after(early, one)
    one = gather(one)
    groups = [
        jnp.concatenate([near, sibling], axis=0),
        jnp.concatenate([early, late, swap(early, 0), swap(late, 0)], axis=0),
    ]
    raws = [scores(group, one) for group in groups]
    two = gather((two + unpack(got_two)).astype(jnp.bfloat16), raws)
    raws = raws + [scores(group, two) for group in groups]

    ordered = in_slot_order(raws, slot_block).reshape(n, owned, 2 * CORES * examples, nq // CORES)
    got = lax.all_to_all(ordered, "rows", split_axis=0, concat_axis=0, tiled=True)

    lists = (query_cluster, cand_blocks, cand_count, slot_block, first_slot)
    query_cluster, cand_blocks, cand_count, slot_block, first_slot = after(lists, ordered)
    allowed = listed_mask(query_cluster, cand_blocks, cand_count, nblocks)
    slots = lax.dynamic_slice(slot_block, (first_slot,), (owned,), allow_negative_indices=False)
    own_allowed = jnp.take(allowed, slots, axis=0, mode="clip")
    return finish(got.reshape(n, owned, 2 * CORES, examples, nq // CORES), own_allowed)


def solution(mesh):
    placed = (
        P("groups", "rows"),
        P("rows", None),
        P("rows", "groups", None),
        P("groups"),
        P("groups", None),
        P("groups"),
        P("groups"),
    )
    return jax.shard_map(
        shards,
        mesh=mesh,
        in_specs=placed,
        out_specs=P(None, ("groups", "rows"), None),
        check_vma=False,
    )
```

```python
import jax
import jax.numpy as jnp
from jax import lax
from jax.experimental import pallas as pl
from jax.experimental.pallas import tpu as pltpu
from jax.sharding import PartitionSpec as P

CORES = 2
CHUNKS = 2
PATHS = 2
UNIT = 2.0 ** 18
LEAST = 2.0 ** -100
LANES = 128
OTHER_VMEM = 44
MINE_VMEM = 16


def listed_mask(query_cluster, cand_blocks, cand_count, nblocks):
    nclusters = cand_blocks.shape[0]
    valid = jnp.arange(cand_blocks.shape[1])[None, :] < cand_count[:, None]
    hits = (cand_blocks[:, :, None] == jnp.arange(nblocks)[None, None, :]) & valid[:, :, None]
    listed = jnp.any(hits, axis=1).astype(jnp.float32)
    onehot = (query_cluster[:, None] == jnp.arange(nclusters)[None, :]).astype(jnp.float32)
    return jnp.dot(listed.T, onehot.T, preferred_element_type=jnp.float32)


def split(value):
    high = value.astype(jnp.bfloat16)
    return high, (value - high.astype(jnp.float32)).astype(jnp.bfloat16)


def rows_of(core_ref, rows_ref):
    half = rows_ref.shape[0] // CORES
    return rows_ref[pl.ds(pl.multiple_of(core_ref[0] * half, half), half), :]


def multiply(left, high, low, outs, columns):
    right = jnp.concatenate([high, high, low], axis=0)
    result = jnp.dot(left, right, preferred_element_type=jnp.float32)
    part = result.shape[0] // len(outs)
    for chunk, out_ref in enumerate(outs):
        out_ref[:, columns] = result[chunk * part:(chunk + 1) * part]


def other_kernel(core_ref, rows_ref, columns_hbm, *refs):
    outs, (high_ref, low_ref, columns_ref, sems) = refs[:-4], refs[-4:]
    steps, _, block = columns_ref.shape

    def load(i):
        return pltpu.make_async_copy(
            columns_hbm.at[:, i * block:(i + 1) * block], columns_ref.at[i], sems.at[i]
        )

    for i in range(steps):
        load(i).start()
    left = rows_of(core_ref, rows_ref)
    for i in range(steps):
        load(i).wait()
        columns = slice(i * block, (i + 1) * block)
        high, low = split(columns_ref[i])
        high_ref[:, columns] = high
        low_ref[:, columns] = low
        multiply(left, high, low, outs, columns)


def mine_kernel(core_ref, rows_ref, high_ref, low_ref, *outs):
    chunks = len(outs) // PATHS
    half = rows_ref.shape[0] // CORES
    count = half // CHUNKS * chunks
    first = core_ref[0] * half + core_ref[1] * (half // CHUNKS)
    left = rows_ref[pl.ds(pl.multiple_of(first, half // CHUNKS), count), :]
    width = high_ref.shape[1]
    block = min(512, width)
    for i in range(width // block):
        columns = slice(i * block, (i + 1) * block)
        multiply(left, high_ref[:, columns], low_ref[:, columns], outs, columns)


def product(core, rows, columns, kernel, vmem, pieces):
    nrows = rows.shape[0]
    depth, width = columns[0].shape
    block = min(512, width)
    whole = CHUNKS if kernel is other_kernel else CHUNKS * PATHS
    out = [jax.ShapeDtypeStruct((nrows // CORES // whole, width), jnp.float32)] * pieces
    in_vmem = pl.BlockSpec(memory_space=pltpu.VMEM)
    operand, scratch = in_vmem, []
    if kernel is other_kernel:
        out = out + [jax.ShapeDtypeStruct((depth, width), jnp.bfloat16)] * 2
        operand = pl.BlockSpec(memory_space=pltpu.HBM)
        scratch = [
            pltpu.VMEM((width // block, depth, block), jnp.float32),
            pltpu.SemaphoreType.DMA((width // block,)),
        ]
    return pl.pallas_call(
        kernel,
        in_specs=[pl.BlockSpec(memory_space=pltpu.SMEM), in_vmem] + [operand] * len(columns),
        out_specs=[in_vmem] * len(out),
        out_shape=out,
        scratch_shapes=scratch,
        compiler_params=pltpu.CompilerParams(vmem_limit_bytes=vmem * 1024 * 1024),
        cost_estimate=pl.CostEstimate(
            flops=3 * nrows * depth * width,
            bytes_accessed=4 * width * depth + 2 * width * nrows,
            transcendentals=0,
        ),
    )(core, rows, *columns)


def order_kernel(slots_ref, *refs):
    raws, (out_hbm, staged_ref, sems) = refs[:-3], refs[-3:]
    nblocks = slots_ref.shape[0]
    groups = len(raws) // CHUNKS
    parts = sems.shape[0]
    size = nblocks // parts

    def send(part):
        slots = pl.ds(part * size, size)
        return pltpu.make_async_copy(staged_ref.at[slots], out_hbm.at[slots], sems.at[part])

    for part in range(parts):
        for slot in range(part * size, (part + 1) * size):
            for i, raw_ref in enumerate(raws):
                examples, width = raw_ref.shape[0] // nblocks, raw_ref.shape[1]
                chunk, group = divmod(i, groups)
                rows = pl.ds(slots_ref[slot], examples, stride=nblocks)
                staged_ref[
                    slot, group * examples:(group + 1) * examples, chunk * width:(chunk + 1) * width
                ] = raw_ref[rows, :].astype(staged_ref.dtype)
        send(part).start()
    for part in range(parts):
        send(part).wait()


def in_slot_order(raws, slots):
    nblocks = slots.shape[0]
    rows, width = raws[0].shape
    groups = len(raws) // CHUNKS
    shape = (nblocks, groups * rows // nblocks, CHUNKS * width)
    return pl.pallas_call(
        order_kernel,
        in_specs=[pl.BlockSpec(memory_space=pltpu.SMEM)] + [pl.BlockSpec(memory_space=pltpu.VMEM)] * len(raws),
        out_specs=pl.BlockSpec(memory_space=pltpu.HBM),
        out_shape=jax.ShapeDtypeStruct(shape, jnp.bfloat16),
        scratch_shapes=[pltpu.VMEM(shape, jnp.bfloat16), pltpu.SemaphoreType.DMA((4,))],
        compiler_params=pltpu.CompilerParams(vmem_limit_bytes=4 * 1024 * 1024),
        cost_estimate=pl.CostEstimate(
            flops=rows * width, bytes_accessed=6 * len(raws) * rows * width, transcendentals=0
        ),
    )(slots, *raws)


def finish_kernel(got_ref, allowed_ref, out_ref):
    n, owned, quad, examples, half = got_ref.shape
    parts = half // LANES
    per_row = owned * CORES * parts
    for device in range(n):
        for core in range(CORES):
            sources = [(device & ~3) | (y << 1) | core for y in range(quad // CORES)]
            for slot in range(owned):
                scores = sum(got_ref[s, slot, s ^ device].astype(jnp.float32) for s in sources)
                scores = scores * allowed_ref[slot:slot + 1, core * half:(core + 1) * half]
                for i in range(parts):
                    first = device * examples * per_row + (slot * CORES + core) * parts + i
                    out_ref[pl.ds(first, examples, stride=per_row), :] = scores[:, i * LANES:(i + 1) * LANES]


def finish(got, allowed):
    n, owned, _, examples, half = got.shape
    flat = pl.pallas_call(
        finish_kernel,
        out_shape=jax.ShapeDtypeStruct((n * examples * owned * CORES * half // LANES, LANES), jnp.float32),
        compiler_params=pltpu.CompilerParams(vmem_limit_bytes=4 * 1024 * 1024),
        cost_estimate=pl.CostEstimate(flops=got.size, bytes_accessed=4 * got.size, transcendentals=0),
    )(got, allowed)
    return flat.reshape(n * examples, owned, CORES * half)


def shards(queries, precond, train, query_cluster, cand_blocks, cand_count, slot_block):
    n = lax.axis_size("rows")
    chips = n // CORES
    bits = chips.bit_length() - 1
    ybit, zbit = 1, 1 + bits // 2
    rest = [bit for bit in range(1, 1 + bits) if bit not in (ybit, zbit)]
    me = lax.axis_index("rows")
    core = me & 1

    examples, nblocks, width = train.shape
    nq = queries.shape[0]

    def swap(value, bit):
        return lax.ppermute(value, "rows", [(r, r ^ (1 << bit)) for r in range(n)])

    rows = nq // CORES // CHUNKS // PATHS
    sizes = {(ybit, width // 2), (zbit, rows // 2)} | {(bit, rows >> (i + 2)) for i, bit in enumerate(rest[:-1])}
    offsets = {}
    first_half = {}
    for bit, size in sorted(sizes):
        side = (me >> bit) & 1
        offsets[bit, size] = (side * size, (1 - side) * size)
        first_half[bit] = side == 0
    owned = nblocks // n
    first_slot = me * owned
    starts = [jnp.stack([core, jnp.int32(chunk)]) for chunk in range(CHUNKS)]
    scalars = (starts, 1 - core, first_slot, offsets, first_half)
    scalars, queries, train = lax.optimization_barrier((scalars, queries, train))
    starts, other_core, first_slot, offsets, first_half = scalars

    def pack(value):
        value = value * UNIT
        return (value * lax.rsqrt(jnp.abs(value) + LEAST)).astype(jnp.float16)

    def unpack(value):
        value = value.astype(jnp.float32)
        return value * jnp.abs(value) * (1.0 / UNIT)

    def part(value, bit, axis, other=0):
        shape = list(value.shape)
        shape[axis] //= 2
        starts = [0] * value.ndim
        starts[axis] = offsets[bit, shape[axis]][other]
        return lax.dynamic_slice(value, starts, shape, allow_negative_indices=False)

    def give(value, bit, axis):
        return pack(part(value, bit, axis, 1))

    def keep(value, got, bit, axis):
        return part(value, bit, axis) + unpack(got)

    def join(own, got, bit):
        mine_first = jnp.concatenate([own, got], axis=1)
        return jnp.where(first_half[bit], mine_first, jnp.concatenate([got, own], axis=1))

    def after(value, first):
        return lax.optimization_barrier((value, first))[0]

    def paths(values, other):
        return [value + unpack(other[i * rows:(i + 1) * rows]) for i, value in enumerate(values)]

    levels = ((ybit, 1), (zbit, 0)), ((zbit, 0), (ybit, 1))

    def messages(values, step):
        return [give(value, *level[step]) for value, level in zip(values, levels)]

    def exchange(values, sent, step):
        got = [swap(message, level[step][0]) for message, level in zip(sent, levels)]
        return [keep(value, message, *level[step]) for value, message, level in zip(values, got, levels)]

    def halve(values):
        value = jnp.stack(values)
        for bit in rest[:-1]:
            value = keep(value, swap(give(value, bit, 1), bit), bit, 1)
        return value

    def gather(value, first=None):
        for bit in reversed([zbit] + rest[:-1]):
            got = swap(value, bit)
            if first is not None and bit == zbit:
                got = after(got, first)
            value = join(value, got, bit)
        return value.reshape(-1, value.shape[-1])

    def scores(group, value):
        return lax.dot_general(group, value, (((1,), (1,)), ((), ())), preferred_element_type=jnp.float32)

    blocks = train.reshape(examples * nblocks, width)
    every = examples * nblocks
    middle = max(1, examples * 5 // 16) * nblocks

    def features(blocks, first, count, other):
        start = offsets[ybit, width // 2][other]
        return lax.dynamic_slice(blocks, (first, start), (count, width // 2), allow_negative_indices=False)

    high = lax.reduce_precision(queries, 8, 7)
    low = (queries - high).astype(jnp.bfloat16)
    high = high.astype(jnp.bfloat16)
    left = jnp.concatenate([high, low, high], axis=1)
    blocks = after(blocks, left)
    early = features(blocks, 0, middle, 1)
    other_core, blocks = after((other_core, blocks), early)
    early = swap(early, ybit)

    *full, high, low = product(other_core.reshape(1), left, [precond], other_kernel, OTHER_VMEM, CHUNKS)
    sent = pack(full[0])
    got = swap(sent, 0)
    mine = product(after(starts[0], sent), left, [high, low], mine_kernel, MINE_VMEM, PATHS)
    one = paths(mine, got)
    sent = messages(one, 0)
    got = swap(pack(after(full[1], mine[0])), 0)
    mine = product(after(starts[1], sent), left, [high, low], mine_kernel, MINE_VMEM, PATHS)
    two = paths(mine, got)
    blocks = after(blocks, sent)
    near = features(blocks, 0, every, 0)
    sibling = swap(near, 0)
    one = exchange(one, sent, 0)
    sent = messages(one, 1)
    sent_two = after(messages(two, 0), (sent, early))
    one = halve(exchange(one, sent, 1))
    sent = pack(one)
    got_one = swap(sent, rest[-1])
    two = exchange(two, sent_two, 0)
    two = exchange(two, messages(two, 1), 1)
    late = swap(features(after(blocks, two[0]), middle, every - middle, 1), ybit)
    two = halve(two)
    sent = pack(two)
    one = (after(one, sent) + unpack(got_one)).astype(jnp.bfloat16)
    got_two = swap(sent, rest[-1])
    early = after(early, one)
    one = gather(one)
    groups = [
        jnp.concatenate([near, sibling], axis=0),
        jnp.concatenate([early, late, swap(early, 0), swap(late, 0)], axis=0),
    ]
    raws = [scores(group, one) for group in groups]
    two = gather((two + unpack(got_two)).astype(jnp.bfloat16), raws)
    raws = raws + [scores(group, two) for group in groups]

    ordered = in_slot_order(raws, slot_block).reshape(n, owned, 2 * CORES * examples, nq // CORES)
    got = lax.all_to_all(ordered, "rows", split_axis=0, concat_axis=0, tiled=True)

    lists = (query_cluster, cand_blocks, cand_count, slot_block, first_slot)
    query_cluster, cand_blocks, cand_count, slot_block, first_slot = after(lists, ordered)
    allowed = listed_mask(query_cluster, cand_blocks, cand_count, nblocks)
    slots = lax.dynamic_slice(slot_block, (first_slot,), (owned,), allow_negative_indices=False)
    own_allowed = jnp.take(allowed, slots, axis=0, mode="clip")
    return finish(got.reshape(n, owned, 2 * CORES, examples, nq // CORES), own_allowed)


def solution(mesh):
    placed = (
        P("groups", "rows"),
        P("rows", None),
        P("rows", "groups", None),
        P("groups"),
        P("groups", None),
        P("groups"),
        P("groups"),
    )
    return jax.shard_map(
        shards,
        mesh=mesh,
        in_specs=placed,
        out_specs=P(None, ("groups", "rows"), None),
        check_vma=False,
    )
```

```python
import jax
import jax.numpy as jnp
from jax import lax
from jax.experimental import pallas as pl
from jax.experimental.pallas import tpu as pltpu
from jax.sharding import PartitionSpec as P

CORES = 2
CHUNKS = 2
PATHS = 2
UNIT = 2.0 ** 18
LEAST = 2.0 ** -100
LANES = 128
OTHER_VMEM = 44
MINE_VMEM = 16


def listed_mask(query_cluster, cand_blocks, cand_count, nblocks):
    nclusters = cand_blocks.shape[0]
    valid = jnp.arange(cand_blocks.shape[1])[None, :] < cand_count[:, None]
    hits = (cand_blocks[:, :, None] == jnp.arange(nblocks)[None, None, :]) & valid[:, :, None]
    listed = jnp.any(hits, axis=1).astype(jnp.float32)
    onehot = (query_cluster[:, None] == jnp.arange(nclusters)[None, :]).astype(jnp.float32)
    return jnp.dot(listed.T, onehot.T, preferred_element_type=jnp.float32)


def split(value):
    high = value.astype(jnp.bfloat16)
    return high, (value - high.astype(jnp.float32)).astype(jnp.bfloat16)


def rows_of(core_ref, rows_ref):
    half = rows_ref.shape[0] // CORES
    return rows_ref[pl.ds(pl.multiple_of(core_ref[0] * half, half), half), :]


def multiply(left, high, low, outs, columns):
    right = jnp.concatenate([high, high, low], axis=0)
    result = jnp.dot(left, right, preferred_element_type=jnp.float32)
    part = result.shape[0] // len(outs)
    for chunk, out_ref in enumerate(outs):
        out_ref[:, columns] = result[chunk * part:(chunk + 1) * part]


def other_kernel(core_ref, rows_ref, columns_hbm, *refs):
    outs, (high_ref, low_ref, columns_ref, sems) = refs[:-4], refs[-4:]
    steps, _, block = columns_ref.shape

    def load(i):
        return pltpu.make_async_copy(
            columns_hbm.at[:, i * block:(i + 1) * block], columns_ref.at[i], sems.at[i]
        )

    for i in range(steps):
        load(i).start()
    left = rows_of(core_ref, rows_ref)
    for i in range(steps):
        load(i).wait()
        columns = slice(i * block, (i + 1) * block)
        high, low = split(columns_ref[i])
        high_ref[:, columns] = high
        low_ref[:, columns] = low
        multiply(left, high, low, outs, columns)


def mine_kernel(core_ref, rows_ref, high_ref, low_ref, *outs):
    chunks = len(outs) // PATHS
    half = rows_ref.shape[0] // CORES
    count = half // CHUNKS * chunks
    first = core_ref[0] * half + core_ref[1] * (half // CHUNKS)
    left = rows_ref[pl.ds(pl.multiple_of(first, half // CHUNKS), count), :]
    width = high_ref.shape[1]
    block = min(512, width)
    for i in range(width // block):
        columns = slice(i * block, (i + 1) * block)
        multiply(left, high_ref[:, columns], low_ref[:, columns], outs, columns)


def product(core, rows, columns, kernel, vmem, pieces):
    nrows = rows.shape[0]
    depth, width = columns[0].shape
    block = min(512, width)
    whole = CHUNKS if kernel is other_kernel else CHUNKS * PATHS
    out = [jax.ShapeDtypeStruct((nrows // CORES // whole, width), jnp.float32)] * pieces
    in_vmem = pl.BlockSpec(memory_space=pltpu.VMEM)
    operand, scratch = in_vmem, []
    if kernel is other_kernel:
        out = out + [jax.ShapeDtypeStruct((depth, width), jnp.bfloat16)] * 2
        operand = pl.BlockSpec(memory_space=pltpu.HBM)
        scratch = [
            pltpu.VMEM((width // block, depth, block), jnp.float32),
            pltpu.SemaphoreType.DMA((width // block,)),
        ]
    return pl.pallas_call(
        kernel,
        in_specs=[pl.BlockSpec(memory_space=pltpu.SMEM), in_vmem] + [operand] * len(columns),
        out_specs=[in_vmem] * len(out),
        out_shape=out,
        scratch_shapes=scratch,
        compiler_params=pltpu.CompilerParams(vmem_limit_bytes=vmem * 1024 * 1024),
        cost_estimate=pl.CostEstimate(
            flops=3 * nrows * depth * width,
            bytes_accessed=4 * width * depth + 2 * width * nrows,
            transcendentals=0,
        ),
    )(core, rows, *columns)


def order_kernel(slots_ref, *refs):
    raws, (out_hbm, staged_ref, sems) = refs[:-3], refs[-3:]
    nblocks = slots_ref.shape[0]
    groups = len(raws) // CHUNKS
    parts = sems.shape[0]
    size = nblocks // parts

    def send(part):
        slots = pl.ds(part * size, size)
        return pltpu.make_async_copy(staged_ref.at[slots], out_hbm.at[slots], sems.at[part])

    for part in range(parts):
        for slot in range(part * size, (part + 1) * size):
            for i, raw_ref in enumerate(raws):
                examples, width = raw_ref.shape[0] // nblocks, raw_ref.shape[1]
                chunk, group = divmod(i, groups)
                rows = pl.ds(slots_ref[slot], examples, stride=nblocks)
                staged_ref[
                    slot, group * examples:(group + 1) * examples, chunk * width:(chunk + 1) * width
                ] = raw_ref[rows, :].astype(staged_ref.dtype)
        send(part).start()
    for part in range(parts):
        send(part).wait()


def in_slot_order(raws, slots):
    nblocks = slots.shape[0]
    rows, width = raws[0].shape
    groups = len(raws) // CHUNKS
    shape = (nblocks, groups * rows // nblocks, CHUNKS * width)
    return pl.pallas_call(
        order_kernel,
        in_specs=[pl.BlockSpec(memory_space=pltpu.SMEM)] + [pl.BlockSpec(memory_space=pltpu.VMEM)] * len(raws),
        out_specs=pl.BlockSpec(memory_space=pltpu.HBM),
        out_shape=jax.ShapeDtypeStruct(shape, jnp.bfloat16),
        scratch_shapes=[pltpu.VMEM(shape, jnp.bfloat16), pltpu.SemaphoreType.DMA((4,))],
        compiler_params=pltpu.CompilerParams(vmem_limit_bytes=4 * 1024 * 1024),
        cost_estimate=pl.CostEstimate(
            flops=rows * width, bytes_accessed=6 * len(raws) * rows * width, transcendentals=0
        ),
    )(slots, *raws)


def finish_kernel(got_ref, allowed_ref, out_ref):
    n, owned, quad, examples, half = got_ref.shape
    parts = half // LANES
    per_row = owned * CORES * parts
    for device in range(n):
        for core in range(CORES):
            sources = [(device & ~3) | (y << 1) | core for y in range(quad // CORES)]
            for slot in range(owned):
                scores = sum(got_ref[s, slot, s ^ device].astype(jnp.float32) for s in sources)
                scores = scores * allowed_ref[slot:slot + 1, core * half:(core + 1) * half]
                for i in range(parts):
                    first = device * examples * per_row + (slot * CORES + core) * parts + i
                    out_ref[pl.ds(first, examples, stride=per_row), :] = scores[:, i * LANES:(i + 1) * LANES]


def finish(got, allowed):
    n, owned, _, examples, half = got.shape
    flat = pl.pallas_call(
        finish_kernel,
        out_shape=jax.ShapeDtypeStruct((n * examples * owned * CORES * half // LANES, LANES), jnp.float32),
        compiler_params=pltpu.CompilerParams(vmem_limit_bytes=4 * 1024 * 1024),
        cost_estimate=pl.CostEstimate(flops=got.size, bytes_accessed=4 * got.size, transcendentals=0),
    )(got, allowed)
    return flat.reshape(n * examples, owned, CORES * half)


def shards(queries, precond, train, query_cluster, cand_blocks, cand_count, slot_block):
    n = lax.axis_size("rows")
    chips = n // CORES
    bits = chips.bit_length() - 1
    ybit, zbit = 1, 1 + bits // 2
    rest = [bit for bit in range(1, 1 + bits) if bit not in (ybit, zbit)]
    me = lax.axis_index("rows")
    core = me & 1

    examples, nblocks, width = train.shape
    nq = queries.shape[0]

    def swap(value, bit):
        return lax.ppermute(value, "rows", [(r, r ^ (1 << bit)) for r in range(n)])

    rows = nq // CORES // CHUNKS // PATHS
    sizes = {(ybit, width // 2), (zbit, rows // 2)} | {(bit, rows >> (i + 2)) for i, bit in enumerate(rest[:-1])}
    offsets = {}
    first_half = {}
    for bit, size in sorted(sizes):
        side = (me >> bit) & 1
        offsets[bit, size] = (side * size, (1 - side) * size)
        first_half[bit] = side == 0
    owned = nblocks // n
    first_slot = me * owned
    starts = [jnp.stack([core, jnp.int32(chunk)]) for chunk in range(CHUNKS)]
    scalars = (starts, 1 - core, first_slot, offsets, first_half)
    scalars, queries, train = lax.optimization_barrier((scalars, queries, train))
    starts, other_core, first_slot, offsets, first_half = scalars

    def pack(value):
        value = value * UNIT
        return (value * lax.rsqrt(jnp.abs(value) + LEAST)).astype(jnp.float16)

    def unpack(value):
        value = value.astype(jnp.float32)
        return value * jnp.abs(value) * (1.0 / UNIT)

    def part(value, bit, axis, other=0):
        shape = list(value.shape)
        shape[axis] //= 2
        starts = [0] * value.ndim
        starts[axis] = offsets[bit, shape[axis]][other]
        return lax.dynamic_slice(value, starts, shape, allow_negative_indices=False)

    def give(value, bit, axis):
        return pack(part(value, bit, axis, 1))

    def keep(value, got, bit, axis):
        return part(value, bit, axis) + unpack(got)

    def join(own, got, bit):
        mine_first = jnp.concatenate([own, got], axis=1)
        return jnp.where(first_half[bit], mine_first, jnp.concatenate([got, own], axis=1))

    def after(value, first):
        return lax.optimization_barrier((value, first))[0]

    def paths(values, other):
        return [value + unpack(other[i * rows:(i + 1) * rows]) for i, value in enumerate(values)]

    levels = ((ybit, 1), (zbit, 0)), ((zbit, 0), (ybit, 1))

    def messages(values, step):
        return [give(value, *level[step]) for value, level in zip(values, levels)]

    def exchange(values, sent, step):
        got = [swap(message, level[step][0]) for message, level in zip(sent, levels)]
        return [keep(value, message, *level[step]) for value, message, level in zip(values, got, levels)]

    def halve(values):
        value = jnp.stack(values)
        for bit in rest[:-1]:
            value = keep(value, swap(give(value, bit, 1), bit), bit, 1)
        return value

    def gather(value, first=None):
        for bit in reversed([zbit] + rest[:-1]):
            got = swap(value, bit)
            if first is not None and bit == zbit:
                got = after(got, first)
            value = join(value, got, bit)
        return value.reshape(-1, value.shape[-1])

    def scores(group, value):
        return lax.dot_general(group, value, (((1,), (1,)), ((), ())), preferred_element_type=jnp.float32)

    blocks = train.reshape(examples * nblocks, width)
    every = examples * nblocks
    middle = max(1, examples * 3 // 8) * nblocks

    def features(blocks, first, count, other):
        start = offsets[ybit, width // 2][other]
        return lax.dynamic_slice(blocks, (first, start), (count, width // 2), allow_negative_indices=False)

    high = lax.reduce_precision(queries, 8, 7)
    low = (queries - high).astype(jnp.bfloat16)
    high = high.astype(jnp.bfloat16)
    left = jnp.concatenate([high, low, high], axis=1)
    blocks = after(blocks, left)
    early = features(blocks, 0, middle, 1)
    other_core, blocks = after((other_core, blocks), early)
    early = swap(early, ybit)

    *full, high, low = product(other_core.reshape(1), left, [precond], other_kernel, OTHER_VMEM, CHUNKS)
    sent = pack(full[0])
    got = swap(sent, 0)
    mine = product(after(starts[0], sent), left, [high, low], mine_kernel, MINE_VMEM, PATHS)
    one = paths(mine, got)
    sent = messages(one, 0)
    got = swap(pack(after(full[1], sent)), 0)
    mine = product(after(starts[1], sent), left, [high, low], mine_kernel, MINE_VMEM, PATHS)
    two = paths(mine, got)
    blocks = after(blocks, sent)
    near = features(blocks, 0, every, 0)
    sibling = swap(near, 0)
    one = exchange(one, sent, 0)
    sent = after(messages(one, 1), two)
    sent_two = after(messages(two, 0), (sent, early))
    one = halve(exchange(one, sent, 1))
    sent = pack(one)
    got_one = swap(sent, rest[-1])
    two = exchange(two, sent_two, 0)
    two = exchange(two, messages(two, 1), 1)
    late = swap(features(after(blocks, two[0]), middle, every - middle, 1), ybit)
    two = halve(two)
    sent = pack(two)
    one = (after(one, sent) + unpack(got_one)).astype(jnp.bfloat16)
    got_two = swap(sent, rest[-1])
    early = after(early, one)
    one = gather(one)
    groups = [
        jnp.concatenate([near, sibling], axis=0),
        jnp.concatenate([early, late, swap(early, 0), swap(late, 0)], axis=0),
    ]
    raws = [scores(group, one) for group in groups]
    two = gather((two + unpack(got_two)).astype(jnp.bfloat16), raws)
    raws = raws + [scores(group, two) for group in groups]

    ordered = in_slot_order(raws, slot_block).reshape(n, owned, 2 * CORES * examples, nq // CORES)
    got = lax.all_to_all(ordered, "rows", split_axis=0, concat_axis=0, tiled=True)

    lists = (query_cluster, cand_blocks, cand_count, slot_block, first_slot)
    query_cluster, cand_blocks, cand_count, slot_block, first_slot = after(lists, ordered)
    allowed = listed_mask(query_cluster, cand_blocks, cand_count, nblocks)
    slots = lax.dynamic_slice(slot_block, (first_slot,), (owned,), allow_negative_indices=False)
    own_allowed = jnp.take(allowed, slots, axis=0, mode="clip")
    return finish(got.reshape(n, owned, 2 * CORES, examples, nq // CORES), own_allowed)


def solution(mesh):
    placed = (
        P("groups", "rows"),
        P("rows", None),
        P("rows", "groups", None),
        P("groups"),
        P("groups", None),
        P("groups"),
        P("groups"),
    )
    return jax.shard_map(
        shards,
        mesh=mesh,
        in_specs=placed,
        out_specs=P(None, ("groups", "rows"), None),
        check_vma=False,
    )
```
